32 devices in a mesh: groups: 2 (over x), expert: 16 (over z, y, core).
Axes of the slice: x: 2, y: 2, z: 4, core: 2. Of those that a mesh axis runs over, the one named last changes fastest.
Arguments:
- layer_input: bfloat16 [4096, 3584], P(('groups', 'expert')), parts along dimension 0, may hold values from -6 to 6
- output_gradient: bfloat16 [4096, 3584], P(('groups', 'expert')), parts along dimension 0, may hold values from -6 to 6
- router_matrix: bfloat16 [3584, 16], replicated, may hold values from -0.09375 to 0.09375
- routed_expert_index: int32 [4096, 4], P(('groups', 'expert')), parts along dimension 0, may hold values from 0 to 15, all different within a row; in each aligned block of 128 rows (0 to 127, 128 to 255, ...) at most 48 rows name the same one
- gate_weight_frozen: bfloat16 [16, 3584, 1024], P('expert'), may hold values from -0.09375 to 0.09375
- up_weight_frozen: bfloat16 [16, 3584, 1024], P('expert'), may hold values from -0.09375 to 0.09375
- down_weight_frozen: bfloat16 [16, 1024, 3584], P('expert'), may hold values from -0.1875 to 0.1875
- gate_adapter_first: bfloat16 [32, 3584, 32], P(('groups', 'expert')), parts along dimension 0, may hold values from -0.09375 to 0.09375
- gate_adapter_second: bfloat16 [32, 32, 1024], P(('groups', 'expert')), parts along dimension 0, may hold values from -1 to 1
- up_adapter_first: bfloat16 [32, 3584, 32], P(('groups', 'expert')), parts along dimension 0, may hold values from -0.09375 to 0.09375
- up_adapter_second: bfloat16 [32, 32, 1024], P(('groups', 'expert')), parts along dimension 0, may hold values from -1 to 1
Outputs:
- in_grad: bfloat16 [4096, 3584], P(('groups', 'expert')), parts along dimension 0
- router_grad: float32 [7168, 16], P(('groups', 'expert')), parts along dimension 0
- grad_gate_a: float32 [32, 3584, 32], P(('groups', 'expert')), parts along dimension 0
- grad_gate_b: float32 [32, 32, 1024], P(('groups', 'expert')), parts along dimension 0
- grad_up_a: float32 [32, 3584, 32], P(('groups', 'expert')), parts along dimension 0
- grad_up_b: float32 [32, 32, 1024], P(('groups', 'expert')), parts along dimension 0
The draws below stay inside these ranges and needn't reach their ends.
There are 2 independent parts, one for each index of `groups`. The reference program is written for one: setup_inputs(seed, part) draws one part's arguments, and reference() takes and returns one part's arrays. A program takes and returns all parts, laid end to end along the dimension named above; an argument that names none is the same for every part. Nothing has to cross between parts.
Inputs may be any that keep to these rules, and one draw needn't show every extreme that they name: `routed_expert_index`: within the 128 rows of one device no expert is named by more than 48 rows, and in every draw some expert is named by exactly 48 rows of some device; the 4 experts of a row differ.
All inputs are finite; a program needn't handle non-finite values.
Results may differ from the reference program's by a relative error of at most 0.0071.
Values may be sent and summed in bfloat16 or wider, within the bound.
No kernel may reach another device: no remote copies, remote signals or barrier semaphores. Data moves between devices by JAX's collectives and lax.ppermute only.
A program may use at most 192 MiB of HBM per device.

```python
import math
import jax
import jax.numpy as jnp
import numpy as np
from jax import lax

MODEL_WIDTH = 3584
HIDDEN_UNITS = 1024
ADAPTER_RANK = 32
TOPK = 4
TOK_DEV = 128
EXPERT_COUNT = 16
CAP = 48
TOKENS = 2048


def spiked(drawn, key, source, target, blocks, factor):
    owner, partner = [(jnp.arange(drawn.shape[axis_at]) // (drawn.shape[axis_at] // blocks)).reshape([-1 if axis == axis_at else 1 for axis in range(drawn.ndim)]) for axis_at in (source, target)]
    chosen = jax.random.permutation(key, blocks)[partner]
    strong = (owner == chosen) | (owner == (partner + blocks // 2) % blocks)
    return jnp.where(strong, factor * drawn, drawn)


def block_levels(rng, shape, shards, low, top_value):
    loudness = 1.0
    for dim, shards_of in shards:
        heights = jax.random.uniform(jax.random.fold_in(jax.random.fold_in(rng, 6), dim), (shards_of,), jnp.float32, low / len(shards), top_value / len(shards))
        loudness = loudness * jnp.repeat(jnp.exp(heights), shape[dim] // shards_of).reshape((-1,) + (1,) * (len(shape) - 1 - dim))
    return loudness


def routed_block(own_key, own, number, rows, number_of, top, reach, lean):
    sequence = jax.random.permutation(own_key, number_of)
    packed, usual = load_shares(number_of, rows * top, reach, lean, True), load_shares(number_of, rows * top, reach, lean, False)
    places = jnp.arange(number_of)

    def named(lengths, turn):
        used = int((lengths > 0).sum())
        fixed = max(1, used // 4)
        passed = fixed + (places - fixed + turn * (used - fixed)) % max(1, number_of - fixed)
        return jnp.zeros((number_of,), jnp.int32).at[sequence[jnp.where(places < fixed, places, passed)]].set(jnp.asarray(lengths, jnp.int32))

    lengths = jnp.where(number % 4 == 0, named(packed, number // 4), named(usual, number - number // 4 - 1))
    mixed = jax.random.permutation(jax.random.fold_in(own, 3), number_of)
    donor, receiver = mixed[0:number_of // 2 * 2:2], mixed[1:number_of // 2 * 2:2]
    room = jnp.minimum(lengths[donor] - 1, reach - lengths[receiver]) // 2
    room = jnp.where((donor == sequence[0]) | (receiver == sequence[0]) | (lengths[receiver] == 0), 0, jnp.maximum(room, 0))
    passed = jax.random.randint(jax.random.fold_in(own, 4), (number_of // 2,), 0, 1 << 20) % (room + 1)
    lengths = lengths.at[donor].add(-passed).at[receiver].add(passed)
    labels = jnp.searchsorted(jnp.cumsum(lengths), jnp.arange(rows * top), side="right").astype(jnp.int32)
    listing = labels.reshape(top, rows).T
    listing = listing[jax.random.permutation(jax.random.fold_in(own, 1), rows)]
    turn = jax.random.randint(jax.random.fold_in(own, 2), (rows, 1), 0, top)
    return jnp.take_along_axis(listing, (jnp.arange(top)[None, :] + turn) % top, axis=1)


def load_shares(count, total, limit, skew, full):
    weights = [(1 << 20) // math.isqrt(grade ** skew) + 1 for grade in range(1, count + 1)]
    largest = limit if full else min(limit, max(-(-total // count), total * weights[0] // sum(weights)))
    least = 1 if total - largest >= count - 1 else 0
    counts, spare = [largest] + [least] * (count - 1), total - largest - least * (count - 1)
    while spare > 0:
        candidates = [i for i in range(1, count) if counts[i] < largest] or [i for i in range(1, count) if counts[i] < limit]
        whole, left = sum([weights[i] for i in candidates]), spare
        for i in candidates:
            more = min(limit - counts[i], max(1, left * weights[i] // whole), spare)
            counts[i] = counts[i] + more
            spare = spare - more
    return np.array(counts)


def gaussian(own_key, dims, width, bound, split=(), kind=jnp.bfloat16):
    entries = width * jax.random.normal(own_key, dims, jnp.float32)
    if split:
        entries = entries * block_levels(own_key, dims, split, -0.22, 0.18)
    return jnp.clip(entries, -bound, bound).astype(kind)


def noise_with(key, dims, width, bound, shards, heavy, kind=jnp.bfloat16):
    array = width * jax.random.normal(key, dims, jnp.float32)
    if shards:
        array = array * block_levels(key, dims, shards, -0.22, 0.18)
    return jnp.clip(spiked(array, jax.random.fold_in(key, 3), *heavy), -bound, bound).astype(kind)


def setup_inputs(seed: int = 0, part: int = 0) -> dict:
    splits = jax.random.split(jax.random.key(seed), 12)
    part_splits = jax.random.split(jax.random.fold_in(splits[11], part), 12)
    layer_input = noise_with(part_splits[0], (TOKENS, MODEL_WIDTH), 1.0, 6.0, ((0, 16),), (0, 1, 16, 2.0))
    output_gradient = gaussian(part_splits[1], (TOKENS, MODEL_WIDTH), 1.0, 6.0, ((0, 16),))
    router_matrix = gaussian(splits[2], (MODEL_WIDTH, EXPERT_COUNT), MODEL_WIDTH ** -0.5, 0.09375)
    routed_expert_index_keys = jax.random.split(jax.random.fold_in(part_splits[3], 1), TOKENS // TOK_DEV)
    routed_expert_index_turns = jax.random.permutation(jax.random.fold_in(part_splits[3], 3), TOKENS // TOK_DEV)
    routed_expert_index = jax.vmap(lambda own, number: routed_block(jax.random.fold_in(part_splits[3], 2), own, number, TOK_DEV, EXPERT_COUNT, TOPK, CAP, 2))(routed_expert_index_keys, routed_expert_index_turns).reshape((TOKENS, TOPK))
    gate_weight_frozen = gaussian(splits[4], (EXPERT_COUNT, MODEL_WIDTH, HIDDEN_UNITS), MODEL_WIDTH ** -0.5, 0.09375, ((0, 16),))
    up_weight_frozen = gaussian(splits[5], (EXPERT_COUNT, MODEL_WIDTH, HIDDEN_UNITS), MODEL_WIDTH ** -0.5, 0.09375, ((0, 16),))
    down_weight_frozen = gaussian(splits[6], (EXPERT_COUNT, HIDDEN_UNITS, MODEL_WIDTH), HIDDEN_UNITS ** -0.5, 0.1875, ((0, 16),))
    gate_adapter_first = gaussian(part_splits[7], (EXPERT_COUNT, MODEL_WIDTH, ADAPTER_RANK), MODEL_WIDTH ** -0.5, 0.09375, ((0, 16),))
    gate_adapter_second = gaussian(part_splits[8], (EXPERT_COUNT, ADAPTER_RANK, HIDDEN_UNITS), ADAPTER_RANK ** -0.5, 1.0, ((0, 16),))
    up_adapter_first = gaussian(part_splits[9], (EXPERT_COUNT, MODEL_WIDTH, ADAPTER_RANK), MODEL_WIDTH ** -0.5, 0.09375, ((0, 16),))
    up_adapter_second = gaussian(part_splits[10], (EXPERT_COUNT, ADAPTER_RANK, HIDDEN_UNITS), ADAPTER_RANK ** -0.5, 1.0, ((0, 16),))
    return {"layer_input": layer_input, "output_gradient": output_gradient, "router_matrix": router_matrix, "routed_expert_index": routed_expert_index, "gate_weight_frozen": gate_weight_frozen, "up_weight_frozen": up_weight_frozen, "down_weight_frozen": down_weight_frozen, "gate_adapter_first": gate_adapter_first, "gate_adapter_second": gate_adapter_second, "up_adapter_first": up_adapter_first, "up_adapter_second": up_adapter_second}


route_scale = 2.5


def dot_nt(left, right):
    return lax.dot_general(left, right, (((1,), (1,)), ((), ())), preferred_element_type=jnp.float32)


def dot_tn(left, right):
    return lax.dot_general(left, right, (((0,), (0,)), ((), ())), preferred_element_type=jnp.float32)


def expert_core(rows_x, rows_dy, rows_w, w_gate, w_up, w_down, a_gate, b_gate, a_up, b_up):
    low_gate = jnp.dot(rows_x, a_gate, preferred_element_type=jnp.float32).astype(jnp.bfloat16)
    low_up = jnp.dot(rows_x, a_up, preferred_element_type=jnp.float32).astype(jnp.bfloat16)
    gate = jnp.dot(rows_x, w_gate, preferred_element_type=jnp.float32) + jnp.dot(low_gate, b_gate, preferred_element_type=jnp.float32)
    upval = jnp.dot(rows_x, w_up, preferred_element_type=jnp.float32) + jnp.dot(low_up, b_up, preferred_element_type=jnp.float32)
    sigma = jax.nn.sigmoid(gate)
    act = gate * sigma
    hidden = act * upval
    back = dot_nt(rows_dy, w_down)
    route_row = jnp.sum(back * hidden, axis=1).astype(jnp.bfloat16)
    scaled = rows_w.astype(jnp.float32)[:, None] * back
    d_gate = (scaled * upval * sigma * (1.0 + gate * (1.0 - sigma))).astype(jnp.bfloat16)
    d_up = (scaled * act).astype(jnp.bfloat16)
    proj_gate = dot_nt(d_gate, b_gate).astype(jnp.bfloat16)
    proj_up = dot_nt(d_up, b_up).astype(jnp.bfloat16)
    row_grad = dot_nt(d_gate, w_gate) + dot_nt(d_up, w_up) + dot_nt(proj_gate, a_gate) + dot_nt(proj_up, a_up)
    adapter_gradient = (dot_tn(rows_x, proj_gate), dot_tn(low_gate, d_gate), dot_tn(rows_x, proj_up), dot_tn(low_up, d_up))
    return row_grad.astype(jnp.bfloat16), route_row, adapter_gradient


def reference(layer_input, output_gradient, router_matrix, routed_expert_index, gate_weight_frozen, up_weight_frozen, down_weight_frozen, gate_adapter_first, gate_adapter_second, up_adapter_first, up_adapter_second):
    scores = jax.nn.sigmoid(jnp.dot(layer_input, router_matrix, preferred_element_type=jnp.float32))
    picked = jnp.take_along_axis(scores, routed_expert_index, axis=1)
    total = jnp.sum(picked, axis=1, keepdims=True)
    combine_b = (route_scale * picked / total).astype(jnp.bfloat16)
    blocks = TOKENS // TOK_DEV
    routed = TOK_DEV * TOPK
    flat_ids = routed_expert_index.reshape(blocks, routed)
    onehot = (flat_ids[:, :, None] == jnp.arange(EXPERT_COUNT, dtype=jnp.int32)[None, None, :]).astype(jnp.int32)
    before = jnp.cumsum(onehot, axis=1) - onehot
    slot = jnp.sum(before * onehot, axis=2).astype(jnp.int32)
    block_ix = jnp.arange(blocks, dtype=jnp.int32)[:, None]
    row_ix = (block_ix * routed + jnp.arange(routed, dtype=jnp.int32)[None, :]).astype(jnp.int32)
    where_pos = (block_ix * CAP + slot).astype(jnp.int32)
    invalid = TOKENS * TOPK
    routing_lookup = jnp.full((EXPERT_COUNT, blocks * CAP), invalid, jnp.int32)
    routing_lookup = routing_lookup.at[flat_ids.reshape(-1), where_pos.reshape(-1)].set(row_ix.reshape(-1))
    flat_w = combine_b.reshape(-1)

    def per_expert_update(carry, inputs):
        gradient_running, router_running = carry
        rows, w_gate, w_up, w_down, a_gate, b_gate, a_up, b_up = inputs
        valid = rows < invalid
        safe = jnp.where(valid, rows, 0).astype(jnp.int32)
        token = (safe // TOPK).astype(jnp.int32)
        rows_x = jnp.where(valid[:, None], layer_input[token], jnp.zeros((), jnp.bfloat16))
        rows_dy = jnp.where(valid[:, None], output_gradient[token], jnp.zeros((), jnp.bfloat16))
        rows_w = jnp.where(valid, flat_w[safe], jnp.zeros((), jnp.bfloat16))
        row_grad, route_row, adapter_gradient = expert_core(rows_x, rows_dy, rows_w, w_gate, w_up, w_down, a_gate, b_gate, a_up, b_up)
        target = jnp.where(valid, token, TOKENS).astype(jnp.int32)
        gradient_running = gradient_running.at[target].add(row_grad.astype(jnp.float32), mode="drop")
        route_target = jnp.where(valid, safe, invalid).astype(jnp.int32)
        router_running = router_running.at[route_target].add(route_row.astype(jnp.float32), mode="drop")
        return (gradient_running, router_running), adapter_gradient

    initial_carry = (jnp.zeros((TOKENS, MODEL_WIDTH), jnp.float32), jnp.zeros((TOKENS * TOPK,), jnp.float32))
    (gradient_running, router_running), adapter_gradient = lax.scan(per_expert_update, initial_carry, (routing_lookup, gate_weight_frozen, up_weight_frozen, down_weight_frozen, gate_adapter_first, gate_adapter_second, up_adapter_first, up_adapter_second))
    route_grad = router_running.reshape(TOKENS, TOPK)
    d_pick = route_scale * (route_grad / total - jnp.sum(route_grad * picked, axis=1, keepdims=True) / (total * total))
    match = (routed_expert_index[:, :, None] == jnp.arange(EXPERT_COUNT, dtype=jnp.int32)[None, None, :]).astype(jnp.float32)
    d_score = jnp.sum(match * d_pick[:, :, None], axis=1)
    d_logit = (d_score * scores * (1.0 - scores)).astype(jnp.bfloat16)
    in_grad = (gradient_running + dot_nt(d_logit, router_matrix)).astype(jnp.bfloat16)
    router_grad = dot_tn(layer_input, d_logit)
    return in_grad, router_grad, adapter_gradient[0], adapter_gradient[1], adapter_gradient[2], adapter_gradient[3]
```

```python
import jax
import jax.numpy as jnp
from jax import lax
from jax.sharding import PartitionSpec as P

route_scale = 2.5
plane = 4
bf16 = jnp.bfloat16
f32 = jnp.float32


def dot_nn(left, right):
    return jnp.dot(left, right, preferred_element_type=f32)


def dot_nt(left, right):
    return lax.dot_general(left, right, (((1,), (1,)), ((), ())), preferred_element_type=f32)


def dot_tn(left, right):
    return lax.dot_general(left, right, (((0,), (0,)), ((), ())), preferred_element_type=f32)


def after(array, *others):
    return lax.optimization_barrier((array, *others))[0]


def expert_rows(rows_x, rows_dy, rows_w, w_gate, w_up, w_down, a_gate, b_gate, a_up, b_up):
    low_gate = dot_nn(rows_x, a_gate).astype(bf16)
    low_up = dot_nn(rows_x, a_up).astype(bf16)
    gate = dot_nn(rows_x, w_gate) + dot_nn(low_gate, b_gate)
    upval = dot_nn(rows_x, w_up) + dot_nn(low_up, b_up)
    sigma = jax.nn.sigmoid(gate)
    act = gate * sigma
    hidden = act * upval
    back = dot_nt(rows_dy, w_down)
    route_row = jnp.sum(back * hidden, axis=1).astype(bf16)
    scaled = rows_w * back
    d_gate = (scaled * upval * sigma * (1.0 + gate * (1.0 - sigma))).astype(bf16)
    d_up = (scaled * act).astype(bf16)
    proj_gate = dot_nt(d_gate, b_gate).astype(bf16)
    proj_up = dot_nt(d_up, b_up).astype(bf16)
    row_grad = (
        dot_nt(d_gate, w_gate)
        + dot_nt(d_up, w_up)
        + dot_nt(proj_gate, a_gate)
        + dot_nt(proj_up, a_up)
    ).astype(bf16)
    return row_grad, route_row, (low_gate, low_up, d_gate, d_up, proj_gate, proj_up)


def solution(mesh):
    devices = mesh.shape["expert"]
    layers = devices // plane

    def along(pairs):
        return [(a * plane + q, b * plane + q) for a, b in pairs for q in range(plane)]

    def across(step):
        return [(i, i ^ step) for i in range(devices)]

    def send(array, pairs):
        return lax.ppermute(array, "expert", pairs)

    def shards(
        layer_input,
        output_gradient,
        router_matrix,
        routed_expert_index,
        gate_weight_frozen,
        up_weight_frozen,
        down_weight_frozen,
        gate_adapter_first,
        gate_adapter_second,
        up_adapter_first,
        up_adapter_second,
    ):
        tok, width = layer_input.shape
        topk = routed_expert_index.shape[1]
        experts = router_matrix.shape[1]
        capacity = 3 * tok * topk // (2 * experts)
        me = lax.axis_index("expert")
        layer = me // plane
        place = me % plane
        mats = (
            gate_weight_frozen[0],
            up_weight_frozen[0],
            down_weight_frozen[0],
            gate_adapter_first[0],
            gate_adapter_second[0],
            up_adapter_first[0],
            up_adapter_second[0],
        )

        scores = jax.nn.sigmoid(dot_nn(layer_input, router_matrix))
        expert_ids = jnp.arange(experts, dtype=jnp.int32)
        mask = jnp.sum(
            (routed_expert_index[:, :, None] == expert_ids[None, None, :]).astype(f32), axis=1
        )
        picked = mask * scores
        total = jnp.sum(picked, axis=1, keepdims=True)
        combine = (route_scale * picked / total).astype(bf16)
        earlier = (
            jnp.arange(tok)[:, None] > jnp.arange(tok)[None, :]
        ).astype(bf16)
        slot = dot_nn(earlier, mask.astype(bf16))
        slot_dense = mask * (slot + 1.0)
        meta_width = -(-2 * experts // 128) * 128
        meta = jnp.concatenate(
            [
                slot_dense.astype(bf16),
                combine,
                jnp.zeros((tok, meta_width - 2 * experts), bf16),
            ],
            axis=1,
        )
        x_ext = jnp.concatenate([layer_input, meta], axis=1)
        dy = output_gradient

        near = [(z, z ^ 1) for z in range(layers)]
        if layers == 4:
            mid = (layer == 1) | (layer == 2)
            end_to_mid = along([(0, 2), (3, 1)])
            mid_to_end = along([(1, 3), (2, 0)])
            mid_swap = along([(1, 2), (2, 1)])
            forward = along([(1, 0), (2, 3)])
            backward = along([(0, 1), (3, 2)])
            dy_p1 = send(dy, end_to_mid)
            dy_a = send(dy, along(near))
            x_p1 = send(x_ext, end_to_mid)
            x_a = send(x_ext, along(near))
            x_p4 = send(x_p1, forward)
            dy_p4 = send(dy_p1, forward)
            x_p3 = send(after(x_ext, x_p1), mid_swap)
            dy_p3 = send(after(dy, dy_p1), mid_swap)
            x_p5 = send(after(x_ext, x_p3), mid_to_end)
            dy_p5 = send(after(dy, dy_p3), mid_to_end)
            blocks = [
                (x_ext, dy, layer),
                (x_a, dy_a, layer ^ 1),
                (
                    jnp.where(mid, x_p1, x_p4),
                    jnp.where(mid, dy_p1, dy_p4),
                    jnp.where(mid, layer ^ 2, layer ^ 3),
                ),
                (
                    jnp.where(mid, x_p3, x_p5),
                    jnp.where(mid, dy_p3, dy_p5),
                    jnp.where(mid, layer ^ 3, layer ^ 2),
                ),
            ]
        else:
            blocks = [(x_ext, dy, layer)]
            for g in range(1, layers):
                pairs = across(g * plane)
                blocks.append((send(x_ext, pairs), send(dy, pairs), layer ^ g))

        here = layer * plane + (place ^ jnp.arange(plane, dtype=jnp.int32))
        column = (expert_ids[:, None] == here[None, :]).astype(bf16)
        mine = (jnp.arange(meta_width) == experts + me).astype(f32)
        slots = jnp.arange(1, capacity + 1, dtype=jnp.int32).astype(f32)

        results = []
        for x_block, dy_block, _ in blocks:
            block_slots = dot_nn(x_block[:, width : width + experts], column)
            placed = (
                (block_slots[:, :, None] == slots[None, None, :])
                .astype(bf16)
                .reshape(tok, plane * capacity)
            )
            sent_x = dot_tn(placed, x_block).astype(bf16)
            sent_dy = dot_tn(placed, dy_block).astype(bf16)
            got_x = [sent_x[:capacity]]
            got_dy = [sent_dy[:capacity]]
            for p in range(1, plane):
                got_x.append(send(sent_x[p * capacity : (p + 1) * capacity], across(p)))
                got_dy.append(send(sent_dy[p * capacity : (p + 1) * capacity], across(p)))
            rows_ext = jnp.concatenate(got_x, axis=0)
            rows_dy = jnp.concatenate(got_dy, axis=0)
            rows_x = rows_ext[:, :width]
            rows_w = jnp.sum(rows_ext[:, width:].astype(f32) * mine[None, :], axis=1, keepdims=True)
            row_grad, route_row, kept = expert_rows(rows_x, rows_dy, rows_w, *mats)
            back = [row_grad[:capacity]]
            for p in range(1, plane):
                back.append(send(row_grad[p * capacity : (p + 1) * capacity], across(p)))
            partial = dot_nn(placed, jnp.concatenate(back, axis=0))
            results.append((partial, route_row, rows_x, kept))

        terms = [results[0][0]]
        if layers == 4:
            terms.append(send(results[1][0].astype(bf16), along(near)))
            third = results[2][0]
            hop = send(third.astype(bf16), backward)
            fourth = results[3][0].astype(bf16)
            terms.append(send(fourth, along([(0, 2), (3, 1)])))
            terms.append(send(fourth, along([(1, 2), (2, 1)])))
            terms.append(send((third + hop.astype(f32)).astype(bf16), mid_to_end))
        else:
            for g in range(1, layers):
                terms.append(send(results[g][0].astype(bf16), across(g * plane)))

        route_all = jnp.stack([r[1] for r in results]).reshape(layers * plane, capacity)
        origin = (
            jnp.stack([b[2] for b in blocks])[:, None] * plane
            + (place ^ jnp.arange(plane, dtype=jnp.int32))[None, :]
        ).reshape(-1)
        order = (origin[None, :] == jnp.arange(devices, dtype=jnp.int32)[:, None]).astype(bf16)
        route_sorted = dot_nn(order, route_all).astype(bf16)
        ret_route = lax.all_to_all(
            route_sorted, "expert", split_axis=0, concat_axis=0, tiled=True
        ).astype(f32)
        hit = slot_dense[:, :, None] == slots[None, None, :]
        route_grad = jnp.sum(jnp.where(hit, ret_route[None, :, :], 0.0), axis=2)
        shared = jnp.sum(route_grad * picked, axis=1, keepdims=True) / (total * total)
        d_pick = route_scale * (route_grad / total - shared)
        d_logit = (mask * d_pick * scores * (1.0 - scores)).astype(bf16)

        router_part = dot_tn(d_logit, layer_input)
        share = width // devices
        router_part = router_part.reshape(experts, devices, share).transpose(1, 0, 2)
        router_got = lax.all_to_all(router_part, "expert", split_axis=0, concat_axis=0, tiled=True)
        router_grad = jnp.sum(router_got, axis=0).T

        in_grad = dot_nt(d_logit, router_matrix)
        for term in terms:
            in_grad = in_grad + term.astype(f32)
        in_grad = in_grad.astype(bf16)

        rows_x = jnp.concatenate([r[2] for r in results], axis=0)
        low_gate, low_up, d_gate, d_up, proj_gate, proj_up = (
            jnp.concatenate([r[3][i] for r in results], axis=0) for i in range(6)
        )
        return (
            in_grad,
            router_grad,
            dot_tn(rows_x, proj_gate)[None],
            dot_tn(low_gate, d_gate)[None],
            dot_tn(rows_x, proj_up)[None],
            dot_tn(low_up, d_up)[None],
        )

    rows = P(("groups", "expert"), None)
    stack = P(("groups", "expert"), None, None)
    frozen = P("expert", None, None)
    in_specs = (rows, rows, P(), rows, frozen, frozen, frozen, stack, stack, stack, stack)
    out_specs = (rows, rows, stack, stack, stack, stack)
    return jax.shard_map(shards, mesh=mesh, in_specs=in_specs, out_specs=out_specs, check_vma=False)
```

```python
import functools

import jax
import jax.numpy as jnp
from jax import lax
from jax.experimental import pallas as pl
from jax.experimental.pallas import tpu as pltpu
from jax.sharding import PartitionSpec as P

route_scale = 2.5
plane = 4
bf16 = jnp.bfloat16
f32 = jnp.float32
vmem_bytes = 56 * 1024 * 1024


def dot_nn(left, right):
    return jnp.dot(left, right, preferred_element_type=f32)


def dot_nt(left, right):
    return lax.dot_general(left, right, (((1,), (1,)), ((), ())), preferred_element_type=f32)


def dot_tn(left, right):
    return lax.dot_general(left, right, (((0,), (0,)), ((), ())), preferred_element_type=f32)


def after(array, *others):
    return lax.optimization_barrier((array, *others))[0]


def chunks(start, stop, step):
    return [(at, min(at + step, stop)) for at in range(start, stop, step)]


def whole_block(shape):
    return pl.BlockSpec(shape, lambda *_: (0,) * len(shape), pipeline_mode=pl.Buffered(1))


vmem = pl.BlockSpec(memory_space=pltpu.VMEM)
smem = pl.BlockSpec(memory_space=pltpu.SMEM)


def select_kernel(parts, meta_at, slots_held, cap, flag_ref, guide_ref, *refs):
    count = sum(len(p) for p in parts)
    ins, outs = refs[:count], refs[count:]
    tok = ins[0].shape[0]
    flag = flag_ref[0] == 1
    groups = []
    for part in parts:
        groups.append((part, ins[: len(part)]))
        ins = ins[len(part) :]

    def load(group, first, last):
        part, arrays = group
        values = [a[:, at + first : at + last] for (at, _), a in zip(part, arrays)]
        return values[0] if len(values) == 1 else jnp.where(flag, values[0], values[1])

    if slots_held:
        placed = guide_ref[...]
    else:
        meta = load(groups[0], *meta_at)
        named = dot_nt(guide_ref[...], meta)
        rank = lax.broadcasted_iota(jnp.int32, (cap, tok), 0).astype(f32) + 1.0
        placed = jnp.concatenate(
            [(named[p : p + 1, :] == rank).astype(bf16) for p in range(plane)], axis=0
        )
        outs[plane][...] = placed
    at = 0
    for group in groups:
        length = group[0][0][1]
        for first, last in chunks(0, length, 512):
            rows = dot_nn(placed, load(group, first, last)).astype(bf16)
            for p in range(plane):
                outs[p][:, at + first : at + last] = rows[p * cap : (p + 1) * cap]
        at += length


def select_rows(flag, guide, parts, arrays, meta_at, slots_held, cap):
    tok = arrays[0].shape[0]
    length = sum(p[0][1] for p in parts)
    shapes = [jax.ShapeDtypeStruct((cap, length), bf16)] * plane
    if not slots_held:
        shapes.append(jax.ShapeDtypeStruct((plane * cap, tok), bf16))
    return pl.pallas_call(
        functools.partial(select_kernel, parts, meta_at, slots_held, cap),
        out_shape=shapes,
        in_specs=[smem] + [vmem] * (1 + len(arrays)),
        out_specs=[vmem] * len(shapes),
        compiler_params=pltpu.CompilerParams(vmem_limit_bytes=vmem_bytes),
        cost_estimate=pl.CostEstimate(
            flops=2 * plane * cap * tok * length,
            bytes_accessed=2 * length * (tok + plane * cap),
            transcendentals=0,
        ),
    )(flag, guide, *arrays)


def sum_kernel(extra, cap, placed_ref, *refs):
    pieces, out = refs[:plane], refs[-1]
    for first, last in chunks(0, out.shape[1], 512):
        rows = jnp.concatenate([p[:, first:last] for p in pieces], axis=0)
        total = dot_tn(placed_ref[...], rows)
        for more in refs[plane : plane + extra]:
            total = total + more[:, first:last].astype(f32)
        out[:, first:last] = total.astype(bf16)


def sum_rows(placed, pieces, extra):
    cap, width = pieces[0].shape
    tok = placed.shape[1]
    return pl.pallas_call(
        functools.partial(sum_kernel, len(extra), cap),
        out_shape=jax.ShapeDtypeStruct((tok, width), bf16),
        in_specs=[vmem] * (1 + plane + len(extra)),
        out_specs=vmem,
        compiler_params=pltpu.CompilerParams(vmem_limit_bytes=vmem_bytes),
        cost_estimate=pl.CostEstimate(
            flops=2 * plane * cap * tok * width,
            bytes_accessed=2 * width * (2 * tok + plane * cap),
            transcendentals=0,
        ),
    )(placed, *pieces, *extra)


def expert_kernel(
    pieces, cap, width, rank, mine_ref, wg_ref, wu_ref, wd_ref, ag_ref, au_ref, bg_ref, bu_ref, *refs
):
    count = sum(len(p) for p in pieces)
    ins, refs = refs[:count], refs[count:]
    back_refs, refs = refs[: len(pieces)], refs[len(pieces) :]
    route_ref, ga_ref, gbg_ref, gbu_ref = refs[:4]
    xs, dys, weight, low, proj, both, acc = refs[4:]
    step = pl.program_id(0)
    tail = width + mine_ref.shape[1]

    @pl.when(step == 0)
    def _():
        left = ins
        for i, piece in enumerate(pieces):
            rows = slice(i * cap, (i + 1) * cap)
            x_ref, dy_ref = left[0], left[len(piece) - 1]
            left = left[len(piece) :]
            offset = tail if len(piece) == 1 else 0
            xs[rows, :] = x_ref[:, :width]
            dys[rows, :] = dy_ref[:, offset : offset + width]
            weight[rows, :] = jnp.sum(
                x_ref[:, width:tail].astype(f32) * mine_ref[...], axis=1, keepdims=True
            )
        both[:rank, :] = ag_ref[...]
        both[rank:, :] = au_ref[...]
        low[...] = dot_nt(xs[...], both[...]).astype(bf16)
        proj[...] = jnp.zeros_like(proj)
        acc[...] = jnp.zeros_like(acc)
        route_ref[...] = jnp.zeros_like(route_ref)

    bg, bu = bg_ref[...], bu_ref[...]
    low_gate, low_up = low[:, :rank], low[:, rank:]
    gate = dot_nn(xs[...], wg_ref[...]) + dot_nn(low_gate, bg)
    upval = dot_nn(xs[...], wu_ref[...]) + dot_nn(low_up, bu)
    back = dot_nt(dys[...], wd_ref[...])
    sigma = jax.nn.sigmoid(gate)
    act = gate * sigma
    route_ref[...] += jnp.sum(back * (act * upval), axis=1, keepdims=True)
    scaled = weight[...] * back
    d_gate = (scaled * upval * sigma * (1.0 + gate * (1.0 - sigma))).astype(bf16)
    d_up = (scaled * act).astype(bf16)
    gbg_ref[...] = dot_tn(low_gate, d_gate)
    gbu_ref[...] = dot_tn(low_up, d_up)
    proj[:, :rank] += dot_nt(d_gate, bg)
    proj[:, rank:] += dot_nt(d_up, bu)
    for first, last in chunks(0, width, 512):
        acc[:, first:last] += dot_nt(d_gate, wg_ref[first:last, :]) + dot_nt(
            d_up, wu_ref[first:last, :]
        )

    @pl.when(step == pl.num_programs(0) - 1)
    def _():
        proj_b = proj[...].astype(bf16)
        for first, last in chunks(0, width, 512):
            rows = (acc[:, first:last] + dot_nn(proj_b, both[:, first:last])).astype(bf16)
            for i, out in enumerate(back_refs):
                out[:, first:last] = rows[i * cap : (i + 1) * cap]
            ga_ref[:, first:last] = dot_tn(proj_b, xs[:, first:last])


def expert_rows(mine, mats, pieces):
    w_gate, w_up, w_down, a_gate, a_up, b_gate, b_up = mats
    width, hidden = w_gate.shape
    rank = a_gate.shape[0]
    cap = pieces[0][0].shape[0]
    rows = cap * len(pieces)
    tile = 256
    arrays = [a for piece in pieces for a in piece]
    return pl.pallas_call(
        functools.partial(expert_kernel, [(0,) * len(p) for p in pieces], cap, width, rank),
        grid=(hidden // tile,),
        in_specs=[
            whole_block(mine.shape),
            pl.BlockSpec((width, tile), lambda j: (0, j)),
            pl.BlockSpec((width, tile), lambda j: (0, j)),
            pl.BlockSpec((tile, width), lambda j: (j, 0)),
            whole_block(a_gate.shape),
            whole_block(a_up.shape),
            pl.BlockSpec((rank, tile), lambda j: (0, j)),
            pl.BlockSpec((rank, tile), lambda j: (0, j)),
        ]
        + [whole_block(a.shape) for a in arrays],
        out_shape=[jax.ShapeDtypeStruct((cap, width), bf16)] * len(pieces)
        + [
            jax.ShapeDtypeStruct((rows, 1), f32),
            jax.ShapeDtypeStruct((2 * rank, width), f32),
            jax.ShapeDtypeStruct((rank, hidden), f32),
            jax.ShapeDtypeStruct((rank, hidden), f32),
        ],
        out_specs=[whole_block((cap, width))] * len(pieces)
        + [
            whole_block((rows, 1)),
            whole_block((2 * rank, width)),
            pl.BlockSpec((rank, tile), lambda j: (0, j)),
            pl.BlockSpec((rank, tile), lambda j: (0, j)),
        ],
        scratch_shapes=[
            pltpu.VMEM((rows, width), bf16),
            pltpu.VMEM((rows, width), bf16),
            pltpu.VMEM((rows, 1), f32),
            pltpu.VMEM((rows, 2 * rank), bf16),
            pltpu.VMEM((rows, 2 * rank), f32),
            pltpu.VMEM((2 * rank, width), bf16),
            pltpu.VMEM((rows, width), f32),
        ],
        compiler_params=pltpu.CompilerParams(vmem_limit_bytes=vmem_bytes),
        cost_estimate=pl.CostEstimate(
            flops=2 * 5 * rows * width * hidden,
            bytes_accessed=2 * 3 * width * hidden + 6 * rows * width,
            transcendentals=rows * hidden,
        ),
    )(mine, w_gate, w_up, w_down, a_gate, a_up, b_gate, b_up, *arrays)


def solution(mesh):
    devices = mesh.shape["expert"]
    layers = devices // plane

    def along(pairs):
        return [(a * plane + q, b * plane + q) for a, b in pairs for q in range(plane)]

    def across(step):
        return [(i, i ^ step) for i in range(devices)]

    def send(array, pairs):
        return lax.ppermute(array, "expert", pairs)

    def spread(pieces):
        return [pieces[0]] + [send(pieces[p], across(p)) for p in range(1, plane)]

    def shards(
        layer_input,
        output_gradient,
        router_matrix,
        routed_expert_index,
        gate_weight_frozen,
        up_weight_frozen,
        down_weight_frozen,
        gate_adapter_first,
        gate_adapter_second,
        up_adapter_first,
        up_adapter_second,
    ):
        tok, width = layer_input.shape
        topk = routed_expert_index.shape[1]
        experts = router_matrix.shape[1]
        capacity = 3 * tok * topk // (2 * experts)
        cap = -(-capacity // 16) * 16
        me = lax.axis_index("expert")
        layer = me // plane
        place = me % plane
        mats = (
            gate_weight_frozen[0],
            up_weight_frozen[0],
            down_weight_frozen[0],
            gate_adapter_first[0].T,
            up_adapter_first[0].T,
            gate_adapter_second[0],
            up_adapter_second[0],
        )
        dy = output_gradient

        scores = jax.nn.sigmoid(dot_nn(layer_input, router_matrix))
        expert_ids = jnp.arange(experts, dtype=jnp.int32)
        mask = jnp.sum(
            (routed_expert_index[:, :, None] == expert_ids[None, None, :]).astype(f32), axis=1
        )
        picked = mask * scores
        total = jnp.sum(picked, axis=1, keepdims=True)
        combine = (route_scale * picked / total).astype(bf16)
        earlier = (jnp.arange(tok)[:, None] > jnp.arange(tok)[None, :]).astype(bf16)
        slot_dense = mask * (dot_nn(earlier, mask.astype(bf16)) + 1.0)
        meta_width = -(-2 * experts // 128) * 128
        meta = jnp.concatenate(
            [slot_dense.astype(bf16), combine, jnp.zeros((tok, meta_width - 2 * experts), bf16)],
            axis=1,
        )
        x_ext = jnp.concatenate([layer_input, meta], axis=1)
        own = jnp.concatenate([x_ext, dy], axis=1)
        ext = width + meta_width
        full = ext + width
        meta_at = (width, ext)

        here = layer * plane + (place ^ jnp.arange(plane, dtype=jnp.int32))
        guide = jnp.zeros((16, meta_width), bf16)
        guide = guide.at[:plane].set(
            (here[:, None] == jnp.arange(meta_width, dtype=jnp.int32)[None, :]).astype(bf16)
        )
        mine = (jnp.arange(meta_width) == experts + me).astype(f32)[None, :]
        take = functools.partial(select_rows, cap=cap)

        if layers == 4:
            mid = (layer == 1) | (layer == 2)
            flag = mid.astype(jnp.int32)[None]
            ends_in = along([(1, 0), (2, 3)])
            second = along([(0, 2), (3, 1), (1, 0), (2, 3)])
            dy_2 = send(dy, second)
            x_2 = send(x_ext, second)
            *sel_0, placed_0 = take(flag, guide, [[(0, full)]], [own], meta_at, False)
            got_0 = spread(sel_0)
            own_3 = after(own, x_2, dy_2)
            onward = jnp.where(mid, jnp.concatenate([x_2, dy_2], axis=1), own)
            block_2 = send(onward, across(plane))
            block_3 = send(own_3, along([(1, 2), (2, 1)]))
            *sel_1, placed_1 = take(
                flag, guide, [[(0, ext)], [(0, width)]], [x_2, dy_2], meta_at, False
            )
            sel_1 = lax.optimization_barrier((*sel_1, *got_0))[:plane]
            got_1 = spread(sel_1)
            x_5, dy_5, _, _ = lax.optimization_barrier((x_ext, dy, block_2, block_3))
            x_3 = send(x_5, along([(1, 3), (2, 0)]))
            dy_3 = send(dy_5, along([(1, 3), (2, 0)]))
            *sel_2, placed_2 = take(flag, guide, [[(0, full)]], [block_2], meta_at, False)
            sel_2 = lax.optimization_barrier((*sel_2, *got_1))[:plane]
            got_2 = spread(sel_2)
            early = lax.optimization_barrier((*got_0, *got_1, sel_2[0]))[: 2 * plane]
            done_01 = expert_rows(mine, mats, [(a,) for a in early])
            back_0 = spread(done_01[:plane])
            back_1 = spread(done_01[plane : 2 * plane])
            done_2 = expert_rows(mine, mats, [(a,) for a in got_2])
            *sel_3x, placed_3 = take(
                flag, guide, [[(0, ext), (0, ext)]], [block_3, x_3], meta_at, False
            )
            sel_3y = take(flag, placed_3, [[(ext, width), (0, width)]], [block_3, dy_3], None, True)
            got_3x = spread(sel_3x)
            got_3y = spread(sel_3y)
            done_3 = expert_rows(mine, mats, list(zip(got_3x, got_3y)))
            back_2 = spread(done_2[:plane])
            back_3 = spread(done_3[:plane])

            part_0 = sum_rows(placed_0, back_0, [])
            part_1 = sum_rows(placed_1, back_1, [])
            term_1 = send(part_1, along([(0, 1), (3, 2)]))
            part_2 = sum_rows(placed_2, back_2, [])
            term_2 = send(part_2, across(plane))
            joined = (part_1.astype(f32) + term_2.astype(f32)).astype(bf16)
            term_3 = send(joined, along([(1, 3), (2, 0)]))
            part_3 = sum_rows(placed_3, back_3, [])
            term_4 = send(part_3, along([(1, 2), (2, 1)]))
            term_5 = send(part_3, along([(0, 2), (3, 1)]))
            terms = [part_0, term_1, jnp.where(mid, jnp.zeros((), bf16), term_2), term_3, term_4, term_5]
            done = [done_01, done_2, done_3]
            counts = [2, 1, 1]
            sources = [
                layer,
                jnp.where(mid, layer ^ 2, layer ^ 1),
                jnp.where(mid, layer ^ 1, layer ^ 3),
                jnp.where(mid, layer ^ 3, layer ^ 2),
            ]
        else:
            flag = jnp.zeros((1,), jnp.int32)
            done, counts, sources, terms = [], [], [], []
            for g in range(layers):
                block = own if g == 0 else send(own, across(g * plane))
                *sel, placed = take(flag, guide, [[(0, full)]], [block], meta_at, False)
                result = expert_rows(mine, mats, [(a,) for a in spread(sel)])
                part = sum_rows(placed, spread(result[:plane]), [])
                terms.append(part if g == 0 else send(part, across(g * plane)))
                done.append(result)
                counts.append(1)
                sources.append(layer ^ g)

        route_all = jnp.concatenate(
            [d[c * plane].reshape(c * plane, cap) for d, c in zip(done, counts)], axis=0
        )
        origin = (
            jnp.stack(sources)[:, None] * plane
            + (place ^ jnp.arange(plane, dtype=jnp.int32))[None, :]
        ).reshape(-1)
        order = (origin[None, :] == jnp.arange(devices, dtype=jnp.int32)[:, None]).astype(bf16)
        route_sorted = dot_nn(order, route_all.astype(bf16)).astype(bf16)
        ret_route = lax.all_to_all(
            route_sorted, "expert", split_axis=0, concat_axis=0, tiled=True
        ).astype(f32)
        slots = jnp.arange(1, cap + 1, dtype=jnp.int32).astype(f32)
        hit = slot_dense[:, :, None] == slots[None, None, :]
        route_grad = jnp.sum(jnp.where(hit, ret_route[None, :, :], 0.0), axis=2)
        shared = jnp.sum(route_grad * picked, axis=1, keepdims=True) / (total * total)
        d_pick = route_scale * (route_grad / total - shared)
        d_logit = (mask * d_pick * scores * (1.0 - scores)).astype(bf16)

        router_part = dot_tn(d_logit, layer_input)
        share = width // devices
        router_part = router_part.reshape(experts, devices, share).transpose(1, 0, 2)
        router_got = lax.all_to_all(router_part, "expert", split_axis=0, concat_axis=0, tiled=True)
        router_grad = jnp.sum(router_got, axis=0).T

        in_grad = dot_nt(d_logit, router_matrix)
        for term in terms:
            in_grad = in_grad + term.astype(f32)
        in_grad = in_grad.astype(bf16)

        rank = gate_adapter_second.shape[1]
        grad_a = sum(d[c * plane + 1] for d, c in zip(done, counts))
        grad_gate_b = sum(d[c * plane + 2] for d, c in zip(done, counts))
        grad_up_b = sum(d[c * plane + 3] for d, c in zip(done, counts))
        return (
            in_grad,
            router_grad,
            grad_a[:rank].T[None],
            grad_gate_b[None],
            grad_a[rank:].T[None],
            grad_up_b[None],
        )

    rows = P(("groups", "expert"), None)
    stack = P(("groups", "expert"), None, None)
    frozen = P("expert", None, None)
    in_specs = (rows, rows, P(), rows, frozen, frozen, frozen, stack, stack, stack, stack)
    out_specs = (rows, rows, stack, stack, stack, stack)
    return jax.shard_map(shards, mesh=mesh, in_specs=in_specs, out_specs=out_specs, check_vma=False)
```

```python
import functools

import jax
import jax.numpy as jnp
from jax import lax
from jax.experimental import pallas as pl
from jax.experimental.pallas import tpu as pltpu
from jax.sharding import PartitionSpec as P

route_scale = 2.5
plane = 4
bf16 = jnp.bfloat16
f32 = jnp.float32
vmem_bytes = 56 * 1024 * 1024
light = pl.CostEstimate(flops=1024, bytes_accessed=1024, transcendentals=0)


def dot_nn(left, right):
    return jnp.dot(left, right, preferred_element_type=f32)


def dot_nt(left, right):
    return lax.dot_general(left, right, (((1,), (1,)), ((), ())), preferred_element_type=f32)


def dot_tn(left, right):
    return lax.dot_general(left, right, (((0,), (0,)), ((), ())), preferred_element_type=f32)


def after(array, *others):
    return lax.optimization_barrier((array, *others))[0]


def chunks(start, stop, step):
    return [(at, min(at + step, stop)) for at in range(start, stop, step)]


def whole_block(shape):
    return pl.BlockSpec(shape, lambda *_: (0,) * len(shape), pipeline_mode=pl.Buffered(1))


vmem = pl.BlockSpec(memory_space=pltpu.VMEM)
smem = pl.BlockSpec(memory_space=pltpu.SMEM)


def select_kernel(parts, meta_at, slots_held, cap, flag_ref, guide_ref, *refs):
    count = sum(len(p) for p in parts)
    ins, outs = refs[:count], refs[count:]
    tok = ins[0].shape[0]
    flag = flag_ref[0] == 1
    groups = []
    for part in parts:
        groups.append((part, ins[: len(part)]))
        ins = ins[len(part) :]

    def load(group, first, last):
        part, arrays = group
        values = [a[:, at + first : at + last] for (at, _), a in zip(part, arrays)]
        return values[0] if len(values) == 1 else jnp.where(flag, values[0], values[1])

    if slots_held:
        placed = guide_ref[...]
    else:
        meta = load(groups[0], *meta_at)
        named = dot_nt(guide_ref[...], meta)
        rank = lax.broadcasted_iota(jnp.int32, (cap, tok), 0).astype(f32) + 1.0
        placed = jnp.concatenate(
            [(named[p : p + 1, :] == rank).astype(bf16) for p in range(plane)], axis=0
        )
        outs[plane][...] = placed
    at = 0
    for group in groups:
        length = group[0][0][1]
        for first, last in chunks(0, length, 512):
            rows = dot_nn(placed, load(group, first, last)).astype(bf16)
            for p in range(plane):
                outs[p][:, at + first : at + last] = rows[p * cap : (p + 1) * cap]
        at += length


def select_rows(flag, guide, parts, arrays, meta_at, slots_held, cap):
    tok = arrays[0].shape[0]
    length = sum(p[0][1] for p in parts)
    shapes = [jax.ShapeDtypeStruct((cap, length), bf16)] * plane
    if not slots_held:
        shapes.append(jax.ShapeDtypeStruct((plane * cap, tok), bf16))
    return pl.pallas_call(
        functools.partial(select_kernel, parts, meta_at, slots_held, cap),
        out_shape=shapes,
        in_specs=[smem] + [vmem] * (1 + len(arrays)),
        out_specs=[vmem] * len(shapes),
        compiler_params=pltpu.CompilerParams(vmem_limit_bytes=vmem_bytes),
        cost_estimate=light,
    )(flag, guide, *arrays)


def sum_kernel(extra, cap, placed_ref, *refs):
    pieces, out = refs[:plane], refs[-1]
    for first, last in chunks(0, out.shape[1], 512):
        rows = jnp.concatenate([p[:, first:last] for p in pieces], axis=0)
        total = dot_tn(placed_ref[...], rows)
        for more in refs[plane : plane + extra]:
            total = total + more[:, first:last].astype(f32)
        out[:, first:last] = total.astype(bf16)


def sum_rows(placed, pieces, extra):
    cap, width = pieces[0].shape
    tok = placed.shape[1]
    return pl.pallas_call(
        functools.partial(sum_kernel, len(extra), cap),
        out_shape=jax.ShapeDtypeStruct((tok, width), bf16),
        in_specs=[vmem] * (1 + plane + len(extra)),
        out_specs=vmem,
        compiler_params=pltpu.CompilerParams(vmem_limit_bytes=vmem_bytes),
        cost_estimate=light,
    )(placed, *pieces, *extra)


def expert_kernel(
    pieces, cap, width, rank, mine_ref, wg_ref, wu_ref, wd_ref, ag_ref, au_ref, bg_ref, bu_ref, *refs
):
    count = sum(len(p) for p in pieces)
    ins, refs = refs[:count], refs[count:]
    back_refs, refs = refs[: len(pieces)], refs[len(pieces) :]
    route_ref, ga_ref, gbg_ref, gbu_ref = refs[:4]
    xs, dys, weight, low, proj, both, acc = refs[4:]
    step = pl.program_id(0)
    tail = width + mine_ref.shape[1]

    @pl.when(step == 0)
    def _():
        left = ins
        for i, piece in enumerate(pieces):
            rows = slice(i * cap, (i + 1) * cap)
            x_ref, dy_ref = left[0], left[len(piece) - 1]
            left = left[len(piece) :]
            offset = tail if len(piece) == 1 else 0
            xs[rows, :] = x_ref[:, :width]
            dys[rows, :] = dy_ref[:, offset : offset + width]
            weight[rows, :] = jnp.sum(
                x_ref[:, width:tail].astype(f32) * mine_ref[...], axis=1, keepdims=True
            )
        both[:rank, :] = ag_ref[...]
        both[rank:, :] = au_ref[...]
        low[...] = dot_nt(xs[...], both[...]).astype(bf16)
        proj[...] = jnp.zeros_like(proj)
        acc[...] = jnp.zeros_like(acc)
        route_ref[...] = jnp.zeros_like(route_ref)

    bg, bu = bg_ref[...], bu_ref[...]
    low_gate, low_up = low[:, :rank], low[:, rank:]
    gate = dot_nn(xs[...], wg_ref[...]) + dot_nn(low_gate, bg)
    upval = dot_nn(xs[...], wu_ref[...]) + dot_nn(low_up, bu)
    back = dot_nt(dys[...], wd_ref[...])
    sigma = jax.nn.sigmoid(gate)
    act = gate * sigma
    route_ref[...] += jnp.sum(back * (act * upval), axis=1, keepdims=True)
    scaled = weight[...] * back
    d_gate = (scaled * upval * sigma * (1.0 + gate * (1.0 - sigma))).astype(bf16)
    d_up = (scaled * act).astype(bf16)
    gbg_ref[...] = dot_tn(low_gate, d_gate)
    gbu_ref[...] = dot_tn(low_up, d_up)
    proj[:, :rank] += dot_nt(d_gate, bg)
    proj[:, rank:] += dot_nt(d_up, bu)
    for first, last in chunks(0, width, 512):
        acc[:, first:last] += dot_nt(d_gate, wg_ref[first:last, :]) + dot_nt(
            d_up, wu_ref[first:last, :]
        )

    @pl.when(step == pl.num_programs(0) - 1)
    def _():
        proj_b = proj[...].astype(bf16)
        for first, last in chunks(0, width, 512):
            rows = (acc[:, first:last] + dot_nn(proj_b, both[:, first:last])).astype(bf16)
            for i, out in enumerate(back_refs):
                out[:, first:last] = rows[i * cap : (i + 1) * cap]
            ga_ref[:, first:last] = dot_tn(proj_b, xs[:, first:last])


def expert_rows(mine, mats, pieces):
    w_gate, w_up, w_down, a_gate, a_up, b_gate, b_up = mats
    width, hidden = w_gate.shape
    rank = a_gate.shape[0]
    cap = pieces[0][0].shape[0]
    rows = cap * len(pieces)
    tile = 256
    arrays = [a for piece in pieces for a in piece]
    return pl.pallas_call(
        functools.partial(expert_kernel, [(0,) * len(p) for p in pieces], cap, width, rank),
        grid=(hidden // tile,),
        in_specs=[
            whole_block(mine.shape),
            pl.BlockSpec((width, tile), lambda j: (0, j)),
            pl.BlockSpec((width, tile), lambda j: (0, j)),
            pl.BlockSpec((tile, width), lambda j: (j, 0)),
            whole_block(a_gate.shape),
            whole_block(a_up.shape),
            pl.BlockSpec((rank, tile), lambda j: (0, j)),
            pl.BlockSpec((rank, tile), lambda j: (0, j)),
        ]
        + [whole_block(a.shape) for a in arrays],
        out_shape=[jax.ShapeDtypeStruct((cap, width), bf16)] * len(pieces)
        + [
            jax.ShapeDtypeStruct((rows, 1), f32),
            jax.ShapeDtypeStruct((2 * rank, width), f32),
            jax.ShapeDtypeStruct((rank, hidden), f32),
            jax.ShapeDtypeStruct((rank, hidden), f32),
        ],
        out_specs=[whole_block((cap, width))] * len(pieces)
        + [
            whole_block((rows, 1)),
            whole_block((2 * rank, width)),
            pl.BlockSpec((rank, tile), lambda j: (0, j)),
            pl.BlockSpec((rank, tile), lambda j: (0, j)),
        ],
        scratch_shapes=[
            pltpu.VMEM((rows, width), bf16),
            pltpu.VMEM((rows, width), bf16),
            pltpu.VMEM((rows, 1), f32),
            pltpu.VMEM((rows, 2 * rank), bf16),
            pltpu.VMEM((rows, 2 * rank), f32),
            pltpu.VMEM((2 * rank, width), bf16),
            pltpu.VMEM((rows, width), f32),
        ],
        compiler_params=pltpu.CompilerParams(vmem_limit_bytes=vmem_bytes),
        cost_estimate=light,
    )(mine, w_gate, w_up, w_down, a_gate, a_up, b_gate, b_up, *arrays)


def solution(mesh):
    devices = mesh.shape["expert"]
    layers = devices // plane

    def along(pairs):
        return [(a * plane + q, b * plane + q) for a, b in pairs for q in range(plane)]

    def across(step):
        return [(i, i ^ step) for i in range(devices)]

    def send(array, pairs):
        return lax.ppermute(array, "expert", pairs)

    def spread(pieces):
        return [pieces[0]] + [send(pieces[p], across(p)) for p in range(1, plane)]

    def shards(
        layer_input,
        output_gradient,
        router_matrix,
        routed_expert_index,
        gate_weight_frozen,
        up_weight_frozen,
        down_weight_frozen,
        gate_adapter_first,
        gate_adapter_second,
        up_adapter_first,
        up_adapter_second,
    ):
        tok, width = layer_input.shape
        topk = routed_expert_index.shape[1]
        experts = router_matrix.shape[1]
        capacity = 3 * tok * topk // (2 * experts)
        cap = -(-capacity // 16) * 16
        me = lax.axis_index("expert")
        layer = me // plane
        place = me % plane
        mats = (
            gate_weight_frozen[0],
            up_weight_frozen[0],
            down_weight_frozen[0],
            gate_adapter_first[0].T,
            up_adapter_first[0].T,
            gate_adapter_second[0],
            up_adapter_second[0],
        )
        dy = output_gradient

        scores = jax.nn.sigmoid(dot_nn(layer_input, router_matrix))
        expert_ids = jnp.arange(experts, dtype=jnp.int32)
        mask = jnp.sum(
            (routed_expert_index[:, :, None] == expert_ids[None, None, :]).astype(f32), axis=1
        )
        picked = mask * scores
        total = jnp.sum(picked, axis=1, keepdims=True)
        combine = (route_scale * picked / total).astype(bf16)
        earlier = (jnp.arange(tok)[:, None] > jnp.arange(tok)[None, :]).astype(bf16)
        slot_dense = mask * (dot_nn(earlier, mask.astype(bf16)) + 1.0)
        meta_width = -(-2 * experts // 128) * 128
        meta = jnp.concatenate(
            [slot_dense.astype(bf16), combine, jnp.zeros((tok, meta_width - 2 * experts), bf16)],
            axis=1,
        )
        own = jnp.concatenate([layer_input, meta, dy], axis=1)
        full = own.shape[1]
        meta_at = (width, width + meta_width)

        here = layer * plane + (place ^ jnp.arange(plane, dtype=jnp.int32))
        guide = jnp.zeros((16, meta_width), bf16)
        guide = guide.at[:plane].set(
            (here[:, None] == jnp.arange(meta_width, dtype=jnp.int32)[None, :]).astype(bf16)
        )
        mine = (jnp.arange(meta_width) == experts + me).astype(f32)[None, :]

        def take(flag, arrays):
            *pieces, placed = select_rows(
                flag, guide, [[(0, full)] * len(arrays)], arrays, meta_at, False, cap
            )
            return pieces, placed

        def run(pieces):
            return expert_rows(mine, mats, [(a,) for a in pieces])

        if layers == 4:
            mid = (layer == 1) | (layer == 2)
            flag = mid.astype(jnp.int32)[None]
            join = lax.optimization_barrier
            block_1 = send(own, along([(0, 2), (3, 1), (1, 0), (2, 3)]))
            sel_0, placed_0 = take(flag, [own])
            block_1, own, got_0 = join((block_1, own, spread(sel_0)))
            block_2f = send(block_1, along([(1, 0), (2, 3)]))
            block_2m = send(own, along([(1, 2), (2, 1)]))
            sel_1, placed_1 = take(flag, [block_1])
            got_1 = spread(sel_1)
            done_0 = run(got_0)
            got_1, done_0, own = join((got_1, done_0, own))
            block_2f, block_2m, own = join((block_2f, block_2m, own))
            block_3 = send(own, along([(0, 1), (3, 2), (1, 3), (2, 0)]))
            sel_2, placed_2 = take(flag, [block_2m, block_2f])
            sel_2, back_0, got_1 = join((sel_2, spread(done_0[:plane]), got_1))
            got_2 = spread(sel_2)
            done_1 = run(got_1)
            part_0 = sum_rows(placed_0, back_0, [])
            got_2, done_1, part_0 = join((got_2, done_1, part_0))
            sel_3, placed_3 = take(flag, [block_3])
            sel_3, back_1, got_2 = join((sel_3, spread(done_1[:plane]), got_2))
            got_3 = spread(sel_3)
            done_2 = run(got_2)
            part_1 = sum_rows(placed_1, back_1, [])
            term_1 = send(part_1, along([(0, 1), (3, 2)]))
            got_3, done_2, part_1 = join((got_3, done_2, part_1))
            back_2 = spread(done_2[:plane])
            done_3 = run(got_3)
            back_2, done_3 = join((back_2, done_3))
            back_3 = spread(done_3[:plane])
            part_2 = sum_rows(placed_2, back_2, [])
            hop = send(part_2, along([(0, 1), (3, 2)]))
            term_2 = send(part_2, along([(1, 2), (2, 1)]))
            joined = (part_1.astype(f32) + hop.astype(f32)).astype(bf16)
            term_3 = send(joined, along([(1, 3), (2, 0)]))
            part_3 = sum_rows(placed_3, back_3, [])
            term_4 = send(part_3, along([(1, 0), (2, 3), (3, 1), (0, 2)]))
            terms = [part_0, term_1, term_2, term_3, term_4]
            done = [done_0, done_1, done_2, done_3]
            counts = [1, 1, 1, 1]
            sources = [
                layer,
                jnp.where(mid, layer ^ 2, layer ^ 1),
                layer ^ 3,
                jnp.where(mid, layer ^ 1, layer ^ 2),
            ]
        else:
            flag = jnp.zeros((1,), jnp.int32)
            done, counts, sources, terms = [], [], [], []
            for g in range(layers):
                block = own if g == 0 else send(own, across(g * plane))
                sel, placed = take(flag, [block])
                result = run(spread(sel))
                part = sum_rows(placed, spread(result[:plane]), [])
                terms.append(part if g == 0 else send(part, across(g * plane)))
                done.append(result)
                counts.append(1)
                sources.append(layer ^ g)

        route_all = jnp.concatenate(
            [d[c * plane].reshape(c * plane, cap) for d, c in zip(done, counts)], axis=0
        )
        origin = (
            jnp.stack(sources)[:, None] * plane
            + (place ^ jnp.arange(plane, dtype=jnp.int32))[None, :]
        ).reshape(-1)
        order = (origin[None, :] == jnp.arange(devices, dtype=jnp.int32)[:, None]).astype(bf16)
        route_sorted = dot_nn(order, route_all.astype(bf16)).astype(bf16)
        ret_route = lax.all_to_all(
            route_sorted, "expert", split_axis=0, concat_axis=0, tiled=True
        ).astype(f32)
        slots = jnp.arange(1, cap + 1, dtype=jnp.int32).astype(f32)
        hit = slot_dense[:, :, None] == slots[None, None, :]
        route_grad = jnp.sum(jnp.where(hit, ret_route[None, :, :], 0.0), axis=2)
        shared = jnp.sum(route_grad * picked, axis=1, keepdims=True) / (total * total)
        d_pick = route_scale * (route_grad / total - shared)
        d_logit = (mask * d_pick * scores * (1.0 - scores)).astype(bf16)

        router_part = dot_tn(d_logit, layer_input)
        share = width // devices
        router_part = router_part.reshape(experts, devices, share).transpose(1, 0, 2)
        router_got = lax.all_to_all(router_part, "expert", split_axis=0, concat_axis=0, tiled=True)
        router_grad = jnp.sum(router_got, axis=0).T

        in_grad = dot_nt(d_logit, router_matrix)
        for term in terms:
            in_grad = in_grad + term.astype(f32)
        in_grad = in_grad.astype(bf16)

        rank = gate_adapter_second.shape[1]
        grad_a = sum(d[c * plane + 1] for d, c in zip(done, counts))
        grad_gate_b = sum(d[c * plane + 2] for d, c in zip(done, counts))
        grad_up_b = sum(d[c * plane + 3] for d, c in zip(done, counts))
        return (
            in_grad,
            router_grad,
            grad_a[:rank].T[None],
            grad_gate_b[None],
            grad_a[rank:].T[None],
            grad_up_b[None],
        )

    rows = P(("groups", "expert"), None)
    stack = P(("groups", "expert"), None, None)
    frozen = P("expert", None, None)
    in_specs = (rows, rows, P(), rows, frozen, frozen, frozen, stack, stack, stack, stack)
    out_specs = (rows, rows, stack, stack, stack, stack)
    return jax.shard_map(shards, mesh=mesh, in_specs=in_specs, out_specs=out_specs, check_vma=False)
```

```python
import functools

import jax
import jax.numpy as jnp
from jax import lax
from jax.experimental import pallas as pl
from jax.experimental.pallas import tpu as pltpu
from jax.sharding import PartitionSpec as P

route_scale = 2.5
plane = 4
bf16 = jnp.bfloat16
f32 = jnp.float32
vmem_bytes = 56 * 1024 * 1024
light = pl.CostEstimate(flops=1024, bytes_accessed=1024, transcendentals=0)


def dot_nn(left, right):
    return jnp.dot(left, right, preferred_element_type=f32)


def dot_nt(left, right):
    return lax.dot_general(left, right, (((1,), (1,)), ((), ())), preferred_element_type=f32)


def dot_tn(left, right):
    return lax.dot_general(left, right, (((0,), (0,)), ((), ())), preferred_element_type=f32)


def after(array, *others):
    return lax.optimization_barrier((array, *others))[0]


def chunks(start, stop, step):
    return [(at, min(at + step, stop)) for at in range(start, stop, step)]


def whole_block(shape):
    return pl.BlockSpec(shape, lambda *_: (0,) * len(shape), pipeline_mode=pl.Buffered(1))


vmem = pl.BlockSpec(memory_space=pltpu.VMEM)
smem = pl.BlockSpec(memory_space=pltpu.SMEM)


def select_kernel(parts, meta_at, slots_held, cap, flag_ref, guide_ref, *refs):
    count = sum(len(p) for p in parts)
    ins, outs = refs[:count], refs[count:]
    tok = ins[0].shape[0]
    flag = flag_ref[0] == 1
    groups = []
    for part in parts:
        groups.append((part, ins[: len(part)]))
        ins = ins[len(part) :]

    def load(group, first, last):
        part, arrays = group
        values = [a[:, at + first : at + last] for (at, _), a in zip(part, arrays)]
        return values[0] if len(values) == 1 else jnp.where(flag, values[0], values[1])

    if slots_held:
        placed = guide_ref[...]
    else:
        meta = load(groups[0], *meta_at)
        named = dot_nt(guide_ref[...], meta)
        rank = lax.broadcasted_iota(jnp.int32, (cap, tok), 0).astype(f32) + 1.0
        placed = jnp.concatenate(
            [(named[p : p + 1, :] == rank).astype(bf16) for p in range(plane)], axis=0
        )
        outs[plane][...] = placed
    at = 0
    for group in groups:
        length = group[0][0][1]
        for first, last in chunks(0, length, 512):
            rows = dot_nn(placed, load(group, first, last)).astype(bf16)
            for p in range(plane):
                outs[p][:, at + first : at + last] = rows[p * cap : (p + 1) * cap]
        at += length


def select_rows(flag, guide, parts, arrays, meta_at, slots_held, cap):
    tok = arrays[0].shape[0]
    length = sum(p[0][1] for p in parts)
    shapes = [jax.ShapeDtypeStruct((cap, length), bf16)] * plane
    if not slots_held:
        shapes.append(jax.ShapeDtypeStruct((plane * cap, tok), bf16))
    return pl.pallas_call(
        functools.partial(select_kernel, parts, meta_at, slots_held, cap),
        out_shape=shapes,
        in_specs=[smem] + [vmem] * (1 + len(arrays)),
        out_specs=[vmem] * len(shapes),
        compiler_params=pltpu.CompilerParams(vmem_limit_bytes=vmem_bytes),
        cost_estimate=light,
    )(flag, guide, *arrays)


def sum_kernel(placed_ref, *refs):
    pieces, outs = refs[:plane], refs[plane:]
    for first, last in chunks(0, outs[0].shape[1], 512):
        rows = jnp.concatenate([p[:, first:last] for p in pieces], axis=0)
        total = dot_tn(placed_ref[...], rows).astype(bf16)
        at = 0
        for out in outs:
            out[:, first:last] = total[at : at + out.shape[0]]
            at += out.shape[0]


def sum_rows(placed, pieces, parts=1):
    cap, width = pieces[0].shape
    tok = placed.shape[1]
    return pl.pallas_call(
        sum_kernel,
        out_shape=[jax.ShapeDtypeStruct((tok // parts, width), bf16)] * parts,
        in_specs=[vmem] * (1 + plane),
        out_specs=[vmem] * parts,
        compiler_params=pltpu.CompilerParams(vmem_limit_bytes=vmem_bytes),
        cost_estimate=light,
    )(placed, *pieces)


def final_kernel(groups, logit_ref, router_ref, *refs):
    out = refs[-1]
    for first, last in chunks(0, out.shape[1], 512):
        total = dot_nn(logit_ref[...], router_ref[:, first:last])
        left = refs
        for count in groups:
            total = total + jnp.concatenate(
                [r[:, first:last] for r in left[:count]], axis=0
            ).astype(f32)
            left = left[count:]
        out[:, first:last] = total.astype(bf16)


def final_sum(logit, router, terms):
    tok, width = logit.shape[0], router.shape[1]
    return pl.pallas_call(
        functools.partial(final_kernel, [len(t) for t in terms]),
        out_shape=jax.ShapeDtypeStruct((tok, width), bf16),
        in_specs=[vmem] * (2 + sum(len(t) for t in terms)),
        out_specs=vmem,
        compiler_params=pltpu.CompilerParams(vmem_limit_bytes=vmem_bytes),
        cost_estimate=light,
    )(logit, router, *[a for t in terms for a in t])


def expert_kernel(
    pieces, cap, width, rank, mine_ref, wg_ref, wu_ref, wd_ref, ag_ref, au_ref, bg_ref, bu_ref, *refs
):
    count = sum(len(p) for p in pieces)
    ins, refs = refs[:count], refs[count:]
    back_refs, refs = refs[: len(pieces)], refs[len(pieces) :]
    route_ref, ga_ref, gbg_ref, gbu_ref = refs[:4]
    xs, dys, weight, low, proj, both, acc = refs[4:]
    step = pl.program_id(0)
    tail = width + mine_ref.shape[1]

    @pl.when(step == 0)
    def _():
        left = ins
        for i, piece in enumerate(pieces):
            rows = slice(i * cap, (i + 1) * cap)
            x_ref, dy_ref = left[0], left[len(piece) - 1]
            left = left[len(piece) :]
            offset = tail if len(piece) == 1 else 0
            xs[rows, :] = x_ref[:, :width]
            dys[rows, :] = dy_ref[:, offset : offset + width]
            weight[rows, :] = jnp.sum(
                x_ref[:, width:tail].astype(f32) * mine_ref[...], axis=1, keepdims=True
            )
        both[:rank, :] = ag_ref[...]
        both[rank:, :] = au_ref[...]
        low[...] = dot_nt(xs[...], both[...]).astype(bf16)
        proj[...] = jnp.zeros_like(proj)
        acc[...] = jnp.zeros_like(acc)
        route_ref[...] = jnp.zeros_like(route_ref)

    bg, bu = bg_ref[...], bu_ref[...]
    low_gate, low_up = low[:, :rank], low[:, rank:]
    gate = dot_nn(xs[...], wg_ref[...]) + dot_nn(low_gate, bg)
    upval = dot_nn(xs[...], wu_ref[...]) + dot_nn(low_up, bu)
    back = dot_nt(dys[...], wd_ref[...])
    sigma = jax.nn.sigmoid(gate)
    act = gate * sigma
    route_ref[...] += jnp.sum(back * (act * upval), axis=1, keepdims=True)
    scaled = weight[...] * back
    d_gate = (scaled * upval * sigma * (1.0 + gate * (1.0 - sigma))).astype(bf16)
    d_up = (scaled * act).astype(bf16)
    gbg_ref[...] = dot_tn(low_gate, d_gate)
    gbu_ref[...] = dot_tn(low_up, d_up)
    proj[:, :rank] += dot_nt(d_gate, bg)
    proj[:, rank:] += dot_nt(d_up, bu)
    for first, last in chunks(0, width, 512):
        acc[:, first:last] += dot_nt(d_gate, wg_ref[first:last, :]) + dot_nt(
            d_up, wu_ref[first:last, :]
        )

    @pl.when(step == pl.num_programs(0) - 1)
    def _():
        proj_b = proj[...].astype(bf16)
        for first, last in chunks(0, width, 512):
            rows = (acc[:, first:last] + dot_nn(proj_b, both[:, first:last])).astype(bf16)
            for i, out in enumerate(back_refs):
                out[:, first:last] = rows[i * cap : (i + 1) * cap]
            ga_ref[:, first:last] = dot_tn(proj_b, xs[:, first:last])


def expert_rows(mine, mats, pieces):
    w_gate, w_up, w_down, a_gate, a_up, b_gate, b_up = mats
    width, hidden = w_gate.shape
    rank = a_gate.shape[0]
    cap = pieces[0][0].shape[0]
    rows = cap * len(pieces)
    tile = 256
    arrays = [a for piece in pieces for a in piece]
    return pl.pallas_call(
        functools.partial(expert_kernel, [(0,) * len(p) for p in pieces], cap, width, rank),
        grid=(hidden // tile,),
        in_specs=[
            whole_block(mine.shape),
            pl.BlockSpec((width, tile), lambda j: (0, j)),
            pl.BlockSpec((width, tile), lambda j: (0, j)),
            pl.BlockSpec((tile, width), lambda j: (j, 0)),
            whole_block(a_gate.shape),
            whole_block(a_up.shape),
            pl.BlockSpec((rank, tile), lambda j: (0, j)),
            pl.BlockSpec((rank, tile), lambda j: (0, j)),
        ]
        + [whole_block(a.shape) for a in arrays],
        out_shape=[jax.ShapeDtypeStruct((cap, width), bf16)] * len(pieces)
        + [
            jax.ShapeDtypeStruct((rows, 1), f32),
            jax.ShapeDtypeStruct((2 * rank, width), f32),
            jax.ShapeDtypeStruct((rank, hidden), f32),
            jax.ShapeDtypeStruct((rank, hidden), f32),
        ],
        out_specs=[whole_block((cap, width))] * len(pieces)
        + [
            whole_block((rows, 1)),
            whole_block((2 * rank, width)),
            pl.BlockSpec((rank, tile), lambda j: (0, j)),
            pl.BlockSpec((rank, tile), lambda j: (0, j)),
        ],
        scratch_shapes=[
            pltpu.VMEM((rows, width), bf16),
            pltpu.VMEM((rows, width), bf16),
            pltpu.VMEM((rows, 1), f32),
            pltpu.VMEM((rows, 2 * rank), bf16),
            pltpu.VMEM((rows, 2 * rank), f32),
            pltpu.VMEM((2 * rank, width), bf16),
            pltpu.VMEM((rows, width), f32),
        ],
        compiler_params=pltpu.CompilerParams(vmem_limit_bytes=vmem_bytes),
        cost_estimate=light,
    )(mine, w_gate, w_up, w_down, a_gate, a_up, b_gate, b_up, *arrays)


def solution(mesh):
    devices = mesh.shape["expert"]
    layers = devices // plane

    def along(pairs):
        return [(a * plane + q, b * plane + q) for a, b in pairs for q in range(plane)]

    def across(step):
        return [(i, i ^ step) for i in range(devices)]

    def send(array, pairs):
        return lax.ppermute(array, "expert", pairs)

    def spread(pieces):
        return [pieces[0]] + [send(pieces[p], across(p)) for p in range(1, plane)]

    def shards(
        layer_input,
        output_gradient,
        router_matrix,
        routed_expert_index,
        gate_weight_frozen,
        up_weight_frozen,
        down_weight_frozen,
        gate_adapter_first,
        gate_adapter_second,
        up_adapter_first,
        up_adapter_second,
    ):
        tok, width = layer_input.shape
        topk = routed_expert_index.shape[1]
        experts = router_matrix.shape[1]
        capacity = 3 * tok * topk // (2 * experts)
        cap = -(-capacity // 16) * 16
        me = lax.axis_index("expert")
        layer = me // plane
        place = me % plane
        mats = (
            gate_weight_frozen[0],
            up_weight_frozen[0],
            down_weight_frozen[0],
            gate_adapter_first[0].T,
            up_adapter_first[0].T,
            gate_adapter_second[0],
            up_adapter_second[0],
        )
        dy = output_gradient

        scores = jax.nn.sigmoid(dot_nn(layer_input, router_matrix))
        expert_ids = jnp.arange(experts, dtype=jnp.int32)
        mask = jnp.sum(
            (routed_expert_index[:, :, None] == expert_ids[None, None, :]).astype(f32), axis=1
        )
        picked = mask * scores
        total = jnp.sum(picked, axis=1, keepdims=True)
        combine = (route_scale * picked / total).astype(bf16)
        earlier = (jnp.arange(tok)[:, None] > jnp.arange(tok)[None, :]).astype(bf16)
        slot_dense = mask * (dot_nn(earlier, mask.astype(bf16)) + 1.0)
        meta_width = -(-2 * experts // 128) * 128
        meta = jnp.concatenate(
            [slot_dense.astype(bf16), combine, jnp.zeros((tok, meta_width - 2 * experts), bf16)],
            axis=1,
        )
        own = jnp.concatenate([layer_input, meta, dy], axis=1)
        full = own.shape[1]
        meta_at = (width, width + meta_width)

        here = layer * plane + (place ^ jnp.arange(plane, dtype=jnp.int32))
        guide = jnp.zeros((16, meta_width), bf16)
        guide = guide.at[:plane].set(
            (here[:, None] == jnp.arange(meta_width, dtype=jnp.int32)[None, :]).astype(bf16)
        )
        mine = (jnp.arange(meta_width) == experts + me).astype(f32)[None, :]

        def take(flag, arrays):
            *pieces, placed = select_rows(
                flag, guide, [[(0, full)] * len(arrays)], arrays, meta_at, False, cap
            )
            return pieces, placed

        def run(pieces):
            return expert_rows(mine, mats, [(a,) for a in pieces])

        if layers == 4:
            mid = (layer == 1) | (layer == 2)
            flag = mid.astype(jnp.int32)[None]
            join = lax.optimization_barrier
            block_1 = send(own, along([(0, 2), (3, 1), (1, 0), (2, 3)]))
            sel_0, placed_0 = take(flag, [own])
            block_1, own, got_0 = join((block_1, own, spread(sel_0)))
            block_2f = send(block_1, along([(1, 0), (2, 3)]))
            block_2m = send(own, along([(1, 2), (2, 1)]))
            sel_1, placed_1 = take(flag, [block_1])
            got_1 = spread(sel_1)
            done_0 = run(got_0)
            got_1, done_0, own = join((got_1, done_0, own))
            back_0 = spread(done_0[:plane])
            block_2f, block_2m, own, back_0[1], back_0[2] = join(
                (block_2f, block_2m, own, back_0[1], back_0[2])
            )
            block_3 = send(own, along([(0, 1), (3, 2), (1, 3), (2, 0)]))
            sel_2, placed_2 = take(flag, [block_2m, block_2f])
            sel_2, got_1 = join((sel_2, got_1))
            got_2 = spread(sel_2)
            done_1 = run(got_1)
            done_1, got_2[1], got_2[2] = join((done_1, got_2[1], got_2[2]))
            back_1 = spread(done_1[:plane])
            sel_3, placed_3 = take(flag, [block_3])
            part_0 = sum_rows(placed_0, back_0)
            sel_3, back_1, got_2 = join((sel_3, back_1, got_2))
            got_3 = spread(sel_3)
            done_2 = run(got_2)
            done_2, got_3[1], got_3[2] = join((done_2, got_3[1], got_3[2]))
            back_2 = spread(done_2[:plane])
            (part_1,) = sum_rows(placed_1, back_1)
            term_1 = send(part_1, along([(0, 1), (3, 2), (1, 3), (2, 0)]))
            got_3, back_2, part_1, part_0 = join((got_3, back_2, part_1, part_0))
            part_2a, part_2b = sum_rows(placed_2, back_2, 2)
            term_2a = send(part_2a, across(3 * plane))
            done_3 = run(got_3)
            done_3, term_1, term_2a, part_2b = join((done_3, term_1, term_2a, part_2b))
            back_3 = spread(done_3[:plane])
            term_2b = send(part_2b, across(3 * plane))
            aux = done_3[plane:]
            back_3[1], back_3[2], aux = join((back_3[1], back_3[2], aux))
            done_3 = [*done_3[:plane], *aux]
            (part_3,) = sum_rows(placed_3, back_3)
            done = [done_0, done_1, done_2, done_3]
            part_3, grads = join((part_3, [d[plane + 1 :] for d in done]))
            done = [[*d[: plane + 1], *g] for d, g in zip(done, grads)]
            term_3 = send(part_3, along([(1, 0), (2, 3), (3, 1), (0, 2)]))
            terms = [part_0, [term_1], [term_2a, term_2b], [term_3]]
            counts = [1, 1, 1, 1]
            sources = [
                layer,
                jnp.where(mid, layer ^ 2, layer ^ 1),
                layer ^ 3,
                jnp.where(mid, layer ^ 1, layer ^ 2),
            ]
        else:
            flag = jnp.zeros((1,), jnp.int32)
            done, counts, sources, terms = [], [], [], []
            for g in range(layers):
                block = own if g == 0 else send(own, across(g * plane))
                sel, placed = take(flag, [block])
                result = run(spread(sel))
                (part,) = sum_rows(placed, spread(result[:plane]))
                terms.append([part if g == 0 else send(part, across(g * plane))])
                done.append(result)
                counts.append(1)
                sources.append(layer ^ g)

        route_all = jnp.concatenate(
            [d[c * plane].reshape(c * plane, cap) for d, c in zip(done, counts)], axis=0
        )
        origin = (
            jnp.stack(sources)[:, None] * plane
            + (place ^ jnp.arange(plane, dtype=jnp.int32))[None, :]
        ).reshape(-1)
        order = (origin[None, :] == jnp.arange(devices, dtype=jnp.int32)[:, None]).astype(bf16)
        route_sorted = dot_nn(order, route_all.astype(bf16)).astype(bf16)
        ret_route = lax.all_to_all(
            route_sorted, "expert", split_axis=0, concat_axis=0, tiled=True
        ).astype(f32)
        slots = jnp.arange(1, cap + 1, dtype=jnp.int32).astype(f32)
        hit = slot_dense[:, :, None] == slots[None, None, :]
        route_grad = jnp.sum(jnp.where(hit, ret_route[None, :, :], 0.0), axis=2)
        shared = jnp.sum(route_grad * picked, axis=1, keepdims=True) / (total * total)
        d_pick = route_scale * (route_grad / total - shared)
        d_logit = (mask * d_pick * scores * (1.0 - scores)).astype(bf16)

        router_part = dot_tn(d_logit, layer_input)
        share = width // devices
        router_part = router_part.reshape(experts, devices, share).transpose(1, 0, 2)
        router_got = lax.all_to_all(router_part, "expert", split_axis=0, concat_axis=0, tiled=True)
        router_grad = jnp.sum(router_got, axis=0).T

        in_grad = final_sum(d_logit, router_matrix.T, terms)

        rank = gate_adapter_second.shape[1]
        grad_a = sum(d[c * plane + 1] for d, c in zip(done, counts))
        grad_gate_b = sum(d[c * plane + 2] for d, c in zip(done, counts))
        grad_up_b = sum(d[c * plane + 3] for d, c in zip(done, counts))
        return (
            in_grad,
            router_grad,
            grad_a[:rank].T[None],
            grad_gate_b[None],
            grad_a[rank:].T[None],
            grad_up_b[None],
        )

    rows = P(("groups", "expert"), None)
    stack = P(("groups", "expert"), None, None)
    frozen = P("expert", None, None)
    in_specs = (rows, rows, P(), rows, frozen, frozen, frozen, stack, stack, stack, stack)
    out_specs = (rows, rows, stack, stack, stack, stack)
    return jax.shard_map(shards, mesh=mesh, in_specs=in_specs, out_specs=out_specs, check_vma=False)
```

```python
import functools

import jax
import jax.numpy as jnp
from jax import lax
from jax.experimental import pallas as pl
from jax.experimental.pallas import tpu as pltpu
from jax.sharding import PartitionSpec as P

route_scale = 2.5
plane = 4
bf16 = jnp.bfloat16
f32 = jnp.float32
vmem_bytes = 56 * 1024 * 1024
light = pl.CostEstimate(flops=1024, bytes_accessed=1024, transcendentals=0)


def dot_nn(left, right):
    return jnp.dot(left, right, preferred_element_type=f32)


def dot_nt(left, right):
    return lax.dot_general(left, right, (((1,), (1,)), ((), ())), preferred_element_type=f32)


def dot_tn(left, right):
    return lax.dot_general(left, right, (((0,), (0,)), ((), ())), preferred_element_type=f32)


def after(array, *others):
    return lax.optimization_barrier((array, *others))[0]


def chunks(start, stop, step):
    return [(at, min(at + step, stop)) for at in range(start, stop, step)]


def whole_block(shape):
    return pl.BlockSpec(shape, lambda *_: (0,) * len(shape), pipeline_mode=pl.Buffered(1))


vmem = pl.BlockSpec(memory_space=pltpu.VMEM)
smem = pl.BlockSpec(memory_space=pltpu.SMEM)


def select_kernel(parts, meta_at, slots_held, cap, flag_ref, guide_ref, *refs):
    count = sum(len(p) for p in parts)
    ins, outs = refs[:count], refs[count:]
    tok = ins[0].shape[0]
    flag = flag_ref[0] == 1
    groups = []
    for part in parts:
        groups.append((part, ins[: len(part)]))
        ins = ins[len(part) :]

    def load(group, first, last):
        part, arrays = group
        values = [a[:, at + first : at + last] for (at, _), a in zip(part, arrays)]
        return values[0] if len(values) == 1 else jnp.where(flag, values[0], values[1])

    if slots_held:
        placed = guide_ref[...]
    else:
        meta = load(groups[0], *meta_at)
        named = dot_nt(guide_ref[...], meta)
        rank = lax.broadcasted_iota(jnp.int32, (cap, tok), 0).astype(f32) + 1.0
        placed = jnp.concatenate(
            [(named[p : p + 1, :] == rank).astype(bf16) for p in range(plane)], axis=0
        )
        outs[plane][...] = placed
    at = 0
    for group in groups:
        length = group[0][0][1]
        for first, last in chunks(0, length, 512):
            rows = dot_nn(placed, load(group, first, last)).astype(bf16)
            for p in range(plane):
                outs[p][:, at + first : at + last] = rows[p * cap : (p + 1) * cap]
        at += length


def select_rows(flag, guide, parts, arrays, meta_at, slots_held, cap):
    tok = arrays[0].shape[0]
    length = sum(p[0][1] for p in parts)
    shapes = [jax.ShapeDtypeStruct((cap, length), bf16)] * plane
    if not slots_held:
        shapes.append(jax.ShapeDtypeStruct((plane * cap, tok), bf16))
    return pl.pallas_call(
        functools.partial(select_kernel, parts, meta_at, slots_held, cap),
        out_shape=shapes,
        in_specs=[smem] + [vmem] * (1 + len(arrays)),
        out_specs=[vmem] * len(shapes),
        compiler_params=pltpu.CompilerParams(vmem_limit_bytes=vmem_bytes),
        cost_estimate=light,
    )(flag, guide, *arrays)


def sum_kernel(placed_ref, *refs):
    pieces, outs = refs[:plane], refs[plane:]
    for first, last in chunks(0, outs[0].shape[1], 512):
        rows = jnp.concatenate([p[:, first:last] for p in pieces], axis=0)
        total = dot_tn(placed_ref[...], rows).astype(bf16)
        at = 0
        for out in outs:
            out[:, first:last] = total[at : at + out.shape[0]]
            at += out.shape[0]


def sum_rows(placed, pieces, parts=1):
    cap, width = pieces[0].shape
    tok = placed.shape[1]
    return pl.pallas_call(
        sum_kernel,
        out_shape=[jax.ShapeDtypeStruct((tok // parts, width), bf16)] * parts,
        in_specs=[vmem] * (1 + plane),
        out_specs=[vmem] * parts,
        compiler_params=pltpu.CompilerParams(vmem_limit_bytes=vmem_bytes),
        cost_estimate=light,
    )(placed, *pieces)


def final_kernel(groups, logit_ref, router_ref, *refs):
    out = refs[-1]
    for first, last in chunks(0, out.shape[1], 512):
        total = dot_nn(logit_ref[...], router_ref[:, first:last])
        left = refs
        for count in groups:
            total = total + jnp.concatenate(
                [r[:, first:last] for r in left[:count]], axis=0
            ).astype(f32)
            left = left[count:]
        out[:, first:last] = total.astype(bf16)


def final_sum(logit, router, terms):
    tok, width = logit.shape[0], router.shape[1]
    return pl.pallas_call(
        functools.partial(final_kernel, [len(t) for t in terms]),
        out_shape=jax.ShapeDtypeStruct((tok, width), bf16),
        in_specs=[vmem] * (2 + sum(len(t) for t in terms)),
        out_specs=vmem,
        compiler_params=pltpu.CompilerParams(vmem_limit_bytes=vmem_bytes),
        cost_estimate=light,
    )(logit, router, *[a for t in terms for a in t])


def expert_kernel(
    held, cap, width, rank, mine_ref, wg_ref, wu_ref, wd_ref, ag_ref, au_ref, bg_ref, bu_ref, *refs
):
    ins, refs = refs[:plane], refs[plane:]
    carry, refs = refs[:held], refs[held:]
    back_refs, refs = refs[:plane], refs[plane:]
    route_ref, gag_ref, gau_ref, gbg_ref, gbu_ref = refs[:5]
    xs, dys, weight, low, proj, both, acc = refs[5:]

    def total(at, value, part=slice(None)):
        return value + carry[at][:, part] if held else value

    step = pl.program_id(0)
    tail = width + mine_ref.shape[1]

    @pl.when(step == 0)
    def _():
        for i, ref in enumerate(ins):
            rows = slice(i * cap, (i + 1) * cap)
            xs[rows, :] = ref[:, :width]
            dys[rows, :] = ref[:, tail:]
            weight[rows, :] = jnp.sum(
                ref[:, width:tail].astype(f32) * mine_ref[...], axis=1, keepdims=True
            )
        both[:rank, :] = ag_ref[...]
        both[rank:, :] = au_ref[...]
        low[...] = dot_nt(xs[...], both[...]).astype(bf16)
        proj[...] = jnp.zeros_like(proj)
        acc[...] = jnp.zeros_like(acc)
        route_ref[...] = jnp.zeros_like(route_ref)

    bg, bu = bg_ref[...], bu_ref[...]
    low_gate, low_up = low[:, :rank], low[:, rank:]
    gate = dot_nn(xs[...], wg_ref[...]) + dot_nn(low_gate, bg)
    upval = dot_nn(xs[...], wu_ref[...]) + dot_nn(low_up, bu)
    back = dot_nt(dys[...], wd_ref[...])
    sigma = jax.nn.sigmoid(gate)
    act = gate * sigma
    route_ref[...] += jnp.sum(back * (act * upval), axis=1, keepdims=True)
    scaled = weight[...] * back
    d_gate = (scaled * upval * sigma * (1.0 + gate * (1.0 - sigma))).astype(bf16)
    d_up = (scaled * act).astype(bf16)
    gbg_ref[...] = total(2, dot_tn(low_gate, d_gate))
    gbu_ref[...] = total(3, dot_tn(low_up, d_up))
    proj[:, :rank] += dot_nt(d_gate, bg)
    proj[:, rank:] += dot_nt(d_up, bu)
    for first, last in chunks(0, width, 512):
        acc[:, first:last] += dot_nt(d_gate, wg_ref[first:last, :]) + dot_nt(
            d_up, wu_ref[first:last, :]
        )

    @pl.when(step == pl.num_programs(0) - 1)
    def _():
        proj_b = proj[...].astype(bf16)
        for first, last in chunks(0, width, 512):
            rows = (acc[:, first:last] + dot_nn(proj_b, both[:, first:last])).astype(bf16)
            for i, out in enumerate(back_refs):
                out[:, first:last] = rows[i * cap : (i + 1) * cap]
            part = slice(first, last)
            grad = dot_tn(proj_b, xs[:, part])
            gag_ref[:, part] = total(0, grad[:rank], part)
            gau_ref[:, part] = total(1, grad[rank:], part)


def expert_rows(mine, mats, pieces, carry=()):
    w_gate, w_up, w_down, a_gate, a_up, b_gate, b_up = mats
    width, hidden = w_gate.shape
    rank = a_gate.shape[0]
    cap = pieces[0].shape[0]
    rows = cap * plane
    tile = 256
    second = pl.BlockSpec((rank, tile), lambda j: (0, j))
    grads = [whole_block((rank, width))] * 2 + [second] * 2
    return pl.pallas_call(
        functools.partial(expert_kernel, len(carry), cap, width, rank),
        grid=(hidden // tile,),
        in_specs=[
            whole_block(mine.shape),
            pl.BlockSpec((width, tile), lambda j: (0, j)),
            pl.BlockSpec((width, tile), lambda j: (0, j)),
            pl.BlockSpec((tile, width), lambda j: (j, 0)),
            whole_block(a_gate.shape),
            whole_block(a_up.shape),
            second,
            second,
        ]
        + [whole_block(a.shape) for a in pieces]
        + (grads if carry else []),
        out_shape=[jax.ShapeDtypeStruct((cap, width), bf16)] * plane
        + [
            jax.ShapeDtypeStruct((rows, 1), f32),
            jax.ShapeDtypeStruct((rank, width), f32),
            jax.ShapeDtypeStruct((rank, width), f32),
            jax.ShapeDtypeStruct((rank, hidden), f32),
            jax.ShapeDtypeStruct((rank, hidden), f32),
        ],
        out_specs=[whole_block((cap, width))] * plane + [whole_block((rows, 1))] + grads,
        scratch_shapes=[
            pltpu.VMEM((rows, width), bf16),
            pltpu.VMEM((rows, width), bf16),
            pltpu.VMEM((rows, 1), f32),
            pltpu.VMEM((rows, 2 * rank), bf16),
            pltpu.VMEM((rows, 2 * rank), f32),
            pltpu.VMEM((2 * rank, width), bf16),
            pltpu.VMEM((rows, width), f32),
        ],
        compiler_params=pltpu.CompilerParams(vmem_limit_bytes=vmem_bytes),
        cost_estimate=light,
    )(mine, w_gate, w_up, w_down, a_gate, a_up, b_gate, b_up, *pieces, *carry)


def solution(mesh):
    devices = mesh.shape["expert"]
    layers = devices // plane

    def along(pairs):
        return [(a * plane + q, b * plane + q) for a, b in pairs for q in range(plane)]

    def across(step):
        return [(i, i ^ step) for i in range(devices)]

    def send(array, pairs):
        return lax.ppermute(array, "expert", pairs)

    def spread(pieces):
        return [pieces[0]] + [send(pieces[p], across(p)) for p in range(1, plane)]

    def shards(
        layer_input,
        output_gradient,
        router_matrix,
        routed_expert_index,
        gate_weight_frozen,
        up_weight_frozen,
        down_weight_frozen,
        gate_adapter_first,
        gate_adapter_second,
        up_adapter_first,
        up_adapter_second,
    ):
        tok, width = layer_input.shape
        topk = routed_expert_index.shape[1]
        experts = router_matrix.shape[1]
        capacity = 3 * tok * topk // (2 * experts)
        cap = -(-capacity // 16) * 16
        me = lax.axis_index("expert")
        layer = me // plane
        place = me % plane
        mats = (
            gate_weight_frozen[0],
            up_weight_frozen[0],
            down_weight_frozen[0],
            gate_adapter_first[0].T,
            up_adapter_first[0].T,
            gate_adapter_second[0],
            up_adapter_second[0],
        )
        dy = output_gradient
        join = lax.optimization_barrier

        scores = jax.nn.sigmoid(dot_nn(layer_input, router_matrix))
        expert_ids = jnp.arange(experts, dtype=jnp.int32)
        mask = jnp.sum(
            (routed_expert_index[:, :, None] == expert_ids[None, None, :]).astype(f32), axis=1
        )
        picked = mask * scores
        total = jnp.sum(picked, axis=1, keepdims=True)
        combine = (route_scale * picked / total).astype(bf16)
        earlier = (jnp.arange(tok)[:, None] > jnp.arange(tok)[None, :]).astype(bf16)
        slot_dense = mask * (dot_nn(earlier, mask.astype(bf16)) + 1.0)
        meta_width = -(-2 * experts // 128) * 128
        meta = jnp.concatenate(
            [slot_dense.astype(bf16), combine, jnp.zeros((tok, meta_width - 2 * experts), bf16)],
            axis=1,
        )
        own = jnp.concatenate([layer_input, meta, dy], axis=1)
        full = own.shape[1]
        meta_at = (width, width + meta_width)

        here = layer * plane + (place ^ jnp.arange(plane, dtype=jnp.int32))
        guide = jnp.zeros((16, meta_width), bf16)
        guide = guide.at[:plane].set(
            (here[:, None] == jnp.arange(meta_width, dtype=jnp.int32)[None, :]).astype(bf16)
        )
        mine = (jnp.arange(meta_width) == experts + me).astype(f32)[None, :]

        def take(flag, arrays):
            *pieces, placed = select_rows(
                flag, guide, [[(0, full)] * len(arrays)], arrays, meta_at, False, cap
            )
            return pieces, placed

        def run(pieces, carry=()):
            return expert_rows(mine, mats, pieces, carry)

        if layers == 4:
            mid = (layer == 1) | (layer == 2)
            flag = mid.astype(jnp.int32)[None]
            block_1 = send(own, along([(0, 2), (3, 1), (1, 0), (2, 3)]))
            sel_0, placed_0 = take(flag, [own])
            block_1, own, got_0 = join((block_1, own, spread(sel_0)))
            block_2f = send(block_1, along([(1, 0), (2, 3)]))
            block_2m = send(own, along([(1, 2), (2, 1)]))
            sel_1, placed_1 = take(flag, [block_1])
            got_1 = spread(sel_1)
            done_0 = run(got_0)
            got_1, done_0, own = join((got_1, done_0, own))
            block_2f, block_2m, own = join((block_2f, block_2m, own))
            block_3 = send(own, along([(0, 1), (3, 2), (1, 3), (2, 0)]))
            sel_2, placed_2 = take(flag, [block_2m, block_2f])
            sel_2, got_1 = join((sel_2, got_1))
            got_2 = spread(sel_2)
            done_1 = run(got_1, done_0[plane + 1 :])
            done_1, got_2[1], got_2[2] = join((done_1, got_2[1], got_2[2]))
            back_1 = spread(done_1[:plane])
            sel_3, placed_3 = take(flag, [block_3])
            sel_3, back_1, got_2 = join((sel_3, back_1, got_2))
            got_3 = spread(sel_3)
            done_2 = run(got_2, done_1[plane + 1 :])
            done_2, got_3[1], got_3[2] = join((done_2, got_3[1], got_3[2]))
            back_2 = spread(done_2[:plane])
            (part_1,) = sum_rows(placed_1, back_1)
            term_1 = send(part_1, along([(0, 1), (3, 2), (1, 3), (2, 0)]))
            got_3, back_2, part_1, done_0 = join((got_3, back_2, part_1, done_0))
            back_0 = spread(done_0[:plane])
            part_2a, part_2b = sum_rows(placed_2, back_2, 2)
            term_2a = send(part_2a, across(3 * plane))
            done_3 = run(got_3, done_2[plane + 1 :])
            done_3, term_1, term_2a, part_2b, back_0 = join(
                (done_3, term_1, term_2a, part_2b, back_0)
            )
            back_3 = spread(done_3[:plane])
            term_2b = send(part_2b, across(3 * plane))
            aux = done_3[plane:]
            back_3[1], back_3[2], aux, back_0 = join((back_3[1], back_3[2], aux, back_0))
            done_3 = [*done_3[:plane], *aux]
            (part_0,) = sum_rows(placed_0, back_0)
            done = [done_0, done_1, done_2, done_3]
            sources = [
                layer,
                jnp.where(mid, layer ^ 2, layer ^ 1),
                layer ^ 3,
                jnp.where(mid, layer ^ 1, layer ^ 2),
            ]
        else:
            flag = jnp.zeros((1,), jnp.int32)
            done, sources, terms = [], [], []
            for g in range(layers):
                block = own if g == 0 else send(own, across(g * plane))
                sel, placed = take(flag, [block])
                result = run(spread(sel), done[-1][plane + 1 :] if done else ())
                (part,) = sum_rows(placed, spread(result[:plane]))
                terms.append([part if g == 0 else send(part, across(g * plane))])
                done.append(result)
                sources.append(layer ^ g)

        route_all = jnp.concatenate(
            [d[plane].reshape(plane, cap) for d in done], axis=0
        )
        origin = (
            jnp.stack(sources)[:, None] * plane
            + (place ^ jnp.arange(plane, dtype=jnp.int32))[None, :]
        ).reshape(-1)
        order = (origin[None, :] == jnp.arange(devices, dtype=jnp.int32)[:, None]).astype(bf16)
        route_sorted = dot_nn(order, route_all.astype(bf16)).astype(bf16)
        ret_route = lax.all_to_all(
            route_sorted, "expert", split_axis=0, concat_axis=0, tiled=True
        ).astype(f32)
        slots = jnp.arange(1, cap + 1, dtype=jnp.int32).astype(f32)
        hit = slot_dense[:, :, None] == slots[None, None, :]
        route_grad = jnp.sum(jnp.where(hit, ret_route[None, :, :], 0.0), axis=2)
        shared = jnp.sum(route_grad * picked, axis=1, keepdims=True) / (total * total)
        d_pick = route_scale * (route_grad / total - shared)
        d_logit = (mask * d_pick * scores * (1.0 - scores)).astype(bf16)

        if layers == 4:
            (part_3,) = sum_rows(placed_3, back_3)
            term_3 = send(part_3, along([(1, 0), (2, 3), (3, 1), (0, 2)]))
            d_logit, part_3, part_0, term_2b = join((d_logit, part_3, part_0, term_2b))
            terms = [[part_0], [term_1], [term_2a, term_2b], [term_3]]

        router_part = dot_tn(d_logit, layer_input)
        share = width // devices
        router_part = router_part.reshape(experts, devices, share).transpose(1, 0, 2)
        router_got = lax.all_to_all(router_part, "expert", split_axis=0, concat_axis=0, tiled=True)
        router_grad = jnp.sum(router_got, axis=0).T

        in_grad = final_sum(d_logit, router_matrix.T, terms)

        grad_gate_a, grad_up_a, grad_gate_b, grad_up_b = done[-1][plane + 1 :]
        return (
            in_grad,
            router_grad,
            grad_gate_a.T[None],
            grad_gate_b[None],
            grad_up_a.T[None],
            grad_up_b[None],
        )

    rows = P(("groups", "expert"), None)
    stack = P(("groups", "expert"), None, None)
    frozen = P("expert", None, None)
    in_specs = (rows, rows, P(), rows, frozen, frozen, frozen, stack, stack, stack, stack)
    out_specs = (rows, rows, stack, stack, stack, stack)
    return jax.shard_map(shards, mesh=mesh, in_specs=in_specs, out_specs=out_specs, check_vma=False)
```

```python
import functools

import jax
import jax.numpy as jnp
from jax import lax
from jax.experimental import pallas as pl
from jax.experimental.pallas import tpu as pltpu
from jax.sharding import PartitionSpec as P

route_scale = 2.5
plane = 4
bf16 = jnp.bfloat16
f32 = jnp.float32
vmem_bytes = 56 * 1024 * 1024
light = pl.CostEstimate(flops=1024, bytes_accessed=1024, transcendentals=0)


def dot_nn(left, right):
    return jnp.dot(left, right, preferred_element_type=f32)


def dot_nt(left, right):
    return lax.dot_general(left, right, (((1,), (1,)), ((), ())), preferred_element_type=f32)


def dot_tn(left, right):
    return lax.dot_general(left, right, (((0,), (0,)), ((), ())), preferred_element_type=f32)


def after(array, *others):
    return lax.optimization_barrier((array, *others))[0]


def chunks(start, stop, step):
    return [(at, min(at + step, stop)) for at in range(start, stop, step)]


def whole_block(shape):
    return pl.BlockSpec(shape, lambda *_: (0,) * len(shape), pipeline_mode=pl.Buffered(1))


vmem = pl.BlockSpec(memory_space=pltpu.VMEM)
smem = pl.BlockSpec(memory_space=pltpu.SMEM)


def select_kernel(parts, meta_at, slots_held, cap, flag_ref, guide_ref, *refs):
    count = sum(len(p) for p in parts)
    ins, outs = refs[:count], refs[count:]
    tok = ins[0].shape[0]
    flag = flag_ref[0] == 1
    groups = []
    for part in parts:
        groups.append((part, ins[: len(part)]))
        ins = ins[len(part) :]

    def load(group, first, last):
        part, arrays = group
        values = [a[:, at + first : at + last] for (at, _), a in zip(part, arrays)]
        return values[0] if len(values) == 1 else jnp.where(flag, values[0], values[1])

    if slots_held:
        placed = guide_ref[...]
    else:
        meta = load(groups[0], *meta_at)
        named = dot_nt(guide_ref[...], meta)
        rank = lax.broadcasted_iota(jnp.int32, (cap, tok), 0).astype(f32) + 1.0
        placed = jnp.concatenate(
            [(named[p : p + 1, :] == rank).astype(bf16) for p in range(plane)], axis=0
        )
        outs[plane][...] = placed
    at = 0
    for group in groups:
        length = group[0][0][1]
        for first, last in chunks(0, length, 512):
            rows = dot_nn(placed, load(group, first, last)).astype(bf16)
            for p in range(plane):
                outs[p][:, at + first : at + last] = rows[p * cap : (p + 1) * cap]
        at += length


def select_rows(flag, guide, parts, arrays, meta_at, slots_held, cap):
    tok = arrays[0].shape[0]
    length = sum(p[0][1] for p in parts)
    shapes = [jax.ShapeDtypeStruct((cap, length), bf16)] * plane
    if not slots_held:
        shapes.append(jax.ShapeDtypeStruct((plane * cap, tok), bf16))
    return pl.pallas_call(
        functools.partial(select_kernel, parts, meta_at, slots_held, cap),
        out_shape=shapes,
        in_specs=[smem] + [vmem] * (1 + len(arrays)),
        out_specs=[vmem] * len(shapes),
        compiler_params=pltpu.CompilerParams(vmem_limit_bytes=vmem_bytes),
        cost_estimate=light,
    )(flag, guide, *arrays)


def sum_kernel(placed_ref, *refs):
    pieces, outs = refs[:plane], refs[plane:]
    for first, last in chunks(0, outs[0].shape[1], 512):
        rows = jnp.concatenate([p[:, first:last] for p in pieces], axis=0)
        total = dot_tn(placed_ref[...], rows).astype(bf16)
        at = 0
        for out in outs:
            out[:, first:last] = total[at : at + out.shape[0]]
            at += out.shape[0]


def sum_rows(placed, pieces, parts=1):
    cap, width = pieces[0].shape
    tok = placed.shape[1]
    return pl.pallas_call(
        sum_kernel,
        out_shape=[jax.ShapeDtypeStruct((tok // parts, width), bf16)] * parts,
        in_specs=[vmem] * (1 + plane),
        out_specs=[vmem] * parts,
        compiler_params=pltpu.CompilerParams(vmem_limit_bytes=vmem_bytes),
        cost_estimate=light,
    )(placed, *pieces)


def final_kernel(groups, logit_ref, router_ref, *refs):
    out = refs[-1]
    for first, last in chunks(0, out.shape[1], 512):
        total = dot_nn(logit_ref[...], router_ref[:, first:last])
        left = refs
        for count in groups:
            total = total + jnp.concatenate(
                [r[:, first:last] for r in left[:count]], axis=0
            ).astype(f32)
            left = left[count:]
        out[:, first:last] = total.astype(bf16)


def final_sum(logit, router, terms):
    tok, width = logit.shape[0], router.shape[1]
    return pl.pallas_call(
        functools.partial(final_kernel, [len(t) for t in terms]),
        out_shape=jax.ShapeDtypeStruct((tok, width), bf16),
        in_specs=[vmem] * (2 + sum(len(t) for t in terms)),
        out_specs=vmem,
        compiler_params=pltpu.CompilerParams(vmem_limit_bytes=vmem_bytes),
        cost_estimate=light,
    )(logit, router, *[a for t in terms for a in t])


def expert_kernel(
    held, cap, width, rank, mine_ref, wg_ref, wu_ref, wd_ref, ag_ref, au_ref, bg_ref, bu_ref, *refs
):
    ins, refs = refs[:plane], refs[plane:]
    carry, refs = refs[:held], refs[held:]
    back_refs, refs = refs[:plane], refs[plane:]
    route_ref, gag_ref, gau_ref, gbg_ref, gbu_ref = refs[:5]
    xs, dys, weight, low, proj, both, acc = refs[5:]

    def total(at, value, part=slice(None)):
        return value + carry[at][:, part] if held else value

    step = pl.program_id(0)
    tail = width + mine_ref.shape[1]

    @pl.when(step == 0)
    def _():
        for i, ref in enumerate(ins):
            rows = slice(i * cap, (i + 1) * cap)
            xs[rows, :] = ref[:, :width]
            dys[rows, :] = ref[:, tail:]
            weight[rows, :] = jnp.sum(
                ref[:, width:tail].astype(f32) * mine_ref[...], axis=1, keepdims=True
            )
        both[:rank, :] = ag_ref[...]
        both[rank:, :] = au_ref[...]
        low[...] = dot_nt(xs[...], both[...]).astype(bf16)
        proj[...] = jnp.zeros_like(proj)
        acc[...] = jnp.zeros_like(acc)
        route_ref[...] = jnp.zeros_like(route_ref)

    bg, bu = bg_ref[...], bu_ref[...]
    low_gate, low_up = low[:, :rank], low[:, rank:]
    gate = dot_nn(xs[...], wg_ref[...]) + dot_nn(low_gate, bg)
    upval = dot_nn(xs[...], wu_ref[...]) + dot_nn(low_up, bu)
    back = dot_nt(dys[...], wd_ref[...])
    sigma = jax.nn.sigmoid(gate)
    act = gate * sigma
    route_ref[...] += jnp.sum(back * (act * upval), axis=1, keepdims=True)
    scaled = weight[...] * back
    d_gate = (scaled * upval * sigma * (1.0 + gate * (1.0 - sigma))).astype(bf16)
    d_up = (scaled * act).astype(bf16)
    gbg_ref[...] = total(2, dot_tn(low_gate, d_gate))
    gbu_ref[...] = total(3, dot_tn(low_up, d_up))
    proj[:, :rank] += dot_nt(d_gate, bg)
    proj[:, rank:] += dot_nt(d_up, bu)
    for first, last in chunks(0, width, 512):
        acc[:, first:last] += dot_nt(d_gate, wg_ref[first:last, :]) + dot_nt(
            d_up, wu_ref[first:last, :]
        )

    @pl.when(step == pl.num_programs(0) - 1)
    def _():
        proj_b = proj[...].astype(bf16)
        for first, last in chunks(0, width, 512):
            rows = (acc[:, first:last] + dot_nn(proj_b, both[:, first:last])).astype(bf16)
            for i, out in enumerate(back_refs):
                out[:, first:last] = rows[i * cap : (i + 1) * cap]
            part = slice(first, last)
            grad = dot_tn(proj_b, xs[:, part])
            gag_ref[:, part] = total(0, grad[:rank], part)
            gau_ref[:, part] = total(1, grad[rank:], part)


def expert_rows(mine, mats, pieces, carry=()):
    w_gate, w_up, w_down, a_gate, a_up, b_gate, b_up = mats
    width, hidden = w_gate.shape
    rank = a_gate.shape[0]
    cap = pieces[0].shape[0]
    rows = cap * plane
    tile = 256
    second = pl.BlockSpec((rank, tile), lambda j: (0, j))
    grads = [whole_block((rank, width))] * 2 + [second] * 2
    return pl.pallas_call(
        functools.partial(expert_kernel, len(carry), cap, width, rank),
        grid=(hidden // tile,),
        in_specs=[
            whole_block(mine.shape),
            pl.BlockSpec((width, tile), lambda j: (0, j)),
            pl.BlockSpec((width, tile), lambda j: (0, j)),
            pl.BlockSpec((tile, width), lambda j: (j, 0)),
            whole_block(a_gate.shape),
            whole_block(a_up.shape),
            second,
            second,
        ]
        + [whole_block(a.shape) for a in pieces]
        + (grads if carry else []),
        out_shape=[jax.ShapeDtypeStruct((cap, width), bf16)] * plane
        + [
            jax.ShapeDtypeStruct((rows, 1), f32),
            jax.ShapeDtypeStruct((rank, width), f32),
            jax.ShapeDtypeStruct((rank, width), f32),
            jax.ShapeDtypeStruct((rank, hidden), f32),
            jax.ShapeDtypeStruct((rank, hidden), f32),
        ],
        out_specs=[whole_block((cap, width))] * plane + [whole_block((rows, 1))] + grads,
        scratch_shapes=[
            pltpu.VMEM((rows, width), bf16),
            pltpu.VMEM((rows, width), bf16),
            pltpu.VMEM((rows, 1), f32),
            pltpu.VMEM((rows, 2 * rank), bf16),
            pltpu.VMEM((rows, 2 * rank), f32),
            pltpu.VMEM((2 * rank, width), bf16),
            pltpu.VMEM((rows, width), f32),
        ],
        compiler_params=pltpu.CompilerParams(vmem_limit_bytes=vmem_bytes),
        cost_estimate=light,
    )(mine, w_gate, w_up, w_down, a_gate, a_up, b_gate, b_up, *pieces, *carry)


def solution(mesh):
    devices = mesh.shape["expert"]
    layers = devices // plane

    def along(pairs):
        return [(a * plane + q, b * plane + q) for a, b in pairs for q in range(plane)]

    def across(step):
        return [(i, i ^ step) for i in range(devices)]

    def send(array, pairs):
        return lax.ppermute(array, "expert", pairs)

    def spread(pieces):
        return [pieces[0]] + [send(pieces[p], across(p)) for p in range(1, plane)]

    def shards(
        layer_input,
        output_gradient,
        router_matrix,
        routed_expert_index,
        gate_weight_frozen,
        up_weight_frozen,
        down_weight_frozen,
        gate_adapter_first,
        gate_adapter_second,
        up_adapter_first,
        up_adapter_second,
    ):
        tok, width = layer_input.shape
        topk = routed_expert_index.shape[1]
        experts = router_matrix.shape[1]
        capacity = 3 * tok * topk // (2 * experts)
        cap = -(-capacity // 16) * 16
        me = lax.axis_index("expert")
        layer = me // plane
        place = me % plane
        mats = (
            gate_weight_frozen[0],
            up_weight_frozen[0],
            down_weight_frozen[0],
            gate_adapter_first[0].T,
            up_adapter_first[0].T,
            gate_adapter_second[0],
            up_adapter_second[0],
        )
        dy = output_gradient
        join = lax.optimization_barrier

        scores = jax.nn.sigmoid(dot_nn(layer_input, router_matrix))
        expert_ids = jnp.arange(experts, dtype=jnp.int32)
        mask = jnp.sum(
            (routed_expert_index[:, :, None] == expert_ids[None, None, :]).astype(f32), axis=1
        )
        picked = mask * scores
        total = jnp.sum(picked, axis=1, keepdims=True)
        combine = (route_scale * picked / total).astype(bf16)
        earlier = (jnp.arange(tok)[:, None] > jnp.arange(tok)[None, :]).astype(bf16)
        slot_dense = mask * (dot_nn(earlier, mask.astype(bf16)) + 1.0)
        meta_width = -(-2 * experts // 128) * 128
        meta = jnp.concatenate(
            [slot_dense.astype(bf16), combine, jnp.zeros((tok, meta_width - 2 * experts), bf16)],
            axis=1,
        )
        own = jnp.concatenate([layer_input, meta, dy], axis=1)
        full = own.shape[1]
        meta_at = (width, width + meta_width)

        here = layer * plane + (place ^ jnp.arange(plane, dtype=jnp.int32))
        guide = jnp.zeros((16, meta_width), bf16)
        guide = guide.at[:plane].set(
            (here[:, None] == jnp.arange(meta_width, dtype=jnp.int32)[None, :]).astype(bf16)
        )
        mine = (jnp.arange(meta_width) == experts + me).astype(f32)[None, :]

        def take(flag, arrays):
            *pieces, placed = select_rows(
                flag, guide, [[(0, full)] * len(arrays)], arrays, meta_at, False, cap
            )
            return pieces, placed

        def run(pieces, carry=()):
            return expert_rows(mine, mats, pieces, carry)

        if layers == 4:
            mid = (layer == 1) | (layer == 2)
            flag = mid.astype(jnp.int32)[None]
            block_1 = send(own, along([(0, 2), (3, 1), (1, 0), (2, 3)]))
            sel_0, placed_0 = take(flag, [own])
            block_1, own, got_0 = join((block_1, own, spread(sel_0)))
            block_2f = send(block_1, along([(1, 0), (2, 3)]))
            block_2m = send(own, along([(1, 2), (2, 1)]))
            sel_1, placed_1 = take(flag, [block_1])
            got_1 = spread(sel_1)
            done_0 = run(got_0)
            got_1, done_0, own = join((got_1, done_0, own))
            sel_2, placed_2 = take(flag, [block_2m, block_2f])
            sel_2, got_1, own = join((sel_2, got_1, own))
            block_3 = send(own, along([(0, 1), (3, 2), (1, 3), (2, 0)]))
            got_2 = spread(sel_2)
            done_1 = run(got_1, done_0[plane + 1 :])
            done_1, got_2[1], got_2[2] = join((done_1, got_2[1], got_2[2]))
            back_1 = spread(done_1[:plane])
            sel_3, placed_3 = take(flag, [block_3])
            sel_3, back_1, got_2 = join((sel_3, back_1, got_2))
            got_3 = spread(sel_3)
            done_2 = run(got_2, done_1[plane + 1 :])
            done_2, got_3[1], got_3[2] = join((done_2, got_3[1], got_3[2]))
            back_2 = spread(done_2[:plane])
            (part_1,) = sum_rows(placed_1, back_1)
            term_1 = send(part_1, along([(0, 1), (3, 2), (1, 3), (2, 0)]))
            got_3, part_1 = join((got_3, part_1))
            done_3 = run(got_3, done_2[plane + 1 :])
            done_3, term_1, back_2, done_0 = join((done_3, term_1, back_2, done_0))
            back_3 = spread(done_3[:plane])
            part_2a, part_2b = sum_rows(placed_2, back_2, 2)
            term_2a = send(part_2a, across(3 * plane))
            aux = done_3[plane:]
            back_3[1], back_3[2], aux, part_2b, done_0 = join(
                (back_3[1], back_3[2], aux, part_2b, done_0)
            )
            done_3 = [*done_3[:plane], *aux]
            done = [done_0, done_1, done_2, done_3]
            sources = [
                layer,
                jnp.where(mid, layer ^ 2, layer ^ 1),
                layer ^ 3,
                jnp.where(mid, layer ^ 1, layer ^ 2),
            ]
        else:
            flag = jnp.zeros((1,), jnp.int32)
            done, sources, terms = [], [], []
            for g in range(layers):
                block = own if g == 0 else send(own, across(g * plane))
                sel, placed = take(flag, [block])
                result = run(spread(sel), done[-1][plane + 1 :] if done else ())
                (part,) = sum_rows(placed, spread(result[:plane]))
                terms.append([part if g == 0 else send(part, across(g * plane))])
                done.append(result)
                sources.append(layer ^ g)

        route_all = jnp.concatenate(
            [d[plane].reshape(plane, cap) for d in done], axis=0
        )
        origin = (
            jnp.stack(sources)[:, None] * plane
            + (place ^ jnp.arange(plane, dtype=jnp.int32))[None, :]
        ).reshape(-1)
        order = (origin[None, :] == jnp.arange(devices, dtype=jnp.int32)[:, None]).astype(bf16)
        route_sorted = dot_nn(order, route_all.astype(bf16)).astype(bf16)
        ret_route = lax.all_to_all(
            route_sorted, "expert", split_axis=0, concat_axis=0, tiled=True
        )
        if layers == 4:
            ret_route, term_2a, part_2b, done_0 = join((ret_route, term_2a, part_2b, done_0))
            term_2b = send(part_2b, across(3 * plane))
            back_0 = spread(done_0[:plane])
            (part_0,) = sum_rows(placed_0, back_0)
        ret_route = ret_route.astype(f32)
        slots = jnp.arange(1, cap + 1, dtype=jnp.int32).astype(f32)
        hit = slot_dense[:, :, None] == slots[None, None, :]
        route_grad = jnp.sum(jnp.where(hit, ret_route[None, :, :], 0.0), axis=2)
        shared = jnp.sum(route_grad * picked, axis=1, keepdims=True) / (total * total)
        d_pick = route_scale * (route_grad / total - shared)
        d_logit = (mask * d_pick * scores * (1.0 - scores)).astype(bf16)

        if layers == 4:
            (part_3,) = sum_rows(placed_3, back_3)
            term_3 = send(part_3, along([(1, 0), (2, 3), (3, 1), (0, 2)]))
            d_logit, part_3 = join((d_logit, part_3))
            terms = [[part_0], [term_1], [term_2a, term_2b], [term_3]]

        router_part = dot_tn(d_logit, layer_input)
        share = width // devices
        router_part = router_part.reshape(experts, devices, share).transpose(1, 0, 2)
        router_got = lax.all_to_all(router_part, "expert", split_axis=0, concat_axis=0, tiled=True)
        router_grad = jnp.sum(router_got, axis=0).T

        in_grad = final_sum(d_logit, router_matrix.T, terms)

        grad_gate_a, grad_up_a, grad_gate_b, grad_up_b = done[-1][plane + 1 :]
        return (
            in_grad,
            router_grad,
            grad_gate_a.T[None],
            grad_gate_b[None],
            grad_up_a.T[None],
            grad_up_b[None],
        )

    rows = P(("groups", "expert"), None)
    stack = P(("groups", "expert"), None, None)
    frozen = P("expert", None, None)
    in_specs = (rows, rows, P(), rows, frozen, frozen, frozen, stack, stack, stack, stack)
    out_specs = (rows, rows, stack, stack, stack, stack)
    return jax.shard_map(shards, mesh=mesh, in_specs=in_specs, out_specs=out_specs, check_vma=False)
```

```python
import functools

import jax
import jax.numpy as jnp
from jax import lax
from jax.experimental import pallas as pl
from jax.experimental.pallas import tpu as pltpu
from jax.sharding import PartitionSpec as P

route_scale = 2.5
plane = 4
bf16 = jnp.bfloat16
f32 = jnp.float32
vmem_bytes = 56 * 1024 * 1024
light = pl.CostEstimate(flops=1024, bytes_accessed=1024, transcendentals=0)


def dot_nn(left, right):
    return jnp.dot(left, right, preferred_element_type=f32)


def dot_nt(left, right):
    return lax.dot_general(left, right, (((1,), (1,)), ((), ())), preferred_element_type=f32)


def dot_tn(left, right):
    return lax.dot_general(left, right, (((0,), (0,)), ((), ())), preferred_element_type=f32)


def after(array, *others):
    return lax.optimization_barrier((array, *others))[0]


def chunks(start, stop, step):
    return [(at, min(at + step, stop)) for at in range(start, stop, step)]


def whole_block(shape):
    return pl.BlockSpec(shape, lambda *_: (0,) * len(shape), pipeline_mode=pl.Buffered(1))


vmem = pl.BlockSpec(memory_space=pltpu.VMEM)
smem = pl.BlockSpec(memory_space=pltpu.SMEM)


def select_kernel(parts, meta_at, slots_held, cap, flag_ref, guide_ref, *refs):
    count = sum(len(p) for p in parts)
    ins, outs = refs[:count], refs[count:]
    tok = ins[0].shape[0]
    flag = flag_ref[0] == 1
    groups = []
    for part in parts:
        groups.append((part, ins[: len(part)]))
        ins = ins[len(part) :]

    def load(group, first, last):
        part, arrays = group
        values = [a[:, at + first : at + last] for (at, _), a in zip(part, arrays)]
        return values[0] if len(values) == 1 else jnp.where(flag, values[0], values[1])

    if slots_held:
        placed = guide_ref[...]
    else:
        meta = load(groups[0], *meta_at)
        named = dot_nt(guide_ref[...], meta)
        rank = lax.broadcasted_iota(jnp.int32, (cap, tok), 0).astype(f32) + 1.0
        placed = jnp.concatenate(
            [(named[p : p + 1, :] == rank).astype(bf16) for p in range(plane)], axis=0
        )
        outs[plane][...] = placed
    at = 0
    for group in groups:
        length = group[0][0][1]
        for first, last in chunks(0, length, 512):
            rows = dot_nn(placed, load(group, first, last)).astype(bf16)
            for p in range(plane):
                outs[p][:, at + first : at + last] = rows[p * cap : (p + 1) * cap]
        at += length


def select_rows(flag, guide, parts, arrays, meta_at, slots_held, cap):
    tok = arrays[0].shape[0]
    length = sum(p[0][1] for p in parts)
    shapes = [jax.ShapeDtypeStruct((cap, length), bf16)] * plane
    if not slots_held:
        shapes.append(jax.ShapeDtypeStruct((plane * cap, tok), bf16))
    return pl.pallas_call(
        functools.partial(select_kernel, parts, meta_at, slots_held, cap),
        out_shape=shapes,
        in_specs=[smem] + [vmem] * (1 + len(arrays)),
        out_specs=[vmem] * len(shapes),
        compiler_params=pltpu.CompilerParams(vmem_limit_bytes=vmem_bytes),
        cost_estimate=light,
    )(flag, guide, *arrays)


def sum_kernel(apart, placed_ref, *refs):
    pieces, outs = refs[:plane], refs[plane:]
    wide = pieces[0].shape[1]
    rows, tags = (outs[:-1], outs[-1]) if apart else (outs, None)
    stop = rows[0].shape[1]
    for first, last in chunks(0, stop, 512) + chunks(stop, wide, 512):
        joined = jnp.concatenate([p[:, first:last] for p in pieces], axis=0)
        total = dot_tn(placed_ref[...], joined).astype(bf16)
        if first >= stop:
            tags[...] = total
            continue
        at = 0
        for out in rows:
            out[:, first:last] = total[at : at + out.shape[0]]
            at += out.shape[0]


def sum_rows(placed, pieces, width, parts=1):
    cap, wide = pieces[0].shape
    tok = placed.shape[1]
    shapes = [jax.ShapeDtypeStruct((tok // parts, width), bf16)] * parts
    apart = width < wide
    if apart:
        shapes.append(jax.ShapeDtypeStruct((tok, wide - width), bf16))
    return pl.pallas_call(
        functools.partial(sum_kernel, apart),
        out_shape=shapes,
        in_specs=[vmem] * (1 + plane),
        out_specs=[vmem] * len(shapes),
        compiler_params=pltpu.CompilerParams(vmem_limit_bytes=vmem_bytes),
        cost_estimate=light,
    )(placed, *pieces)


def final_kernel(groups, logit_ref, router_ref, *refs):
    out = refs[-1]
    for first, last in chunks(0, out.shape[1], 512):
        total = dot_nn(logit_ref[...], router_ref[:, first:last])
        left = refs
        for count in groups:
            total = total + jnp.concatenate(
                [r[:, first:last] for r in left[:count]], axis=0
            ).astype(f32)
            left = left[count:]
        out[:, first:last] = total.astype(bf16)


def final_sum(logit, router, terms):
    tok, width = logit.shape[0], router.shape[1]
    return pl.pallas_call(
        functools.partial(final_kernel, [len(t) for t in terms]),
        out_shape=jax.ShapeDtypeStruct((tok, width), bf16),
        in_specs=[vmem] * (2 + sum(len(t) for t in terms)),
        out_specs=vmem,
        compiler_params=pltpu.CompilerParams(vmem_limit_bytes=vmem_bytes),
        cost_estimate=light,
    )(logit, router, *[a for t in terms for a in t])


def expert_kernel(
    held, cap, width, rank, mine_ref, wg_ref, wu_ref, wd_ref, ag_ref, au_ref, bg_ref, bu_ref, *refs
):
    ins, refs = refs[:plane], refs[plane:]
    carry, refs = refs[:held], refs[held:]
    back_refs, refs = refs[:plane], refs[plane:]
    gag_ref, gau_ref, gbg_ref, gbu_ref = refs[:4]
    xs, dys, weight, route, low, proj, both, acc = refs[4:]

    def total(at, value, part=slice(None)):
        return value + carry[at][:, part] if held else value

    step = pl.program_id(0)
    tail = width + mine_ref.shape[1]

    @pl.when(step == 0)
    def _():
        for i, ref in enumerate(ins):
            rows = slice(i * cap, (i + 1) * cap)
            xs[rows, :] = ref[:, :width]
            dys[rows, :] = ref[:, tail:]
            weight[rows, :] = jnp.sum(
                ref[:, width:tail].astype(f32) * mine_ref[...], axis=1, keepdims=True
            )
        both[:rank, :] = ag_ref[...]
        both[rank:, :] = au_ref[...]
        low[...] = dot_nt(xs[...], both[...]).astype(bf16)
        proj[...] = jnp.zeros_like(proj)
        acc[...] = jnp.zeros_like(acc)
        route[...] = jnp.zeros_like(route)

    bg, bu = bg_ref[...], bu_ref[...]
    low_gate, low_up = low[:, :rank], low[:, rank:]
    gate = dot_nn(xs[...], wg_ref[...]) + dot_nn(low_gate, bg)
    upval = dot_nn(xs[...], wu_ref[...]) + dot_nn(low_up, bu)
    back = dot_nt(dys[...], wd_ref[...])
    sigma = jax.nn.sigmoid(gate)
    act = gate * sigma
    route[...] += jnp.sum(back * (act * upval), axis=1, keepdims=True)
    scaled = weight[...] * back
    d_gate = (scaled * upval * sigma * (1.0 + gate * (1.0 - sigma))).astype(bf16)
    d_up = (scaled * act).astype(bf16)
    gbg_ref[...] = total(2, dot_tn(low_gate, d_gate))
    gbu_ref[...] = total(3, dot_tn(low_up, d_up))
    proj[:, :rank] += dot_nt(d_gate, bg)
    proj[:, rank:] += dot_nt(d_up, bu)
    for first, last in chunks(0, width, 512):
        acc[:, first:last] += dot_nt(d_gate, wg_ref[first:last, :]) + dot_nt(
            d_up, wu_ref[first:last, :]
        )

    @pl.when(step == pl.num_programs(0) - 1)
    def _():
        proj_b = proj[...].astype(bf16)
        routes = (route[...] * mine_ref[...]).astype(bf16)
        for i, out in enumerate(back_refs):
            out[:, width:] = routes[i * cap : (i + 1) * cap]
        for first, last in chunks(0, width, 512):
            rows = (acc[:, first:last] + dot_nn(proj_b, both[:, first:last])).astype(bf16)
            for i, out in enumerate(back_refs):
                out[:, first:last] = rows[i * cap : (i + 1) * cap]
            part = slice(first, last)
            grad = dot_tn(proj_b, xs[:, part])
            gag_ref[:, part] = total(0, grad[:rank], part)
            gau_ref[:, part] = total(1, grad[rank:], part)


def expert_rows(mine, mats, pieces, carry=()):
    w_gate, w_up, w_down, a_gate, a_up, b_gate, b_up = mats
    width, hidden = w_gate.shape
    rank = a_gate.shape[0]
    cap = pieces[0].shape[0]
    rows = cap * plane
    wide = width + mine.shape[1]
    tile = 512
    second = pl.BlockSpec((rank, tile), lambda j: (0, j))
    grads = [whole_block((rank, width))] * 2 + [second] * 2
    return pl.pallas_call(
        functools.partial(expert_kernel, len(carry), cap, width, rank),
        grid=(hidden // tile,),
        in_specs=[
            whole_block(mine.shape),
            pl.BlockSpec((width, tile), lambda j: (0, j)),
            pl.BlockSpec((width, tile), lambda j: (0, j)),
            pl.BlockSpec((tile, width), lambda j: (j, 0)),
            whole_block(a_gate.shape),
            whole_block(a_up.shape),
            second,
            second,
        ]
        + [whole_block(a.shape) for a in pieces]
        + (grads if carry else []),
        out_shape=[jax.ShapeDtypeStruct((cap, wide), bf16)] * plane
        + [
            jax.ShapeDtypeStruct((rank, width), f32),
            jax.ShapeDtypeStruct((rank, width), f32),
            jax.ShapeDtypeStruct((rank, hidden), f32),
            jax.ShapeDtypeStruct((rank, hidden), f32),
        ],
        out_specs=[whole_block((cap, wide))] * plane + grads,
        scratch_shapes=[
            pltpu.VMEM((rows, width), bf16),
            pltpu.VMEM((rows, width), bf16),
            pltpu.VMEM((rows, 1), f32),
            pltpu.VMEM((rows, 1), f32),
            pltpu.VMEM((rows, 2 * rank), bf16),
            pltpu.VMEM((rows, 2 * rank), f32),
            pltpu.VMEM((2 * rank, width), bf16),
            pltpu.VMEM((rows, width), f32),
        ],
        compiler_params=pltpu.CompilerParams(vmem_limit_bytes=vmem_bytes),
        cost_estimate=light,
    )(mine, w_gate, w_up, w_down, a_gate, a_up, b_gate, b_up, *pieces, *carry)


def solution(mesh):
    devices = mesh.shape["expert"]
    layers = devices // plane

    def along(pairs):
        return [(a * plane + q, b * plane + q) for a, b in pairs for q in range(plane)]

    def across(step):
        return [(i, i ^ step) for i in range(devices)]

    def send(array, pairs):
        return lax.ppermute(array, "expert", pairs)

    def spread(pieces):
        return [pieces[0]] + [send(pieces[p], across(p)) for p in range(1, plane)]

    def shards(
        layer_input,
        output_gradient,
        router_matrix,
        routed_expert_index,
        gate_weight_frozen,
        up_weight_frozen,
        down_weight_frozen,
        gate_adapter_first,
        gate_adapter_second,
        up_adapter_first,
        up_adapter_second,
    ):
        tok, width = layer_input.shape
        topk = routed_expert_index.shape[1]
        experts = router_matrix.shape[1]
        capacity = 3 * tok * topk // (2 * experts)
        cap = -(-capacity // 16) * 16
        me = lax.axis_index("expert")
        layer = me // plane
        place = me % plane
        mats = (
            gate_weight_frozen[0],
            up_weight_frozen[0],
            down_weight_frozen[0],
            gate_adapter_first[0].T,
            up_adapter_first[0].T,
            gate_adapter_second[0],
            up_adapter_second[0],
        )
        dy = output_gradient
        join = lax.optimization_barrier

        scores = jax.nn.sigmoid(dot_nn(layer_input, router_matrix))
        expert_ids = jnp.arange(experts, dtype=jnp.int32)
        mask = jnp.sum(
            (routed_expert_index[:, :, None] == expert_ids[None, None, :]).astype(f32), axis=1
        )
        picked = mask * scores
        total = jnp.sum(picked, axis=1, keepdims=True)
        combine = (route_scale * picked / total).astype(bf16)
        earlier = (jnp.arange(tok)[:, None] > jnp.arange(tok)[None, :]).astype(bf16)
        slot_dense = mask * (dot_nn(earlier, mask.astype(bf16)) + 1.0)
        meta_width = -(-2 * experts // 128) * 128
        meta = jnp.concatenate(
            [slot_dense.astype(bf16), combine, jnp.zeros((tok, meta_width - 2 * experts), bf16)],
            axis=1,
        )
        own = jnp.concatenate([layer_input, meta, dy], axis=1)
        full = own.shape[1]
        wide = width + meta_width
        meta_at = (width, width + meta_width)

        here = layer * plane + (place ^ jnp.arange(plane, dtype=jnp.int32))
        guide = jnp.zeros((16, meta_width), bf16)
        guide = guide.at[:plane].set(
            (here[:, None] == jnp.arange(meta_width, dtype=jnp.int32)[None, :]).astype(bf16)
        )
        mine = (jnp.arange(meta_width) == experts + me).astype(f32)[None, :]

        def take(flag, arrays):
            *pieces, placed = select_rows(
                flag, guide, [[(0, full)] * len(arrays)], arrays, meta_at, False, cap
            )
            return pieces, placed

        def run(pieces, carry=()):
            return expert_rows(mine, mats, pieces, carry)

        if layers == 4:
            mid = (layer == 1) | (layer == 2)
            flag = mid.astype(jnp.int32)[None]
            block_1 = send(own, along([(0, 2), (3, 1), (1, 0), (2, 3)]))
            sel_0, placed_0 = take(flag, [own])
            block_1, own, got_0 = join((block_1, own, spread(sel_0)))
            block_2f = send(block_1, along([(1, 0), (2, 3)]))
            block_2m = send(own, along([(1, 2), (2, 1)]))
            sel_1, placed_1 = take(flag, [block_1])
            got_1 = spread(sel_1)
            done_0 = run(got_0)
            got_1, done_0, own = join((got_1, done_0, own))
            back_0 = [done_0[0], send(done_0[1], across(1)), send(done_0[2], across(2))]
            block_2f, block_2m, own, back_0[1] = join((block_2f, block_2m, own, back_0[1]))
            sel_2, placed_2 = take(flag, [block_2m, block_2f])
            sel_2, got_1, own, back_0[2] = join((sel_2, got_1, own, back_0[2]))
            block_3 = send(own, along([(0, 1), (3, 2), (1, 3), (2, 0)]))
            got_2 = spread(sel_2)
            done_1 = run(got_1, done_0[plane:])
            done_1, got_2[1], got_2[2] = join((done_1, got_2[1], got_2[2]))
            back_1 = spread(done_1[:plane])
            sel_3, placed_3 = take(flag, [block_3])
            sel_3, back_1, got_2 = join((sel_3, back_1, got_2))
            got_3 = spread(sel_3)
            done_2 = run(got_2, done_1[plane:])
            done_2, got_3[1], got_3[2], last_0 = join((done_2, got_3[1], got_3[2], done_0[3]))
            back_2 = spread(done_2[:plane])
            (part_1,) = sum_rows(placed_1, back_1, wide)
            term_1 = send(part_1, along([(0, 1), (3, 2), (1, 3), (2, 0)]))
            got_3, part_1, back_2[1], last_0 = join((got_3, part_1, back_2[1], last_0))
            back_0.append(send(last_0, across(3)))
            done_3 = run(got_3, done_2[plane:])
            done_3, term_1, back_2, back_0 = join((done_3, term_1, back_2, back_0))
            back_3 = spread(done_3[:plane])
            part_2a, part_2b, tag_2 = sum_rows(placed_2, back_2, width, 2)
            tag_2 = send(tag_2, across(3 * plane))
            term_2a = send(part_2a, across(3 * plane))
            back_3[1], back_3[2], part_2b, back_0, tag_2 = join(
                (back_3[1], back_3[2], part_2b, back_0, tag_2)
            )
            part_0, tag_0 = sum_rows(placed_0, back_0, width)
            part_3, tag_3 = sum_rows(placed_3, back_3, width)
            swap_3 = along([(1, 0), (2, 3), (3, 1), (0, 2)])
            tag_3 = send(tag_3, swap_3)
            term_3 = send(part_3, swap_3)
            tag_3, term_2a, part_2b = join((tag_3, term_2a, part_2b))
            term_2b = send(part_2b, across(3 * plane))
            tags = [tag_0, term_1[:, width:], tag_2, tag_3]
            terms = [[part_0], [term_1], [term_2a, term_2b], [term_3]]
            done = [done_3]
        else:
            flag = jnp.zeros((1,), jnp.int32)
            done, tags, terms = [], [], []
            for g in range(layers):
                block = own if g == 0 else send(own, across(g * plane))
                sel, placed = take(flag, [block])
                result = run(spread(sel), done[-1][plane:] if done else ())
                (part,) = sum_rows(placed, spread(result[:plane]), wide)
                terms.append([part if g == 0 else send(part, across(g * plane))])
                done.append(result)
                tags.append(terms[-1][0][:, width:])

        route_grad = sum(t[:, experts : 2 * experts].astype(f32) for t in tags)
        shared = jnp.sum(route_grad * picked, axis=1, keepdims=True) / (total * total)
        d_pick = route_scale * (route_grad / total - shared)
        d_logit = (mask * d_pick * scores * (1.0 - scores)).astype(bf16)

        router_part = dot_tn(d_logit, layer_input)
        share = width // devices
        router_part = router_part.reshape(experts, devices, share).transpose(1, 0, 2)
        router_got = lax.all_to_all(router_part, "expert", split_axis=0, concat_axis=0, tiled=True)
        router_grad = jnp.sum(router_got, axis=0).T

        in_grad = final_sum(d_logit, router_matrix.T, terms)

        grad_gate_a, grad_up_a, grad_gate_b, grad_up_b = done[-1][plane:]
        return (
            in_grad,
            router_grad,
            grad_gate_a.T[None],
            grad_gate_b[None],
            grad_up_a.T[None],
            grad_up_b[None],
        )

    rows = P(("groups", "expert"), None)
    stack = P(("groups", "expert"), None, None)
    frozen = P("expert", None, None)
    in_specs = (rows, rows, P(), rows, frozen, frozen, frozen, stack, stack, stack, stack)
    out_specs = (rows, rows, stack, stack, stack, stack)
    return jax.shard_map(shards, mesh=mesh, in_specs=in_specs, out_specs=out_specs, check_vma=False)
```

```python
import functools

import jax
import jax.numpy as jnp
from jax import lax
from jax.experimental import pallas as pl
from jax.experimental.pallas import tpu as pltpu
from jax.sharding import PartitionSpec as P

route_scale = 2.5
plane = 4
bf16 = jnp.bfloat16
f32 = jnp.float32
vmem_bytes = 56 * 1024 * 1024
light = pl.CostEstimate(flops=1024, bytes_accessed=1024, transcendentals=0)


def dot_nn(left, right):
    return jnp.dot(left, right, preferred_element_type=f32)


def dot_nt(left, right):
    return lax.dot_general(left, right, (((1,), (1,)), ((), ())), preferred_element_type=f32)


def dot_tn(left, right):
    return lax.dot_general(left, right, (((0,), (0,)), ((), ())), preferred_element_type=f32)


def after(array, *others):
    return lax.optimization_barrier((array, *others))[0]


def chunks(start, stop, step):
    return [(at, min(at + step, stop)) for at in range(start, stop, step)]


def whole_block(shape):
    return pl.BlockSpec(shape, lambda *_: (0,) * len(shape), pipeline_mode=pl.Buffered(1))


vmem = pl.BlockSpec(memory_space=pltpu.VMEM)
smem = pl.BlockSpec(memory_space=pltpu.SMEM)


def select_kernel(count, cap, flag_ref, guide_ref, *refs):
    metas, blocks, outs = refs[:count], refs[count : 2 * count], refs[2 * count :]
    placed_ref = outs[plane]
    tok, step = blocks[0].shape
    flag = flag_ref[0] == 1

    def pick(arrays, part):
        values = [a[:, part] for a in arrays]
        return values[0] if count == 1 else jnp.where(flag, values[0], values[1])

    @pl.when(pl.program_id(0) == 0)
    def _():
        named = dot_nt(guide_ref[...], pick(metas, slice(None)))
        rank = lax.broadcasted_iota(jnp.int32, (cap, tok), 0).astype(f32) + 1.0
        for p in range(plane):
            hit = (named[p : p + 1, :] == rank).astype(bf16)
            placed_ref[p * cap : (p + 1) * cap, :] = hit

    for first, last in chunks(0, step, 512):
        rows = dot_nn(placed_ref[...], pick(blocks, slice(first, last))).astype(bf16)
        for p in range(plane):
            outs[p][:, first:last] = rows[p * cap : (p + 1) * cap]


def select_rows(flag, guide, arrays, width, cap):
    tok, full = arrays[0].shape
    meta = guide.shape[1]
    step = full // 3 if full % 384 == 0 else full
    column = pl.BlockSpec((tok, step), lambda j: (0, j))
    return pl.pallas_call(
        functools.partial(select_kernel, len(arrays), cap),
        grid=(full // step,),
        out_shape=[jax.ShapeDtypeStruct((cap, full), bf16)] * plane
        + [jax.ShapeDtypeStruct((plane * cap, tok), bf16)],
        in_specs=[smem, whole_block(guide.shape)]
        + [pl.BlockSpec((tok, meta), lambda j: (0, width // meta))] * len(arrays)
        + [column] * len(arrays),
        out_specs=[pl.BlockSpec((cap, step), lambda j: (0, j))] * plane
        + [whole_block((plane * cap, tok))],
        compiler_params=pltpu.CompilerParams(vmem_limit_bytes=vmem_bytes),
        cost_estimate=light,
    )(flag, guide, *arrays, *arrays)


def sum_kernel(placed_ref, *refs):
    tags, pieces, (out, tag) = refs[:plane], refs[plane : 2 * plane], refs[2 * plane :]

    def total(arrays):
        return dot_tn(placed_ref[...], jnp.concatenate([a[...] for a in arrays], axis=0))

    @pl.when(pl.program_id(0) == 0)
    def _():
        tag[...] = total(tags).astype(bf16)

    out[...] = total(pieces).astype(bf16)


def sum_rows(placed, pieces, width):
    cap, wide = pieces[0].shape
    tok = placed.shape[1]
    meta = wide - width
    step = width // 4 if width % 512 == 0 else width
    return pl.pallas_call(
        sum_kernel,
        grid=(width // step,),
        out_shape=[
            jax.ShapeDtypeStruct((tok, width), bf16),
            jax.ShapeDtypeStruct((tok, meta), bf16),
        ],
        in_specs=[whole_block(placed.shape)]
        + [pl.BlockSpec((cap, meta), lambda j: (0, width // meta))] * plane
        + [pl.BlockSpec((cap, step), lambda j: (0, j))] * plane,
        out_specs=[pl.BlockSpec((tok, step), lambda j: (0, j)), whole_block((tok, meta))],
        compiler_params=pltpu.CompilerParams(vmem_limit_bytes=vmem_bytes),
        cost_estimate=light,
    )(placed, *pieces, *pieces)


def final_kernel(logit_ref, router_ref, *refs):
    total = dot_nn(logit_ref[...], router_ref[...])
    for term in refs[:-1]:
        total = total + term[...].astype(f32)
    refs[-1][...] = total.astype(bf16)


def final_sum(logit, router, terms):
    tok, width = terms[0].shape
    step = width // 4 if width % 512 == 0 else width
    column = pl.BlockSpec((tok, step), lambda j: (0, j))
    return pl.pallas_call(
        final_kernel,
        grid=(width // step,),
        out_shape=jax.ShapeDtypeStruct((tok, width), bf16),
        in_specs=[whole_block(logit.shape), pl.BlockSpec((router.shape[0], step), lambda j: (0, j))]
        + [column] * len(terms),
        out_specs=column,
        compiler_params=pltpu.CompilerParams(vmem_limit_bytes=vmem_bytes),
        cost_estimate=light,
    )(logit, router, *terms)


def expert_kernel(
    held, cap, width, rank, mine_ref, wg_ref, wu_ref, wd_ref, ag_ref, au_ref, bg_ref, bu_ref, *refs
):
    ins, refs = refs[:plane], refs[plane:]
    carry, refs = refs[:held], refs[held:]
    back_refs, refs = refs[:plane], refs[plane:]
    gag_ref, gau_ref, gbg_ref, gbu_ref = refs[:4]
    xs, dys, weight, route, low, proj, both, acc = refs[4:]

    def total(at, value, part=slice(None)):
        return value + carry[at][:, part] if held else value

    step = pl.program_id(0)
    tail = width + mine_ref.shape[1]

    @pl.when(step == 0)
    def _():
        for i, ref in enumerate(ins):
            rows = slice(i * cap, (i + 1) * cap)
            xs[rows, :] = ref[:, :width]
            dys[rows, :] = ref[:, tail:]
            weight[rows, :] = jnp.sum(
                ref[:, width:tail].astype(f32) * mine_ref[...], axis=1, keepdims=True
            )
        both[:rank, :] = ag_ref[...]
        both[rank:, :] = au_ref[...]
        low[...] = dot_nt(xs[...], both[...]).astype(bf16)
        proj[...] = jnp.zeros_like(proj)
        acc[...] = jnp.zeros_like(acc)
        route[...] = jnp.zeros_like(route)

    bg, bu = bg_ref[...], bu_ref[...]
    low_gate, low_up = low[:, :rank], low[:, rank:]
    gate = dot_nn(xs[...], wg_ref[...]) + dot_nn(low_gate, bg)
    upval = dot_nn(xs[...], wu_ref[...]) + dot_nn(low_up, bu)
    back = dot_nt(dys[...], wd_ref[...])
    sigma = jax.nn.sigmoid(gate)
    act = gate * sigma
    route[...] += jnp.sum(back * (act * upval), axis=1, keepdims=True)
    scaled = weight[...] * back
    d_gate = (scaled * upval * sigma * (1.0 + gate * (1.0 - sigma))).astype(bf16)
    d_up = (scaled * act).astype(bf16)
    gbg_ref[...] = total(2, dot_tn(low_gate, d_gate))
    gbu_ref[...] = total(3, dot_tn(low_up, d_up))
    proj[:, :rank] += dot_nt(d_gate, bg)
    proj[:, rank:] += dot_nt(d_up, bu)
    for first, last in chunks(0, width, 512):
        acc[:, first:last] += dot_nt(d_gate, wg_ref[first:last, :]) + dot_nt(
            d_up, wu_ref[first:last, :]
        )

    @pl.when(step == pl.num_programs(0) - 1)
    def _():
        proj_b = proj[...].astype(bf16)
        routes = (route[...] * mine_ref[...]).astype(bf16)
        for i, out in enumerate(back_refs):
            out[:, width:] = routes[i * cap : (i + 1) * cap]
        for first, last in chunks(0, width, 512):
            rows = (acc[:, first:last] + dot_nn(proj_b, both[:, first:last])).astype(bf16)
            for i, out in enumerate(back_refs):
                out[:, first:last] = rows[i * cap : (i + 1) * cap]
            part = slice(first, last)
            grad = dot_tn(proj_b, xs[:, part])
            gag_ref[:, part] = total(0, grad[:rank], part)
            gau_ref[:, part] = total(1, grad[rank:], part)


def expert_rows(mine, mats, pieces, carry=()):
    w_gate, w_up, w_down, a_gate, a_up, b_gate, b_up = mats
    width, hidden = w_gate.shape
    rank = a_gate.shape[0]
    cap = pieces[0].shape[0]
    rows = cap * plane
    wide = width + mine.shape[1]
    tile = 512
    second = pl.BlockSpec((rank, tile), lambda j: (0, j))
    grads = [whole_block((rank, width))] * 2 + [second] * 2
    return pl.pallas_call(
        functools.partial(expert_kernel, len(carry), cap, width, rank),
        grid=(hidden // tile,),
        in_specs=[
            whole_block(mine.shape),
            pl.BlockSpec((width, tile), lambda j: (0, j)),
            pl.BlockSpec((width, tile), lambda j: (0, j)),
            pl.BlockSpec((tile, width), lambda j: (j, 0)),
            whole_block(a_gate.shape),
            whole_block(a_up.shape),
            second,
            second,
        ]
        + [whole_block(a.shape) for a in pieces]
        + (grads if carry else []),
        out_shape=[jax.ShapeDtypeStruct((cap, wide), bf16)] * plane
        + [
            jax.ShapeDtypeStruct((rank, width), f32),
            jax.ShapeDtypeStruct((rank, width), f32),
            jax.ShapeDtypeStruct((rank, hidden), f32),
            jax.ShapeDtypeStruct((rank, hidden), f32),
        ],
        out_specs=[whole_block((cap, wide))] * plane + grads,
        scratch_shapes=[
            pltpu.VMEM((rows, width), bf16),
            pltpu.VMEM((rows, width), bf16),
            pltpu.VMEM((rows, 1), f32),
            pltpu.VMEM((rows, 1), f32),
            pltpu.VMEM((rows, 2 * rank), bf16),
            pltpu.VMEM((rows, 2 * rank), f32),
            pltpu.VMEM((2 * rank, width), bf16),
            pltpu.VMEM((rows, width), f32),
        ],
        compiler_params=pltpu.CompilerParams(vmem_limit_bytes=vmem_bytes),
        cost_estimate=light,
    )(mine, w_gate, w_up, w_down, a_gate, a_up, b_gate, b_up, *pieces, *carry)


def solution(mesh):
    devices = mesh.shape["expert"]
    layers = devices // plane

    def along(pairs):
        return [(a * plane + q, b * plane + q) for a, b in pairs for q in range(plane)]

    def across(step):
        return [(i, i ^ step) for i in range(devices)]

    def send(array, pairs):
        return lax.ppermute(array, "expert", pairs)

    def spread(pieces):
        return [pieces[0]] + [send(pieces[p], across(p)) for p in range(1, plane)]

    def shards(
        layer_input,
        output_gradient,
        router_matrix,
        routed_expert_index,
        gate_weight_frozen,
        up_weight_frozen,
        down_weight_frozen,
        gate_adapter_first,
        gate_adapter_second,
        up_adapter_first,
        up_adapter_second,
    ):
        tok, width = layer_input.shape
        topk = routed_expert_index.shape[1]
        experts = router_matrix.shape[1]
        capacity = 3 * tok * topk // (2 * experts)
        cap = -(-capacity // 16) * 16
        me = lax.axis_index("expert")
        layer = me // plane
        place = me % plane
        mats = (
            gate_weight_frozen[0],
            up_weight_frozen[0],
            down_weight_frozen[0],
            gate_adapter_first[0].T,
            up_adapter_first[0].T,
            gate_adapter_second[0],
            up_adapter_second[0],
        )
        dy = output_gradient
        join = lax.optimization_barrier

        scores = jax.nn.sigmoid(dot_nn(layer_input, router_matrix))
        expert_ids = jnp.arange(experts, dtype=jnp.int32)
        mask = jnp.sum(
            (routed_expert_index[:, :, None] == expert_ids[None, None, :]).astype(f32), axis=1
        )
        picked = mask * scores
        total = jnp.sum(picked, axis=1, keepdims=True)
        combine = (route_scale * picked / total).astype(bf16)
        earlier = (jnp.arange(tok)[:, None] > jnp.arange(tok)[None, :]).astype(bf16)
        slot_dense = mask * (dot_nn(earlier, mask.astype(bf16)) + 1.0)
        meta_width = -(-2 * experts // 128) * 128
        meta = jnp.concatenate(
            [slot_dense.astype(bf16), combine, jnp.zeros((tok, meta_width - 2 * experts), bf16)],
            axis=1,
        )
        own = jnp.concatenate([layer_input, meta, dy], axis=1)
        full = own.shape[1]

        here = layer * plane + (place ^ jnp.arange(plane, dtype=jnp.int32))
        guide = jnp.zeros((16, meta_width), bf16)
        guide = guide.at[:plane].set(
            (here[:, None] == jnp.arange(meta_width, dtype=jnp.int32)[None, :]).astype(bf16)
        )
        mine = (jnp.arange(meta_width) == experts + me).astype(f32)[None, :]

        def take(flag, arrays):
            *pieces, placed = select_rows(flag, guide, arrays, width, cap)
            return pieces, placed

        def run(pieces, carry=()):
            return expert_rows(mine, mats, pieces, carry)

        if layers == 4:
            mid = (layer == 1) | (layer == 2)
            flag = mid.astype(jnp.int32)[None]
            block_1 = send(own, along([(0, 2), (3, 1), (1, 0), (2, 3)]))
            sel_0, placed_0 = take(flag, [own])
            block_1, own, got_0 = join((block_1, own, spread(sel_0)))
            block_2f = send(block_1, along([(1, 0), (2, 3)]))
            block_2m = send(own, along([(1, 2), (2, 1)]))
            sel_1, placed_1 = take(flag, [block_1])
            got_1 = spread(sel_1)
            done_0 = run(got_0)
            got_1, done_0, own = join((got_1, done_0, own))
            back_0 = [done_0[0], send(done_0[1], across(1)), send(done_0[2], across(2))]
            block_2f, block_2m, own, back_0[1] = join((block_2f, block_2m, own, back_0[1]))
            sel_2, placed_2 = take(flag, [block_2m, block_2f])
            sel_2, got_1, own, back_0[2] = join((sel_2, got_1, own, back_0[2]))
            block_3 = send(own, along([(0, 1), (3, 2), (1, 3), (2, 0)]))
            got_2 = spread(sel_2)
            done_1 = run(got_1, done_0[plane:])
            done_1, got_2[1], got_2[2] = join((done_1, got_2[1], got_2[2]))
            back_1 = spread(done_1[:plane])
            sel_3, placed_3 = take(flag, [block_3])
            sel_3, back_1, got_2 = join((sel_3, back_1, got_2))
            got_3 = spread(sel_3)
            done_2 = run(got_2, done_1[plane:])
            done_2, got_3[1], got_3[2], last_0 = join((done_2, got_3[1], got_3[2], done_0[3]))
            back_2 = spread(done_2[:plane])
            part_1, tag_1 = sum_rows(placed_1, back_1, width)
            swap_1 = along([(0, 1), (3, 2), (1, 3), (2, 0)])
            tag_1, term_1 = send(tag_1, swap_1), send(part_1, swap_1)
            got_3, part_1, back_2[1], last_0 = join((got_3, part_1, back_2[1], last_0))
            back_0.append(send(last_0, across(3)))
            done_3 = run(got_3, done_2[plane:])
            done_3, term_1, tag_1, back_2, back_0 = join((done_3, term_1, tag_1, back_2, back_0))
            back_3 = spread(done_3[:plane])
            part_2, tag_2 = sum_rows(placed_2, back_2, width)
            tag_2, term_2 = send(tag_2, across(3 * plane)), send(part_2, across(3 * plane))
            back_3[1], back_3[2], back_0 = join((back_3[1], back_3[2], back_0))
            part_0, tag_0 = sum_rows(placed_0, back_0, width)
            part_3, tag_3 = sum_rows(placed_3, back_3, width)
            swap_3 = along([(1, 0), (2, 3), (3, 1), (0, 2)])
            tag_3 = send(tag_3, swap_3)
            term_3 = send(part_3, swap_3)
            tag_3, tag_2, term_2, part_0 = join((tag_3, tag_2, term_2, part_0))
            tags = [tag_0, tag_1, tag_2, tag_3]
            terms = [part_0, term_1, term_2, term_3]
            done = [done_3]
        else:
            flag = jnp.zeros((1,), jnp.int32)
            done, tags, terms = [], [], []
            for g in range(layers):
                block = own if g == 0 else send(own, across(g * plane))
                sel, placed = take(flag, [block])
                result = run(spread(sel), done[-1][plane:] if done else ())
                part, tag = sum_rows(placed, spread(result[:plane]), width)
                terms.append(part if g == 0 else send(part, across(g * plane)))
                tags.append(tag if g == 0 else send(tag, across(g * plane)))
                done.append(result)

        route_grad = sum(t[:, experts : 2 * experts].astype(f32) for t in tags)
        shared = jnp.sum(route_grad * picked, axis=1, keepdims=True) / (total * total)
        d_pick = route_scale * (route_grad / total - shared)
        d_logit = (mask * d_pick * scores * (1.0 - scores)).astype(bf16)

        router_part = dot_tn(d_logit, layer_input)
        share = width // devices
        router_part = router_part.reshape(experts, devices, share).transpose(1, 0, 2)
        router_got = lax.all_to_all(router_part, "expert", split_axis=0, concat_axis=0, tiled=True)
        router_grad = jnp.sum(router_got, axis=0).T

        in_grad = final_sum(d_logit, router_matrix.T, terms)

        grad_gate_a, grad_up_a, grad_gate_b, grad_up_b = done[-1][plane:]
        return (
            in_grad,
            router_grad,
            grad_gate_a.T[None],
            grad_gate_b[None],
            grad_up_a.T[None],
            grad_up_b[None],
        )

    rows = P(("groups", "expert"), None)
    stack = P(("groups", "expert"), None, None)
    frozen = P("expert", None, None)
    in_specs = (rows, rows, P(), rows, frozen, frozen, frozen, stack, stack, stack, stack)
    out_specs = (rows, rows, stack, stack, stack, stack)
    return jax.shard_map(shards, mesh=mesh, in_specs=in_specs, out_specs=out_specs, check_vma=False)
```

```python
import functools

import jax
import jax.numpy as jnp
from jax import lax
from jax.experimental import pallas as pl
from jax.experimental.pallas import tpu as pltpu
from jax.sharding import PartitionSpec as P

route_scale = 2.5
plane = 4
bf16 = jnp.bfloat16
f32 = jnp.float32
vmem_bytes = 56 * 1024 * 1024
light = pl.CostEstimate(flops=1024, bytes_accessed=1024, transcendentals=0)


def dot_nn(left, right):
    return jnp.dot(left, right, preferred_element_type=f32)


def dot_nt(left, right):
    return lax.dot_general(left, right, (((1,), (1,)), ((), ())), preferred_element_type=f32)


def dot_tn(left, right):
    return lax.dot_general(left, right, (((0,), (0,)), ((), ())), preferred_element_type=f32)


def after(array, *others):
    return lax.optimization_barrier((array, *others))[0]


def chunks(start, stop, step):
    return [(at, min(at + step, stop)) for at in range(start, stop, step)]


def whole_block(shape):
    return pl.BlockSpec(shape, lambda *_: (0,) * len(shape), pipeline_mode=pl.Buffered(1))


vmem = pl.BlockSpec(memory_space=pltpu.VMEM)
smem = pl.BlockSpec(memory_space=pltpu.SMEM)


def select_kernel(parts, meta_at, slots_held, cap, flag_ref, guide_ref, *refs):
    count = sum(len(p) for p in parts)
    ins, outs = refs[:count], refs[count:]
    tok = ins[0].shape[0]
    flag = flag_ref[0] == 1
    groups = []
    for part in parts:
        groups.append((part, ins[: len(part)]))
        ins = ins[len(part) :]

    def load(group, first, last):
        part, arrays = group
        values = [a[:, at + first : at + last] for (at, _), a in zip(part, arrays)]
        return values[0] if len(values) == 1 else jnp.where(flag, values[0], values[1])

    if slots_held:
        placed = guide_ref[...]
    else:
        meta = load(groups[0], *meta_at)
        named = dot_nt(guide_ref[...], meta)
        rank = lax.broadcasted_iota(jnp.int32, (cap, tok), 0).astype(f32) + 1.0
        placed = jnp.concatenate(
            [(named[p : p + 1, :] == rank).astype(bf16) for p in range(plane)], axis=0
        )
        outs[plane][...] = placed
    at = 0
    for group in groups:
        length = group[0][0][1]
        for first, last in chunks(0, length, 512):
            rows = dot_nn(placed, load(group, first, last)).astype(bf16)
            for p in range(plane):
                outs[p][:, at + first : at + last] = rows[p * cap : (p + 1) * cap]
        at += length


def select_rows(flag, guide, parts, arrays, meta_at, slots_held, cap):
    tok = arrays[0].shape[0]
    length = sum(p[0][1] for p in parts)
    shapes = [jax.ShapeDtypeStruct((cap, length), bf16)] * plane
    if not slots_held:
        shapes.append(jax.ShapeDtypeStruct((plane * cap, tok), bf16))
    return pl.pallas_call(
        functools.partial(select_kernel, parts, meta_at, slots_held, cap),
        out_shape=shapes,
        in_specs=[smem] + [vmem] * (1 + len(arrays)),
        out_specs=[vmem] * len(shapes),
        compiler_params=pltpu.CompilerParams(vmem_limit_bytes=vmem_bytes),
        cost_estimate=light,
    )(flag, guide, *arrays)


def sum_kernel(apart, placed_ref, *refs):
    pieces, outs = refs[:plane], refs[plane:]
    wide = pieces[0].shape[1]
    rows, tags = (outs[:-1], outs[-1]) if apart else (outs, None)
    stop = rows[0].shape[1]
    for first, last in chunks(0, stop, 512) + chunks(stop, wide, 512):
        joined = jnp.concatenate([p[:, first:last] for p in pieces], axis=0)
        total = dot_tn(placed_ref[...], joined).astype(bf16)
        if first >= stop:
            tags[...] = total
            continue
        at = 0
        for out in rows:
            out[:, first:last] = total[at : at + out.shape[0]]
            at += out.shape[0]


def sum_rows(placed, pieces, width, lengths=None):
    cap, wide = pieces[0].shape
    tok = placed.shape[1]
    shapes = [jax.ShapeDtypeStruct((length, width), bf16) for length in lengths or (tok,)]
    apart = width < wide
    if apart:
        shapes.append(jax.ShapeDtypeStruct((tok, wide - width), bf16))
    return pl.pallas_call(
        functools.partial(sum_kernel, apart),
        out_shape=shapes,
        in_specs=[vmem] * (1 + plane),
        out_specs=[vmem] * len(shapes),
        compiler_params=pltpu.CompilerParams(vmem_limit_bytes=vmem_bytes),
        cost_estimate=light,
    )(placed, *pieces)


def final_kernel(groups, logit_ref, router_ref, *refs):
    out = refs[-1]
    for first, last in chunks(0, out.shape[1], 512):
        total = dot_nn(logit_ref[...], router_ref[:, first:last])
        left = refs
        for count in groups:
            total = total + jnp.concatenate(
                [r[:, first:last] for r in left[:count]], axis=0
            ).astype(f32)
            left = left[count:]
        out[:, first:last] = total.astype(bf16)


def final_sum(logit, router, terms):
    tok, width = logit.shape[0], router.shape[1]
    return pl.pallas_call(
        functools.partial(final_kernel, [len(t) for t in terms]),
        out_shape=jax.ShapeDtypeStruct((tok, width), bf16),
        in_specs=[vmem] * (2 + sum(len(t) for t in terms)),
        out_specs=vmem,
        compiler_params=pltpu.CompilerParams(vmem_limit_bytes=vmem_bytes),
        cost_estimate=light,
    )(logit, router, *[a for t in terms for a in t])


def expert_kernel(
    held, cap, width, rank, mine_ref, wg_ref, wu_ref, wd_ref, ag_ref, au_ref, bg_ref, bu_ref, *refs
):
    ins, refs = refs[:plane], refs[plane:]
    carry, refs = refs[:held], refs[held:]
    back_refs, refs = refs[:plane], refs[plane:]
    gag_ref, gau_ref, gbg_ref, gbu_ref = refs[:4]
    xs, dys, weight, route, low, proj, both, acc = refs[4:]

    def total(at, value, part=slice(None)):
        return value + carry[at][:, part] if held else value

    step = pl.program_id(0)
    tail = width + mine_ref.shape[1]

    @pl.when(step == 0)
    def _():
        for i, ref in enumerate(ins):
            rows = slice(i * cap, (i + 1) * cap)
            xs[rows, :] = ref[:, :width]
            dys[rows, :] = ref[:, tail:]
            weight[rows, :] = jnp.sum(
                ref[:, width:tail].astype(f32) * mine_ref[...], axis=1, keepdims=True
            )
        both[:rank, :] = ag_ref[...]
        both[rank:, :] = au_ref[...]
        low[...] = dot_nt(xs[...], both[...]).astype(bf16)
        proj[...] = jnp.zeros_like(proj)
        acc[...] = jnp.zeros_like(acc)
        route[...] = jnp.zeros_like(route)

    bg, bu = bg_ref[...], bu_ref[...]
    low_gate, low_up = low[:, :rank], low[:, rank:]
    gate = dot_nn(xs[...], wg_ref[...]) + dot_nn(low_gate, bg)
    upval = dot_nn(xs[...], wu_ref[...]) + dot_nn(low_up, bu)
    back = dot_nt(dys[...], wd_ref[...])
    sigma = jax.nn.sigmoid(gate)
    act = gate * sigma
    route[...] += jnp.sum(back * (act * upval), axis=1, keepdims=True)
    scaled = weight[...] * back
    d_gate = (scaled * upval * sigma * (1.0 + gate * (1.0 - sigma))).astype(bf16)
    d_up = (scaled * act).astype(bf16)
    gbg_ref[...] = total(2, dot_tn(low_gate, d_gate))
    gbu_ref[...] = total(3, dot_tn(low_up, d_up))
    proj[:, :rank] += dot_nt(d_gate, bg)
    proj[:, rank:] += dot_nt(d_up, bu)
    for first, last in chunks(0, width, 512):
        acc[:, first:last] += dot_nt(d_gate, wg_ref[first:last, :]) + dot_nt(
            d_up, wu_ref[first:last, :]
        )

    @pl.when(step == pl.num_programs(0) - 1)
    def _():
        proj_b = proj[...].astype(bf16)
        routes = (route[...] * mine_ref[...]).astype(bf16)
        for i, out in enumerate(back_refs):
            out[:, width:] = routes[i * cap : (i + 1) * cap]
        for first, last in chunks(0, width, 512):
            rows = (acc[:, first:last] + dot_nn(proj_b, both[:, first:last])).astype(bf16)
            for i, out in enumerate(back_refs):
                out[:, first:last] = rows[i * cap : (i + 1) * cap]
            part = slice(first, last)
            grad = dot_tn(proj_b, xs[:, part])
            gag_ref[:, part] = total(0, grad[:rank], part)
            gau_ref[:, part] = total(1, grad[rank:], part)


def expert_rows(mine, mats, pieces, carry=()):
    w_gate, w_up, w_down, a_gate, a_up, b_gate, b_up = mats
    width, hidden = w_gate.shape
    rank = a_gate.shape[0]
    cap = pieces[0].shape[0]
    rows = cap * plane
    wide = width + mine.shape[1]
    tile = 512
    second = pl.BlockSpec((rank, tile), lambda j: (0, j))
    grads = [whole_block((rank, width))] * 2 + [second] * 2
    return pl.pallas_call(
        functools.partial(expert_kernel, len(carry), cap, width, rank),
        grid=(hidden // tile,),
        in_specs=[
            whole_block(mine.shape),
            pl.BlockSpec((width, tile), lambda j: (0, j)),
            pl.BlockSpec((width, tile), lambda j: (0, j)),
            pl.BlockSpec((tile, width), lambda j: (j, 0)),
            whole_block(a_gate.shape),
            whole_block(a_up.shape),
            second,
            second,
        ]
        + [whole_block(a.shape) for a in pieces]
        + (grads if carry else []),
        out_shape=[jax.ShapeDtypeStruct((cap, wide), bf16)] * plane
        + [
            jax.ShapeDtypeStruct((rank, width), f32),
            jax.ShapeDtypeStruct((rank, width), f32),
            jax.ShapeDtypeStruct((rank, hidden), f32),
            jax.ShapeDtypeStruct((rank, hidden), f32),
        ],
        out_specs=[whole_block((cap, wide))] * plane + grads,
        scratch_shapes=[
            pltpu.VMEM((rows, width), bf16),
            pltpu.VMEM((rows, width), bf16),
            pltpu.VMEM((rows, 1), f32),
            pltpu.VMEM((rows, 1), f32),
            pltpu.VMEM((rows, 2 * rank), bf16),
            pltpu.VMEM((rows, 2 * rank), f32),
            pltpu.VMEM((2 * rank, width), bf16),
            pltpu.VMEM((rows, width), f32),
        ],
        compiler_params=pltpu.CompilerParams(vmem_limit_bytes=vmem_bytes),
        cost_estimate=light,
    )(mine, w_gate, w_up, w_down, a_gate, a_up, b_gate, b_up, *pieces, *carry)


def solution(mesh):
    devices = mesh.shape["expert"]
    layers = devices // plane

    def along(pairs):
        return [(a * plane + q, b * plane + q) for a, b in pairs for q in range(plane)]

    def across(step):
        return [(i, i ^ step) for i in range(devices)]

    def send(array, pairs):
        return lax.ppermute(array, "expert", pairs)

    def spread(pieces):
        return [pieces[0]] + [send(pieces[p], across(p)) for p in range(1, plane)]

    def shards(
        layer_input,
        output_gradient,
        router_matrix,
        routed_expert_index,
        gate_weight_frozen,
        up_weight_frozen,
        down_weight_frozen,
        gate_adapter_first,
        gate_adapter_second,
        up_adapter_first,
        up_adapter_second,
    ):
        tok, width = layer_input.shape
        topk = routed_expert_index.shape[1]
        experts = router_matrix.shape[1]
        capacity = 3 * tok * topk // (2 * experts)
        cap = -(-capacity // 16) * 16
        me = lax.axis_index("expert")
        layer = me // plane
        place = me % plane
        mats = (
            gate_weight_frozen[0],
            up_weight_frozen[0],
            down_weight_frozen[0],
            gate_adapter_first[0].T,
            up_adapter_first[0].T,
            gate_adapter_second[0],
            up_adapter_second[0],
        )
        dy = output_gradient
        join = lax.optimization_barrier

        scores = jax.nn.sigmoid(dot_nn(layer_input, router_matrix))
        expert_ids = jnp.arange(experts, dtype=jnp.int32)
        mask = jnp.sum(
            (routed_expert_index[:, :, None] == expert_ids[None, None, :]).astype(f32), axis=1
        )
        picked = mask * scores
        total = jnp.sum(picked, axis=1, keepdims=True)
        combine = (route_scale * picked / total).astype(bf16)
        earlier = (jnp.arange(tok)[:, None] > jnp.arange(tok)[None, :]).astype(bf16)
        slot_dense = mask * (dot_nn(earlier, mask.astype(bf16)) + 1.0)
        meta_width = -(-2 * experts // 128) * 128
        meta = jnp.concatenate(
            [slot_dense.astype(bf16), combine, jnp.zeros((tok, meta_width - 2 * experts), bf16)],
            axis=1,
        )
        own = jnp.concatenate([layer_input, meta, dy], axis=1)
        full = own.shape[1]
        wide = width + meta_width
        meta_at = (width, width + meta_width)

        here = layer * plane + (place ^ jnp.arange(plane, dtype=jnp.int32))
        guide = jnp.zeros((16, meta_width), bf16)
        guide = guide.at[:plane].set(
            (here[:, None] == jnp.arange(meta_width, dtype=jnp.int32)[None, :]).astype(bf16)
        )
        mine = (jnp.arange(meta_width) == experts + me).astype(f32)[None, :]

        def take(flag, arrays):
            *pieces, placed = select_rows(
                flag, guide, [[(0, full)] * len(arrays)], arrays, meta_at, False, cap
            )
            return pieces, placed

        def run(pieces, carry=()):
            return expert_rows(mine, mats, pieces, carry)

        if layers == 4:
            mid = (layer == 1) | (layer == 2)
            flag = mid.astype(jnp.int32)[None]
            block_1 = send(own, along([(0, 2), (3, 1), (1, 0), (2, 3)]))
            sel_0, placed_0 = take(flag, [own])
            block_1, own, got_0 = join((block_1, own, spread(sel_0)))
            block_2f = send(block_1, along([(1, 0), (2, 3)]))
            block_2m = send(own, along([(1, 2), (2, 1)]))
            sel_1, placed_1 = take(flag, [block_1])
            got_1 = spread(sel_1)
            done_0 = run(got_0)
            got_1, done_0, own = join((got_1, done_0, own))
            back_0 = [done_0[0], send(done_0[1], across(1)), send(done_0[2], across(2))]
            block_2f, block_2m, own, back_0[1] = join((block_2f, block_2m, own, back_0[1]))
            sel_2, placed_2 = take(flag, [block_2m, block_2f])
            sel_2, got_1, own, back_0[2] = join((sel_2, got_1, own, back_0[2]))
            block_3 = send(own, along([(0, 1), (3, 2), (1, 3), (2, 0)]))
            got_2 = spread(sel_2)
            done_1 = run(got_1, done_0[plane:])
            done_1, got_2[1], got_2[2] = join((done_1, got_2[1], got_2[2]))
            back_1 = spread(done_1[:plane])
            sel_3, placed_3 = take(flag, [block_3])
            sel_3, back_1, got_2 = join((sel_3, back_1, got_2))
            got_3 = spread(sel_3)
            done_2 = run(got_2, done_1[plane:])
            done_2, got_3[1], got_3[2], last_0 = join((done_2, got_3[1], got_3[2], done_0[3]))
            back_2 = spread(done_2[:plane])
            (part_1,) = sum_rows(placed_1, back_1, wide)
            term_1 = send(part_1, along([(0, 1), (3, 2), (1, 3), (2, 0)]))
            got_3, part_1, back_2, last_0 = join((got_3, part_1, back_2, last_0))
            part_2a, part_2b, tag_2 = sum_rows(placed_2, back_2, width, (tok * 5 // 8, tok * 3 // 8))
            tag_2 = send(tag_2, across(3 * plane))
            term_2a = send(part_2a, across(3 * plane))
            back_0.append(send(last_0, across(3)))
            done_3 = run(got_3, done_2[plane:])
            done_3, term_1, term_2a, tag_2, part_2b, back_0 = join(
                (done_3, term_1, term_2a, tag_2, part_2b, back_0)
            )
            back_3 = spread(done_3[:plane])
            term_2b = send(part_2b, across(3 * plane))
            back_3, back_0, term_2b = join((back_3, back_0, term_2b))
            part_0, tag_0 = sum_rows(placed_0, back_0, width)
            part_3, tag_3 = sum_rows(placed_3, back_3, width)
            swap_3 = along([(1, 0), (2, 3), (3, 1), (0, 2)])
            tag_3 = send(tag_3, swap_3)
            term_3 = send(part_3, swap_3)
            tags = [tag_0, term_1[:, width:], tag_2, tag_3]
            terms = [[part_0], [term_1], [term_2a, term_2b], [term_3]]
            done = [done_3]
        else:
            flag = jnp.zeros((1,), jnp.int32)
            done, tags, terms = [], [], []
            for g in range(layers):
                block = own if g == 0 else send(own, across(g * plane))
                sel, placed = take(flag, [block])
                result = run(spread(sel), done[-1][plane:] if done else ())
                (part,) = sum_rows(placed, spread(result[:plane]), wide)
                terms.append([part if g == 0 else send(part, across(g * plane))])
                done.append(result)
                tags.append(terms[-1][0][:, width:])

        route_grad = sum(t[:, experts : 2 * experts].astype(f32) for t in tags)
        shared = jnp.sum(route_grad * picked, axis=1, keepdims=True) / (total * total)
        d_pick = route_scale * (route_grad / total - shared)
        d_logit = (mask * d_pick * scores * (1.0 - scores)).astype(bf16)

        router_part = dot_tn(d_logit, layer_input)
        share = width // devices
        router_part = router_part.reshape(experts, devices, share).transpose(1, 0, 2)
        router_got = lax.all_to_all(router_part, "expert", split_axis=0, concat_axis=0, tiled=True)
        router_grad = jnp.sum(router_got, axis=0).T

        in_grad = final_sum(d_logit, router_matrix.T, terms)

        grad_gate_a, grad_up_a, grad_gate_b, grad_up_b = done[-1][plane:]
        return (
            in_grad,
            router_grad,
            grad_gate_a.T[None],
            grad_gate_b[None],
            grad_up_a.T[None],
            grad_up_b[None],
        )

    rows = P(("groups", "expert"), None)
    stack = P(("groups", "expert"), None, None)
    frozen = P("expert", None, None)
    in_specs = (rows, rows, P(), rows, frozen, frozen, frozen, stack, stack, stack, stack)
    out_specs = (rows, rows, stack, stack, stack, stack)
    return jax.shard_map(shards, mesh=mesh, in_specs=in_specs, out_specs=out_specs, check_vma=False)
```

```python
import functools

import jax
import jax.numpy as jnp
from jax import lax
from jax.experimental import pallas as pl
from jax.experimental.pallas import tpu as pltpu
from jax.sharding import PartitionSpec as P

route_scale = 2.5
plane = 4
bf16 = jnp.bfloat16
f32 = jnp.float32
vmem_bytes = 56 * 1024 * 1024
light = pl.CostEstimate(flops=1024, bytes_accessed=1024, transcendentals=0)


def dot_nn(left, right):
    return jnp.dot(left, right, preferred_element_type=f32)


def dot_nt(left, right):
    return lax.dot_general(left, right, (((1,), (1,)), ((), ())), preferred_element_type=f32)


def dot_tn(left, right):
    return lax.dot_general(left, right, (((0,), (0,)), ((), ())), preferred_element_type=f32)


def after(array, *others):
    return lax.optimization_barrier((array, *others))[0]


def chunks(start, stop, step):
    return [(at, min(at + step, stop)) for at in range(start, stop, step)]


def whole_block(shape):
    return pl.BlockSpec(shape, lambda *_: (0,) * len(shape), pipeline_mode=pl.Buffered(1))


vmem = pl.BlockSpec(memory_space=pltpu.VMEM)
smem = pl.BlockSpec(memory_space=pltpu.SMEM)


def select_kernel(parts, meta_at, slots_held, cap, flag_ref, guide_ref, *refs):
    count = sum(len(p) for p in parts)
    ins, outs = refs[:count], refs[count:]
    tok = ins[0].shape[0]
    flag = flag_ref[0] == 1
    groups = []
    for part in parts:
        groups.append((part, ins[: len(part)]))
        ins = ins[len(part) :]

    def load(group, first, last):
        part, arrays = group
        values = [a[:, at + first : at + last] for (at, _), a in zip(part, arrays)]
        return values[0] if len(values) == 1 else jnp.where(flag, values[0], values[1])

    if slots_held:
        placed = guide_ref[...]
    else:
        meta = load(groups[0], *meta_at)
        named = dot_nt(guide_ref[...], meta)
        rank = lax.broadcasted_iota(jnp.int32, (cap, tok), 0).astype(f32) + 1.0
        placed = jnp.concatenate(
            [(named[p : p + 1, :] == rank).astype(bf16) for p in range(plane)], axis=0
        )
        outs[plane][...] = placed
    at = 0
    for group in groups:
        length = group[0][0][1]
        for first, last in chunks(0, length, 512):
            rows = dot_nn(placed, load(group, first, last)).astype(bf16)
            for p in range(plane):
                outs[p][:, at + first : at + last] = rows[p * cap : (p + 1) * cap]
        at += length


def select_rows(flag, guide, parts, arrays, meta_at, slots_held, cap):
    tok = arrays[0].shape[0]
    length = sum(p[0][1] for p in parts)
    shapes = [jax.ShapeDtypeStruct((cap, length), bf16)] * plane
    if not slots_held:
        shapes.append(jax.ShapeDtypeStruct((plane * cap, tok), bf16))
    return pl.pallas_call(
        functools.partial(select_kernel, parts, meta_at, slots_held, cap),
        out_shape=shapes,
        in_specs=[smem] + [vmem] * (1 + len(arrays)),
        out_specs=[vmem] * len(shapes),
        compiler_params=pltpu.CompilerParams(vmem_limit_bytes=vmem_bytes),
        cost_estimate=light,
    )(flag, guide, *arrays)


def sum_kernel(apart, placed_ref, *refs):
    pieces, outs = refs[:plane], refs[plane:]
    wide = pieces[0].shape[1]
    rows, tags = (outs[:-1], outs[-1]) if apart else (outs, None)
    stop = rows[0].shape[1]
    for first, last in chunks(0, stop, 512) + chunks(stop, wide, 512):
        joined = jnp.concatenate([p[:, first:last] for p in pieces], axis=0)
        total = dot_tn(placed_ref[...], joined).astype(bf16)
        if first >= stop:
            tags[...] = total
            continue
        at = 0
        for out in rows:
            out[:, first:last] = total[at : at + out.shape[0]]
            at += out.shape[0]


def sum_rows(placed, pieces, width, lengths=None):
    cap, wide = pieces[0].shape
    tok = placed.shape[1]
    shapes = [jax.ShapeDtypeStruct((length, width), bf16) for length in lengths or (tok,)]
    apart = width < wide
    if apart:
        shapes.append(jax.ShapeDtypeStruct((tok, wide - width), bf16))
    return pl.pallas_call(
        functools.partial(sum_kernel, apart),
        out_shape=shapes,
        in_specs=[vmem] * (1 + plane),
        out_specs=[vmem] * len(shapes),
        compiler_params=pltpu.CompilerParams(vmem_limit_bytes=vmem_bytes),
        cost_estimate=light,
    )(placed, *pieces)


def final_kernel(groups, logit_ref, router_ref, *refs):
    out = refs[-1]
    for first, last in chunks(0, out.shape[1], 512):
        total = dot_nn(logit_ref[...], router_ref[:, first:last])
        left = refs
        for count in groups:
            total = total + jnp.concatenate(
                [r[:, first:last] for r in left[:count]], axis=0
            ).astype(f32)
            left = left[count:]
        out[:, first:last] = total.astype(bf16)


def final_sum(logit, router, terms):
    tok, width = logit.shape[0], router.shape[1]
    return pl.pallas_call(
        functools.partial(final_kernel, [len(t) for t in terms]),
        out_shape=jax.ShapeDtypeStruct((tok, width), bf16),
        in_specs=[vmem] * (2 + sum(len(t) for t in terms)),
        out_specs=vmem,
        compiler_params=pltpu.CompilerParams(vmem_limit_bytes=vmem_bytes),
        cost_estimate=light,
    )(logit, router, *[a for t in terms for a in t])


def expert_kernel(
    held, cap, width, rank, mine_ref, wg_ref, wu_ref, wd_ref, ag_ref, au_ref, bg_ref, bu_ref, *refs
):
    ins, refs = refs[:plane], refs[plane:]
    carry, refs = refs[:held], refs[held:]
    back_refs, refs = refs[:plane], refs[plane:]
    gag_ref, gau_ref, gbg_ref, gbu_ref = refs[:4]
    xs, dys, weight, route, low, proj, both, acc = refs[4:]

    def total(at, value, part=slice(None)):
        return value + carry[at][:, part] if held else value

    step = pl.program_id(0)
    tail = width + mine_ref.shape[1]

    @pl.when(step == 0)
    def _():
        for i, ref in enumerate(ins):
            rows = slice(i * cap, (i + 1) * cap)
            xs[rows, :] = ref[:, :width]
            dys[rows, :] = ref[:, tail:]
            weight[rows, :] = jnp.sum(
                ref[:, width:tail].astype(f32) * mine_ref[...], axis=1, keepdims=True
            )
        both[:rank, :] = ag_ref[...]
        both[rank:, :] = au_ref[...]
        low[...] = dot_nt(xs[...], both[...]).astype(bf16)
        proj[...] = jnp.zeros_like(proj)
        acc[...] = jnp.zeros_like(acc)
        route[...] = jnp.zeros_like(route)

    bg, bu = bg_ref[...], bu_ref[...]
    low_gate, low_up = low[:, :rank], low[:, rank:]
    gate = dot_nn(xs[...], wg_ref[...]) + dot_nn(low_gate, bg)
    upval = dot_nn(xs[...], wu_ref[...]) + dot_nn(low_up, bu)
    back = dot_nt(dys[...], wd_ref[...])
    sigma = jax.nn.sigmoid(gate)
    act = gate * sigma
    route[...] += jnp.sum(back * (act * upval), axis=1, keepdims=True)
    scaled = weight[...] * back
    d_gate = (scaled * upval * sigma * (1.0 + gate * (1.0 - sigma))).astype(bf16)
    d_up = (scaled * act).astype(bf16)
    gbg_ref[...] = total(2, dot_tn(low_gate, d_gate))
    gbu_ref[...] = total(3, dot_tn(low_up, d_up))
    proj[:, :rank] += dot_nt(d_gate, bg)
    proj[:, rank:] += dot_nt(d_up, bu)
    for first, last in chunks(0, width, 512):
        acc[:, first:last] += dot_nt(d_gate, wg_ref[first:last, :]) + dot_nt(
            d_up, wu_ref[first:last, :]
        )

    @pl.when(step == pl.num_programs(0) - 1)
    def _():
        proj_b = proj[...].astype(bf16)
        routes = (route[...] * mine_ref[...]).astype(bf16)
        for i, out in enumerate(back_refs):
            out[:, width:] = routes[i * cap : (i + 1) * cap]
        for first, last in chunks(0, width, 512):
            rows = (acc[:, first:last] + dot_nn(proj_b, both[:, first:last])).astype(bf16)
            for i, out in enumerate(back_refs):
                out[:, first:last] = rows[i * cap : (i + 1) * cap]
            part = slice(first, last)
            grad = dot_tn(proj_b, xs[:, part])
            gag_ref[:, part] = total(0, grad[:rank], part)
            gau_ref[:, part] = total(1, grad[rank:], part)


def expert_rows(mine, mats, pieces, carry=()):
    w_gate, w_up, w_down, a_gate, a_up, b_gate, b_up = mats
    width, hidden = w_gate.shape
    rank = a_gate.shape[0]
    cap = pieces[0].shape[0]
    rows = cap * plane
    wide = width + mine.shape[1]
    tile = 512
    second = pl.BlockSpec((rank, tile), lambda j: (0, j))
    grads = [whole_block((rank, width))] * 2 + [second] * 2
    return pl.pallas_call(
        functools.partial(expert_kernel, len(carry), cap, width, rank),
        grid=(hidden // tile,),
        in_specs=[
            whole_block(mine.shape),
            pl.BlockSpec((width, tile), lambda j: (0, j)),
            pl.BlockSpec((width, tile), lambda j: (0, j)),
            pl.BlockSpec((tile, width), lambda j: (j, 0)),
            whole_block(a_gate.shape),
            whole_block(a_up.shape),
            second,
            second,
        ]
        + [whole_block(a.shape) for a in pieces]
        + (grads if carry else []),
        out_shape=[jax.ShapeDtypeStruct((cap, wide), bf16)] * plane
        + [
            jax.ShapeDtypeStruct((rank, width), f32),
            jax.ShapeDtypeStruct((rank, width), f32),
            jax.ShapeDtypeStruct((rank, hidden), f32),
            jax.ShapeDtypeStruct((rank, hidden), f32),
        ],
        out_specs=[whole_block((cap, wide))] * plane + grads,
        scratch_shapes=[
            pltpu.VMEM((rows, width), bf16),
            pltpu.VMEM((rows, width), bf16),
            pltpu.VMEM((rows, 1), f32),
            pltpu.VMEM((rows, 1), f32),
            pltpu.VMEM((rows, 2 * rank), bf16),
            pltpu.VMEM((rows, 2 * rank), f32),
            pltpu.VMEM((2 * rank, width), bf16),
            pltpu.VMEM((rows, width), f32),
        ],
        compiler_params=pltpu.CompilerParams(vmem_limit_bytes=vmem_bytes),
        cost_estimate=light,
    )(mine, w_gate, w_up, w_down, a_gate, a_up, b_gate, b_up, *pieces, *carry)


def solution(mesh):
    devices = mesh.shape["expert"]
    layers = devices // plane

    def along(pairs):
        return [(a * plane + q, b * plane + q) for a, b in pairs for q in range(plane)]

    def across(step):
        return [(i, i ^ step) for i in range(devices)]

    def send(array, pairs):
        return lax.ppermute(array, "expert", pairs)

    def spread(pieces):
        return [pieces[0]] + [send(pieces[p], across(p)) for p in range(1, plane)]

    def shards(
        layer_input,
        output_gradient,
        router_matrix,
        routed_expert_index,
        gate_weight_frozen,
        up_weight_frozen,
        down_weight_frozen,
        gate_adapter_first,
        gate_adapter_second,
        up_adapter_first,
        up_adapter_second,
    ):
        tok, width = layer_input.shape
        topk = routed_expert_index.shape[1]
        experts = router_matrix.shape[1]
        capacity = 3 * tok * topk // (2 * experts)
        cap = -(-capacity // 16) * 16
        me = lax.axis_index("expert")
        layer = me // plane
        place = me % plane
        mats = (
            gate_weight_frozen[0],
            up_weight_frozen[0],
            down_weight_frozen[0],
            gate_adapter_first[0].T,
            up_adapter_first[0].T,
            gate_adapter_second[0],
            up_adapter_second[0],
        )
        dy = output_gradient
        join = lax.optimization_barrier

        scores = jax.nn.sigmoid(dot_nn(layer_input, router_matrix))
        expert_ids = jnp.arange(experts, dtype=jnp.int32)
        mask = jnp.sum(
            (routed_expert_index[:, :, None] == expert_ids[None, None, :]).astype(f32), axis=1
        )
        picked = mask * scores
        total = jnp.sum(picked, axis=1, keepdims=True)
        combine = (route_scale * picked / total).astype(bf16)
        earlier = (jnp.arange(tok)[:, None] > jnp.arange(tok)[None, :]).astype(bf16)
        slot_dense = mask * (dot_nn(earlier, mask.astype(bf16)) + 1.0)
        meta_width = -(-2 * experts // 128) * 128
        meta = jnp.concatenate(
            [slot_dense.astype(bf16), combine, jnp.zeros((tok, meta_width - 2 * experts), bf16)],
            axis=1,
        )
        own = jnp.concatenate([layer_input, meta, dy], axis=1)
        full = own.shape[1]
        wide = width + meta_width
        meta_at = (width, width + meta_width)

        here = layer * plane + (place ^ jnp.arange(plane, dtype=jnp.int32))
        guide = jnp.zeros((16, meta_width), bf16)
        guide = guide.at[:plane].set(
            (here[:, None] == jnp.arange(meta_width, dtype=jnp.int32)[None, :]).astype(bf16)
        )
        mine = (jnp.arange(meta_width) == experts + me).astype(f32)[None, :]

        def take(flag, arrays):
            *pieces, placed = select_rows(
                flag, guide, [[(0, full)] * len(arrays)], arrays, meta_at, False, cap
            )
            return pieces, placed

        def run(pieces, carry=()):
            return expert_rows(mine, mats, pieces, carry)

        if layers == 4:
            mid = (layer == 1) | (layer == 2)
            flag = mid.astype(jnp.int32)[None]
            block_1 = send(own, along([(0, 2), (3, 1), (1, 0), (2, 3)]))
            sel_0, placed_0 = take(flag, [own])
            block_1, own, got_0 = join((block_1, own, spread(sel_0)))
            block_2f = send(block_1, along([(1, 0), (2, 3)]))
            block_2m = send(own, along([(1, 2), (2, 1)]))
            sel_1, placed_1 = take(flag, [block_1])
            got_1 = spread(sel_1)
            done_0 = run(got_0)
            got_1, done_0, own = join((got_1, done_0, own))
            sel_2, placed_2 = take(flag, [block_2m, block_2f])
            sel_2, got_1, own = join((sel_2, got_1, own))
            block_3 = send(own, along([(0, 1), (3, 2), (1, 3), (2, 0)]))
            got_2 = spread(sel_2)
            done_1 = run(got_1, done_0[plane:])
            done_1, got_2[1], got_2[2] = join((done_1, got_2[1], got_2[2]))
            back_1 = spread(done_1[:plane])
            sel_3, placed_3 = take(flag, [block_3])
            sel_3, back_1, got_2 = join((sel_3, back_1, got_2))
            got_3 = spread(sel_3)
            done_2 = run(got_2, done_1[plane:])
            done_2, got_3[1], got_3[2], done_0 = join((done_2, got_3[1], got_3[2], done_0))
            back_2 = spread(done_2[:plane])
            (part_1,) = sum_rows(placed_1, back_1, wide)
            term_1 = send(part_1, along([(0, 1), (3, 2), (1, 3), (2, 0)]))
            got_3, part_1, back_2, done_0 = join((got_3, part_1, back_2, done_0))
            part_2a, part_2b, tag_2 = sum_rows(placed_2, back_2, width, (tok * 5 // 8, tok * 3 // 8))
            tag_2 = send(tag_2, across(3 * plane))
            term_2a = send(part_2a, across(3 * plane))
            back_0 = spread(done_0[:plane])
            done_3 = run(got_3, done_2[plane:])
            done_3, term_1, term_2a, part_2b, back_0 = join(
                (done_3, term_1, term_2a, part_2b, back_0)
            )
            back_3 = spread(done_3[:plane])
            term_2b = send(part_2b, across(3 * plane))
            back_3, back_0, term_2b = join((back_3, back_0, term_2b))
            part_0, tag_0 = sum_rows(placed_0, back_0, width)
            part_3, tag_3 = sum_rows(placed_3, back_3, width)
            swap_3 = along([(1, 0), (2, 3), (3, 1), (0, 2)])
            tag_3 = send(tag_3, swap_3)
            term_3 = send(part_3, swap_3)
            tags = [tag_0, term_1[:, width:], tag_2, tag_3]
            terms = [[part_0], [term_1], [term_2a, term_2b], [term_3]]
            done = [done_3]
        else:
            flag = jnp.zeros((1,), jnp.int32)
            done, tags, terms = [], [], []
            for g in range(layers):
                block = own if g == 0 else send(own, across(g * plane))
                sel, placed = take(flag, [block])
                result = run(spread(sel), done[-1][plane:] if done else ())
                (part,) = sum_rows(placed, spread(result[:plane]), wide)
                terms.append([part if g == 0 else send(part, across(g * plane))])
                done.append(result)
                tags.append(terms[-1][0][:, width:])

        route_grad = sum(t[:, experts : 2 * experts].astype(f32) for t in tags)
        shared = jnp.sum(route_grad * picked, axis=1, keepdims=True) / (total * total)
        d_pick = route_scale * (route_grad / total - shared)
        d_logit = (mask * d_pick * scores * (1.0 - scores)).astype(bf16)

        router_part = dot_tn(d_logit, layer_input)
        share = width // devices
        router_part = router_part.reshape(experts, devices, share).transpose(1, 0, 2)
        router_got = lax.all_to_all(router_part, "expert", split_axis=0, concat_axis=0, tiled=True)
        router_grad = jnp.sum(router_got, axis=0).T

        in_grad = final_sum(d_logit, router_matrix.T, terms)

        grad_gate_a, grad_up_a, grad_gate_b, grad_up_b = done[-1][plane:]
        return (
            in_grad,
            router_grad,
            grad_gate_a.T[None],
            grad_gate_b[None],
            grad_up_a.T[None],
            grad_up_b[None],
        )

    rows = P(("groups", "expert"), None)
    stack = P(("groups", "expert"), None, None)
    frozen = P("expert", None, None)
    in_specs = (rows, rows, P(), rows, frozen, frozen, frozen, stack, stack, stack, stack)
    out_specs = (rows, rows, stack, stack, stack, stack)
    return jax.shard_map(shards, mesh=mesh, in_specs=in_specs, out_specs=out_specs, check_vma=False)
```

```python
import functools

import jax
import jax.numpy as jnp
from jax import lax
from jax.experimental import pallas as pl
from jax.experimental.pallas import tpu as pltpu
from jax.sharding import PartitionSpec as P

route_scale = 2.5
plane = 4
bf16 = jnp.bfloat16
f32 = jnp.float32
vmem_bytes = 56 * 1024 * 1024
light = pl.CostEstimate(flops=1024, bytes_accessed=1024, transcendentals=0)


def dot_nn(left, right):
    return jnp.dot(left, right, preferred_element_type=f32)


def dot_nt(left, right):
    return lax.dot_general(left, right, (((1,), (1,)), ((), ())), preferred_element_type=f32)


def dot_tn(left, right):
    return lax.dot_general(left, right, (((0,), (0,)), ((), ())), preferred_element_type=f32)


def after(array, *others):
    return lax.optimization_barrier((array, *others))[0]


def chunks(start, stop, step):
    return [(at, min(at + step, stop)) for at in range(start, stop, step)]


def whole_block(shape):
    return pl.BlockSpec(shape, lambda *_: (0,) * len(shape), pipeline_mode=pl.Buffered(1))


vmem = pl.BlockSpec(memory_space=pltpu.VMEM)
smem = pl.BlockSpec(memory_space=pltpu.SMEM)


def select_kernel(parts, meta_at, slots_held, cap, flag_ref, guide_ref, *refs):
    count = sum(len(p) for p in parts)
    ins, outs = refs[:count], refs[count:]
    tok = ins[0].shape[0]
    flag = flag_ref[0] == 1
    groups = []
    for part in parts:
        groups.append((part, ins[: len(part)]))
        ins = ins[len(part) :]

    def load(group, first, last):
        part, arrays = group
        values = [a[:, at + first : at + last] for (at, _), a in zip(part, arrays)]
        return values[0] if len(values) == 1 else jnp.where(flag, values[0], values[1])

    if slots_held:
        placed = guide_ref[...]
    else:
        meta = load(groups[0], *meta_at)
        named = dot_nt(guide_ref[...], meta)
        rank = lax.broadcasted_iota(jnp.int32, (cap, tok), 0).astype(f32) + 1.0
        placed = jnp.concatenate(
            [(named[p : p + 1, :] == rank).astype(bf16) for p in range(plane)], axis=0
        )
        outs[plane][...] = placed
    at = 0
    for group in groups:
        length = group[0][0][1]
        for first, last in chunks(0, length, 512):
            rows = dot_nn(placed, load(group, first, last)).astype(bf16)
            for p in range(plane):
                outs[p][:, at + first : at + last] = rows[p * cap : (p + 1) * cap]
        at += length


def select_rows(flag, guide, parts, arrays, meta_at, slots_held, cap):
    tok = arrays[0].shape[0]
    length = sum(p[0][1] for p in parts)
    shapes = [jax.ShapeDtypeStruct((cap, length), bf16)] * plane
    if not slots_held:
        shapes.append(jax.ShapeDtypeStruct((plane * cap, tok), bf16))
    return pl.pallas_call(
        functools.partial(select_kernel, parts, meta_at, slots_held, cap),
        out_shape=shapes,
        in_specs=[smem] + [vmem] * (1 + len(arrays)),
        out_specs=[vmem] * len(shapes),
        compiler_params=pltpu.CompilerParams(vmem_limit_bytes=vmem_bytes),
        cost_estimate=light,
    )(flag, guide, *arrays)


def sum_kernel(apart, placed_ref, *refs):
    pieces, outs = refs[:plane], refs[plane:]
    wide = pieces[0].shape[1]
    rows, tags = (outs[:-1], outs[-1]) if apart else (outs, None)
    stop = rows[0].shape[1]
    for first, last in chunks(0, stop, 512) + chunks(stop, wide, 512):
        joined = jnp.concatenate([p[:, first:last] for p in pieces], axis=0)
        total = dot_tn(placed_ref[...], joined).astype(bf16)
        if first >= stop:
            tags[...] = total
            continue
        at = 0
        for out in rows:
            out[:, first:last] = total[at : at + out.shape[0]]
            at += out.shape[0]


def sum_rows(placed, pieces, width, lengths=None):
    cap, wide = pieces[0].shape
    tok = placed.shape[1]
    shapes = [jax.ShapeDtypeStruct((length, width), bf16) for length in lengths or (tok,)]
    apart = width < wide
    if apart:
        shapes.append(jax.ShapeDtypeStruct((tok, wide - width), bf16))
    return pl.pallas_call(
        functools.partial(sum_kernel, apart),
        out_shape=shapes,
        in_specs=[vmem] * (1 + plane),
        out_specs=[vmem] * len(shapes),
        compiler_params=pltpu.CompilerParams(vmem_limit_bytes=vmem_bytes),
        cost_estimate=light,
    )(placed, *pieces)


def final_kernel(groups, logit_ref, router_ref, *refs):
    out = refs[-1]
    for first, last in chunks(0, out.shape[1], 512):
        total = dot_nn(logit_ref[...], router_ref[:, first:last])
        left = refs
        for count in groups:
            total = total + jnp.concatenate(
                [r[:, first:last] for r in left[:count]], axis=0
            ).astype(f32)
            left = left[count:]
        out[:, first:last] = total.astype(bf16)


def final_sum(logit, router, terms):
    tok, width = logit.shape[0], router.shape[1]
    return pl.pallas_call(
        functools.partial(final_kernel, [len(t) for t in terms]),
        out_shape=jax.ShapeDtypeStruct((tok, width), bf16),
        in_specs=[vmem] * (2 + sum(len(t) for t in terms)),
        out_specs=vmem,
        compiler_params=pltpu.CompilerParams(vmem_limit_bytes=vmem_bytes),
        cost_estimate=light,
    )(logit, router, *[a for t in terms for a in t])


def expert_kernel(
    held, cap, width, rank, mine_ref, wg_ref, wu_ref, wd_ref, ag_ref, au_ref, bg_ref, bu_ref, *refs
):
    ins, refs = refs[:plane], refs[plane:]
    carry, refs = refs[:held], refs[held:]
    back_refs, refs = refs[:plane], refs[plane:]
    gag_ref, gau_ref, gbg_ref, gbu_ref, tag_ref = refs[:5]
    xs, dys, weight, route, low, proj, both, acc = refs[5:]

    def total(at, value, part=slice(None)):
        return value + carry[at][:, part] if held else value

    step = pl.program_id(0)
    tail = width + mine_ref.shape[1]

    @pl.when(step == 0)
    def _():
        for i, ref in enumerate(ins):
            rows = slice(i * cap, (i + 1) * cap)
            xs[rows, :] = ref[:, :width]
            dys[rows, :] = ref[:, tail:]
            weight[rows, :] = jnp.sum(
                ref[:, width:tail].astype(f32) * mine_ref[...], axis=1, keepdims=True
            )
        both[:rank, :] = ag_ref[...]
        both[rank:, :] = au_ref[...]
        low[...] = dot_nt(xs[...], both[...]).astype(bf16)
        proj[...] = jnp.zeros_like(proj)
        acc[...] = jnp.zeros_like(acc)
        route[...] = jnp.zeros_like(route)

    bg, bu = bg_ref[...], bu_ref[...]
    low_gate, low_up = low[:, :rank], low[:, rank:]
    gate = dot_nn(xs[...], wg_ref[...]) + dot_nn(low_gate, bg)
    upval = dot_nn(xs[...], wu_ref[...]) + dot_nn(low_up, bu)
    back = dot_nt(dys[...], wd_ref[...])
    sigma = jax.nn.sigmoid(gate)
    act = gate * sigma
    route[...] += jnp.sum(back * (act * upval), axis=1, keepdims=True)
    scaled = weight[...] * back
    d_gate = (scaled * upval * sigma * (1.0 + gate * (1.0 - sigma))).astype(bf16)
    d_up = (scaled * act).astype(bf16)
    gbg_ref[...] = total(2, dot_tn(low_gate, d_gate))
    gbu_ref[...] = total(3, dot_tn(low_up, d_up))
    proj[:, :rank] += dot_nt(d_gate, bg)
    proj[:, rank:] += dot_nt(d_up, bu)
    for first, last in chunks(0, width, 512):
        acc[:, first:last] += dot_nt(d_gate, wg_ref[first:last, :]) + dot_nt(
            d_up, wu_ref[first:last, :]
        )

    @pl.when(step == pl.num_programs(0) - 1)
    def _():
        proj_b = proj[...].astype(bf16)
        routes = (route[...] * mine_ref[...]).astype(bf16)
        tag_ref[...] = routes
        for i, out in enumerate(back_refs):
            out[:, width:] = routes[i * cap : (i + 1) * cap]
        for first, last in chunks(0, width, 512):
            rows = (acc[:, first:last] + dot_nn(proj_b, both[:, first:last])).astype(bf16)
            for i, out in enumerate(back_refs):
                out[:, first:last] = rows[i * cap : (i + 1) * cap]
            part = slice(first, last)
            grad = dot_tn(proj_b, xs[:, part])
            gag_ref[:, part] = total(0, grad[:rank], part)
            gau_ref[:, part] = total(1, grad[rank:], part)


def expert_rows(mine, mats, pieces, carry=()):
    w_gate, w_up, w_down, a_gate, a_up, b_gate, b_up = mats
    width, hidden = w_gate.shape
    rank = a_gate.shape[0]
    cap = pieces[0].shape[0]
    rows = cap * plane
    wide = width + mine.shape[1]
    tile = 512
    second = pl.BlockSpec((rank, tile), lambda j: (0, j))
    grads = [whole_block((rank, width))] * 2 + [second] * 2
    return pl.pallas_call(
        functools.partial(expert_kernel, len(carry), cap, width, rank),
        grid=(hidden // tile,),
        in_specs=[
            whole_block(mine.shape),
            pl.BlockSpec((width, tile), lambda j: (0, j)),
            pl.BlockSpec((width, tile), lambda j: (0, j)),
            pl.BlockSpec((tile, width), lambda j: (j, 0)),
            whole_block(a_gate.shape),
            whole_block(a_up.shape),
            second,
            second,
        ]
        + [whole_block(a.shape) for a in pieces]
        + (grads if carry else []),
        out_shape=[jax.ShapeDtypeStruct((cap, wide), bf16)] * plane
        + [
            jax.ShapeDtypeStruct((rank, width), f32),
            jax.ShapeDtypeStruct((rank, width), f32),
            jax.ShapeDtypeStruct((rank, hidden), f32),
            jax.ShapeDtypeStruct((rank, hidden), f32),
            jax.ShapeDtypeStruct((rows, wide - width), bf16),
        ],
        out_specs=[whole_block((cap, wide))] * plane
        + grads
        + [whole_block((rows, wide - width))],
        scratch_shapes=[
            pltpu.VMEM((rows, width), bf16),
            pltpu.VMEM((rows, width), bf16),
            pltpu.VMEM((rows, 1), f32),
            pltpu.VMEM((rows, 1), f32),
            pltpu.VMEM((rows, 2 * rank), bf16),
            pltpu.VMEM((rows, 2 * rank), f32),
            pltpu.VMEM((2 * rank, width), bf16),
            pltpu.VMEM((rows, width), f32),
        ],
        compiler_params=pltpu.CompilerParams(vmem_limit_bytes=vmem_bytes),
        cost_estimate=light,
    )(mine, w_gate, w_up, w_down, a_gate, a_up, b_gate, b_up, *pieces, *carry)


def solution(mesh):
    devices = mesh.shape["expert"]
    layers = devices // plane

    def along(pairs):
        return [(a * plane + q, b * plane + q) for a, b in pairs for q in range(plane)]

    def across(step):
        return [(i, i ^ step) for i in range(devices)]

    def send(array, pairs):
        return lax.ppermute(array, "expert", pairs)

    def spread(pieces):
        return [pieces[0]] + [send(pieces[p], across(p)) for p in range(1, plane)]

    def shards(
        layer_input,
        output_gradient,
        router_matrix,
        routed_expert_index,
        gate_weight_frozen,
        up_weight_frozen,
        down_weight_frozen,
        gate_adapter_first,
        gate_adapter_second,
        up_adapter_first,
        up_adapter_second,
    ):
        tok, width = layer_input.shape
        topk = routed_expert_index.shape[1]
        experts = router_matrix.shape[1]
        capacity = 3 * tok * topk // (2 * experts)
        cap = -(-capacity // 16) * 16
        me = lax.axis_index("expert")
        layer = me // plane
        place = me % plane
        mats = (
            gate_weight_frozen[0],
            up_weight_frozen[0],
            down_weight_frozen[0],
            gate_adapter_first[0].T,
            up_adapter_first[0].T,
            gate_adapter_second[0],
            up_adapter_second[0],
        )
        dy = output_gradient
        join = lax.optimization_barrier

        scores = jax.nn.sigmoid(dot_nn(layer_input, router_matrix))
        expert_ids = jnp.arange(experts, dtype=jnp.int32)
        mask = jnp.sum(
            (routed_expert_index[:, :, None] == expert_ids[None, None, :]).astype(f32), axis=1
        )
        picked = mask * scores
        total = jnp.sum(picked, axis=1, keepdims=True)
        combine = (route_scale * picked / total).astype(bf16)
        earlier = (jnp.arange(tok)[:, None] > jnp.arange(tok)[None, :]).astype(bf16)
        slot_dense = mask * (dot_nn(earlier, mask.astype(bf16)) + 1.0)
        meta_width = -(-2 * experts // 128) * 128
        meta = jnp.concatenate(
            [slot_dense.astype(bf16), combine, jnp.zeros((tok, meta_width - 2 * experts), bf16)],
            axis=1,
        )
        own = jnp.concatenate([layer_input, meta, dy], axis=1)
        full = own.shape[1]
        wide = width + meta_width
        meta_at = (width, width + meta_width)

        here = layer * plane + (place ^ jnp.arange(plane, dtype=jnp.int32))
        guide = jnp.zeros((16, meta_width), bf16)
        guide = guide.at[:plane].set(
            (here[:, None] == jnp.arange(meta_width, dtype=jnp.int32)[None, :]).astype(bf16)
        )
        mine = (jnp.arange(meta_width) == experts + me).astype(f32)[None, :]

        def take(flag, arrays):
            *pieces, placed = select_rows(
                flag, guide, [[(0, full)] * len(arrays)], arrays, meta_at, False, cap
            )
            return pieces, placed

        def run(pieces, carry=()):
            return expert_rows(mine, mats, pieces, carry)

        if layers == 4:
            mid = (layer == 1) | (layer == 2)
            flag = mid.astype(jnp.int32)[None]
            block_1 = send(own, along([(0, 2), (3, 1), (1, 0), (2, 3)]))
            sel_0, placed_0 = take(flag, [own])
            block_1, own, got_0 = join((block_1, own, spread(sel_0)))
            block_2f = send(block_1, along([(1, 0), (2, 3)]))
            block_2m = send(own, along([(1, 2), (2, 1)]))
            sel_1, placed_1 = take(flag, [block_1])
            got_1 = spread(sel_1)
            done_0 = run(got_0)
            got_1, done_0, own = join((got_1, done_0, own))
            sel_2, placed_2 = take(flag, [block_2m, block_2f])
            sel_2, got_1, own = join((sel_2, got_1, own))
            block_3 = send(own, along([(0, 1), (3, 2), (1, 3), (2, 0)]))
            got_2 = spread(sel_2)
            done_1 = run(got_1, done_0[plane:-1])
            done_1, got_2[1], got_2[2] = join((done_1, got_2[1], got_2[2]))
            back_1 = spread(done_1[:plane])
            sel_3, placed_3 = take(flag, [block_3])
            sel_3, back_1, got_2 = join((sel_3, back_1, got_2))
            got_3 = spread(sel_3)
            done_2 = run(got_2, done_1[plane:-1])
            done_2, got_3[1], got_3[2], done_0 = join((done_2, got_3[1], got_3[2], done_0))
            back_2 = spread(done_2[:plane])
            (part_1,) = sum_rows(placed_1, back_1, wide)
            term_1 = send(part_1, along([(0, 1), (3, 2), (1, 3), (2, 0)]))
            got_3, part_1, back_2, done_0 = join((got_3, part_1, back_2, done_0))
            part_2a, part_2b, tag_2 = sum_rows(placed_2, back_2, width, (tok // 2, tok // 2))
            tag_2 = send(tag_2, across(3 * plane))
            term_2a = send(part_2a, across(3 * plane))
            back_0 = spread(done_0[:plane])
            done_3 = run(got_3, done_2[plane:-1])
            done_3, term_1, term_2a, part_2b, back_0 = join(
                (done_3, term_1, term_2a, part_2b, back_0)
            )
            pieces = spread([done_3[-1][p * cap : (p + 1) * cap] for p in range(plane)])
            done_3, pieces, tag_2 = join((done_3, pieces, tag_2))
            swap_3 = along([(1, 0), (2, 3), (3, 1), (0, 2)])
            tag_3 = dot_tn(placed_3, jnp.concatenate(pieces, axis=0)).astype(bf16)
            tag_3 = send(tag_3, swap_3)
            back_3 = spread(done_3[:plane])
            term_2b = send(part_2b, across(3 * plane))
            part_0, tag_0 = sum_rows(placed_0, back_0, width)
            back_3, term_2b = join((back_3, term_2b))
            part_3, _ = sum_rows(placed_3, back_3, width)
            term_3 = send(part_3, swap_3)
            tags = [tag_0, term_1[:, width:], tag_2, tag_3]
            terms = [[part_0], [term_1], [term_2a, term_2b], [term_3]]
            done = [done_3]
        else:
            flag = jnp.zeros((1,), jnp.int32)
            done, tags, terms = [], [], []
            for g in range(layers):
                block = own if g == 0 else send(own, across(g * plane))
                sel, placed = take(flag, [block])
                result = run(spread(sel), done[-1][plane:-1] if done else ())
                (part,) = sum_rows(placed, spread(result[:plane]), wide)
                terms.append([part if g == 0 else send(part, across(g * plane))])
                done.append(result)
                tags.append(terms[-1][0][:, width:])

        route_grad = sum(t[:, experts : 2 * experts].astype(f32) for t in tags)
        shared = jnp.sum(route_grad * picked, axis=1, keepdims=True) / (total * total)
        d_pick = route_scale * (route_grad / total - shared)
        d_logit = (mask * d_pick * scores * (1.0 - scores)).astype(bf16)

        router_part = dot_tn(d_logit, layer_input)
        share = width // devices
        router_part = router_part.reshape(experts, devices, share).transpose(1, 0, 2)
        router_got = lax.all_to_all(router_part, "expert", split_axis=0, concat_axis=0, tiled=True)
        router_grad = jnp.sum(router_got, axis=0).T

        in_grad = final_sum(d_logit, router_matrix.T, terms)

        grad_gate_a, grad_up_a, grad_gate_b, grad_up_b = done[-1][plane:-1]
        return (
            in_grad,
            router_grad,
            grad_gate_a.T[None],
            grad_gate_b[None],
            grad_up_a.T[None],
            grad_up_b[None],
        )

    rows = P(("groups", "expert"), None)
    stack = P(("groups", "expert"), None, None)
    frozen = P("expert", None, None)
    in_specs = (rows, rows, P(), rows, frozen, frozen, frozen, stack, stack, stack, stack)
    out_specs = (rows, rows, stack, stack, stack, stack)
    return jax.shard_map(shards, mesh=mesh, in_specs=in_specs, out_specs=out_specs, check_vma=False)
```

```python
import functools

import jax
import jax.numpy as jnp
from jax import lax
from jax.experimental import pallas as pl
from jax.experimental.pallas import tpu as pltpu
from jax.sharding import PartitionSpec as P

route_scale = 2.5
plane = 4
bf16 = jnp.bfloat16
f32 = jnp.float32
vmem_bytes = 56 * 1024 * 1024
light = pl.CostEstimate(flops=1024, bytes_accessed=1024, transcendentals=0)


def dot_nn(left, right):
    return jnp.dot(left, right, preferred_element_type=f32)


def dot_nt(left, right):
    return lax.dot_general(left, right, (((1,), (1,)), ((), ())), preferred_element_type=f32)


def dot_tn(left, right):
    return lax.dot_general(left, right, (((0,), (0,)), ((), ())), preferred_element_type=f32)


def after(array, *others):
    return lax.optimization_barrier((array, *others))[0]


def chunks(start, stop, step):
    return [(at, min(at + step, stop)) for at in range(start, stop, step)]


def whole_block(shape):
    return pl.BlockSpec(shape, lambda *_: (0,) * len(shape), pipeline_mode=pl.Buffered(1))


vmem = pl.BlockSpec(memory_space=pltpu.VMEM)
smem = pl.BlockSpec(memory_space=pltpu.SMEM)


def select_kernel(parts, meta_at, slots_held, cap, flag_ref, guide_ref, *refs):
    count = sum(len(p) for p in parts)
    ins, outs = refs[:count], refs[count:]
    tok = ins[0].shape[0]
    flag = flag_ref[0] == 1
    groups = []
    for part in parts:
        groups.append((part, ins[: len(part)]))
        ins = ins[len(part) :]

    def load(group, first, last):
        part, arrays = group
        values = [a[:, at + first : at + last] for (at, _), a in zip(part, arrays)]
        return values[0] if len(values) == 1 else jnp.where(flag, values[0], values[1])

    if slots_held:
        placed = guide_ref[...]
    else:
        meta = load(groups[0], *meta_at)
        named = dot_nt(guide_ref[...], meta)
        rank = lax.broadcasted_iota(jnp.int32, (cap, tok), 0).astype(f32) + 1.0
        placed = jnp.concatenate(
            [(named[p : p + 1, :] == rank).astype(bf16) for p in range(plane)], axis=0
        )
        outs[plane][...] = placed
    at = 0
    for group in groups:
        length = group[0][0][1]
        for first, last in chunks(0, length, 512):
            rows = dot_nn(placed, load(group, first, last)).astype(bf16)
            for p in range(plane):
                outs[p][:, at + first : at + last] = rows[p * cap : (p + 1) * cap]
        at += length


def select_rows(flag, guide, parts, arrays, meta_at, slots_held, cap):
    tok = arrays[0].shape[0]
    length = sum(p[0][1] for p in parts)
    shapes = [jax.ShapeDtypeStruct((cap, length), bf16)] * plane
    if not slots_held:
        shapes.append(jax.ShapeDtypeStruct((plane * cap, tok), bf16))
    return pl.pallas_call(
        functools.partial(select_kernel, parts, meta_at, slots_held, cap),
        out_shape=shapes,
        in_specs=[smem] + [vmem] * (1 + len(arrays)),
        out_specs=[vmem] * len(shapes),
        compiler_params=pltpu.CompilerParams(vmem_limit_bytes=vmem_bytes),
        cost_estimate=light,
    )(flag, guide, *arrays)


def sum_kernel(apart, placed_ref, *refs):
    pieces, outs = refs[:plane], refs[plane:]
    wide = pieces[0].shape[1]
    rows, tags = (outs[:-1], outs[-1]) if apart else (outs, None)
    stop = rows[0].shape[1]
    for first, last in chunks(0, stop, 512) + chunks(stop, wide, 512):
        joined = jnp.concatenate([p[:, first:last] for p in pieces], axis=0)
        total = dot_tn(placed_ref[...], joined).astype(bf16)
        if first >= stop:
            tags[...] = total
            continue
        at = 0
        for out in rows:
            out[:, first:last] = total[at : at + out.shape[0]]
            at += out.shape[0]


def sum_rows(placed, pieces, width, lengths=None):
    cap, wide = pieces[0].shape
    tok = placed.shape[1]
    shapes = [jax.ShapeDtypeStruct((length, width), bf16) for length in lengths or (tok,)]
    apart = width < wide
    if apart:
        shapes.append(jax.ShapeDtypeStruct((tok, wide - width), bf16))
    return pl.pallas_call(
        functools.partial(sum_kernel, apart),
        out_shape=shapes,
        in_specs=[vmem] * (1 + plane),
        out_specs=[vmem] * len(shapes),
        compiler_params=pltpu.CompilerParams(vmem_limit_bytes=vmem_bytes),
        cost_estimate=light,
    )(placed, *pieces)


def final_kernel(groups, logit_ref, router_ref, *refs):
    out = refs[-1]
    for first, last in chunks(0, out.shape[1], 512):
        total = dot_nn(logit_ref[...], router_ref[:, first:last])
        left = refs
        for count in groups:
            total = total + jnp.concatenate(
                [r[:, first:last] for r in left[:count]], axis=0
            ).astype(f32)
            left = left[count:]
        out[:, first:last] = total.astype(bf16)


def final_sum(logit, router, terms):
    tok, width = logit.shape[0], router.shape[1]
    return pl.pallas_call(
        functools.partial(final_kernel, [len(t) for t in terms]),
        out_shape=jax.ShapeDtypeStruct((tok, width), bf16),
        in_specs=[vmem] * (2 + sum(len(t) for t in terms)),
        out_specs=vmem,
        compiler_params=pltpu.CompilerParams(vmem_limit_bytes=vmem_bytes),
        cost_estimate=light,
    )(logit, router, *[a for t in terms for a in t])


def expert_kernel(
    held, cap, width, rank, mine_ref, wg_ref, wu_ref, wd_ref, ag_ref, au_ref, bg_ref, bu_ref, *refs
):
    ins, refs = refs[:plane], refs[plane:]
    carry, refs = refs[:held], refs[held:]
    back_refs, refs = refs[:plane], refs[plane:]
    gag_ref, gau_ref, gbg_ref, gbu_ref, tag_ref = refs[:5]
    xs, dys, weight, route, low, proj, both, acc = refs[5:]

    def total(at, value, part=slice(None)):
        return value + carry[at][:, part] if held else value

    step = pl.program_id(0)
    tail = width + mine_ref.shape[1]

    @pl.when(step == 0)
    def _():
        for i, ref in enumerate(ins):
            rows = slice(i * cap, (i + 1) * cap)
            xs[rows, :] = ref[:, :width]
            dys[rows, :] = ref[:, tail:]
            weight[rows, :] = jnp.sum(
                ref[:, width:tail].astype(f32) * mine_ref[...], axis=1, keepdims=True
            )
        both[:rank, :] = ag_ref[...]
        both[rank:, :] = au_ref[...]
        low[...] = dot_nt(xs[...], both[...]).astype(bf16)
        proj[...] = jnp.zeros_like(proj)
        acc[...] = jnp.zeros_like(acc)
        route[...] = jnp.zeros_like(route)

    bg, bu = bg_ref[...], bu_ref[...]
    low_gate, low_up = low[:, :rank], low[:, rank:]
    gate = dot_nn(xs[...], wg_ref[...]) + dot_nn(low_gate, bg)
    upval = dot_nn(xs[...], wu_ref[...]) + dot_nn(low_up, bu)
    back = dot_nt(dys[...], wd_ref[...])
    sigma = jax.nn.sigmoid(gate)
    act = gate * sigma
    route[...] += jnp.sum(back * (act * upval), axis=1, keepdims=True)
    scaled = weight[...] * back
    d_gate = (scaled * upval * sigma * (1.0 + gate * (1.0 - sigma))).astype(bf16)
    d_up = (scaled * act).astype(bf16)
    gbg_ref[...] = total(2, dot_tn(low_gate, d_gate))
    gbu_ref[...] = total(3, dot_tn(low_up, d_up))
    proj[:, :rank] += dot_nt(d_gate, bg)
    proj[:, rank:] += dot_nt(d_up, bu)
    for first, last in chunks(0, width, 512):
        acc[:, first:last] += dot_nt(d_gate, wg_ref[first:last, :]) + dot_nt(
            d_up, wu_ref[first:last, :]
        )

    @pl.when(step == pl.num_programs(0) - 1)
    def _():
        proj_b = proj[...].astype(bf16)
        routes = (route[...] * mine_ref[...]).astype(bf16)
        tag_ref[...] = routes
        for i, out in enumerate(back_refs):
            out[:, width:] = routes[i * cap : (i + 1) * cap]
        for first, last in chunks(0, width, 512):
            rows = (acc[:, first:last] + dot_nn(proj_b, both[:, first:last])).astype(bf16)
            for i, out in enumerate(back_refs):
                out[:, first:last] = rows[i * cap : (i + 1) * cap]
            part = slice(first, last)
            grad = dot_tn(proj_b, xs[:, part])
            gag_ref[:, part] = total(0, grad[:rank], part)
            gau_ref[:, part] = total(1, grad[rank:], part)


def expert_rows(mine, mats, pieces, carry=()):
    w_gate, w_up, w_down, a_gate, a_up, b_gate, b_up = mats
    width, hidden = w_gate.shape
    rank = a_gate.shape[0]
    cap = pieces[0].shape[0]
    rows = cap * plane
    wide = width + mine.shape[1]
    tile = 512
    second = pl.BlockSpec((rank, tile), lambda j: (0, j))
    grads = [whole_block((rank, width))] * 2 + [second] * 2
    return pl.pallas_call(
        functools.partial(expert_kernel, len(carry), cap, width, rank),
        grid=(hidden // tile,),
        in_specs=[
            whole_block(mine.shape),
            pl.BlockSpec((width, tile), lambda j: (0, j)),
            pl.BlockSpec((width, tile), lambda j: (0, j)),
            pl.BlockSpec((tile, width), lambda j: (j, 0)),
            whole_block(a_gate.shape),
            whole_block(a_up.shape),
            second,
            second,
        ]
        + [whole_block(a.shape) for a in pieces]
        + (grads if carry else []),
        out_shape=[jax.ShapeDtypeStruct((cap, wide), bf16)] * plane
        + [
            jax.ShapeDtypeStruct((rank, width), f32),
            jax.ShapeDtypeStruct((rank, width), f32),
            jax.ShapeDtypeStruct((rank, hidden), f32),
            jax.ShapeDtypeStruct((rank, hidden), f32),
            jax.ShapeDtypeStruct((rows, wide - width), bf16),
        ],
        out_specs=[whole_block((cap, wide))] * plane
        + grads
        + [whole_block((rows, wide - width))],
        scratch_shapes=[
            pltpu.VMEM((rows, width), bf16),
            pltpu.VMEM((rows, width), bf16),
            pltpu.VMEM((rows, 1), f32),
            pltpu.VMEM((rows, 1), f32),
            pltpu.VMEM((rows, 2 * rank), bf16),
            pltpu.VMEM((rows, 2 * rank), f32),
            pltpu.VMEM((2 * rank, width), bf16),
            pltpu.VMEM((rows, width), f32),
        ],
        compiler_params=pltpu.CompilerParams(vmem_limit_bytes=vmem_bytes),
        cost_estimate=light,
    )(mine, w_gate, w_up, w_down, a_gate, a_up, b_gate, b_up, *pieces, *carry)


def solution(mesh):
    devices = mesh.shape["expert"]
    layers = devices // plane

    def along(pairs):
        return [(a * plane + q, b * plane + q) for a, b in pairs for q in range(plane)]

    def across(step):
        return [(i, i ^ step) for i in range(devices)]

    def send(array, pairs):
        return lax.ppermute(array, "expert", pairs)

    def spread(pieces):
        return [pieces[0]] + [send(pieces[p], across(p)) for p in range(1, plane)]

    def shards(
        layer_input,
        output_gradient,
        router_matrix,
        routed_expert_index,
        gate_weight_frozen,
        up_weight_frozen,
        down_weight_frozen,
        gate_adapter_first,
        gate_adapter_second,
        up_adapter_first,
        up_adapter_second,
    ):
        tok, width = layer_input.shape
        topk = routed_expert_index.shape[1]
        experts = router_matrix.shape[1]
        capacity = 3 * tok * topk // (2 * experts)
        cap = -(-capacity // 16) * 16
        me = lax.axis_index("expert")
        layer = me // plane
        place = me % plane
        mats = (
            gate_weight_frozen[0],
            up_weight_frozen[0],
            down_weight_frozen[0],
            gate_adapter_first[0].T,
            up_adapter_first[0].T,
            gate_adapter_second[0],
            up_adapter_second[0],
        )
        dy = output_gradient
        join = lax.optimization_barrier

        scores = jax.nn.sigmoid(dot_nn(layer_input, router_matrix))
        expert_ids = jnp.arange(experts, dtype=jnp.int32)
        mask = jnp.sum(
            (routed_expert_index[:, :, None] == expert_ids[None, None, :]).astype(f32), axis=1
        )
        picked = mask * scores
        total = jnp.sum(picked, axis=1, keepdims=True)
        combine = (route_scale * picked / total).astype(bf16)
        earlier = (jnp.arange(tok)[:, None] > jnp.arange(tok)[None, :]).astype(bf16)
        slot_dense = mask * (dot_nn(earlier, mask.astype(bf16)) + 1.0)
        meta_width = -(-2 * experts // 128) * 128
        meta = jnp.concatenate(
            [slot_dense.astype(bf16), combine, jnp.zeros((tok, meta_width - 2 * experts), bf16)],
            axis=1,
        )
        own = jnp.concatenate([layer_input, meta, dy], axis=1)
        full = own.shape[1]
        wide = width + meta_width
        meta_at = (width, width + meta_width)

        here = layer * plane + (place ^ jnp.arange(plane, dtype=jnp.int32))
        guide = jnp.zeros((16, meta_width), bf16)
        guide = guide.at[:plane].set(
            (here[:, None] == jnp.arange(meta_width, dtype=jnp.int32)[None, :]).astype(bf16)
        )
        mine = (jnp.arange(meta_width) == experts + me).astype(f32)[None, :]

        def take(flag, arrays):
            *pieces, placed = select_rows(
                flag, guide, [[(0, full)] * len(arrays)], arrays, meta_at, False, cap
            )
            return pieces, placed

        def run(pieces, carry=()):
            return expert_rows(mine, mats, pieces, carry)

        if layers == 4:
            mid = (layer == 1) | (layer == 2)
            flag = mid.astype(jnp.int32)[None]
            block_1 = send(own, along([(0, 2), (3, 1), (1, 0), (2, 3)]))
            sel_0, placed_0 = take(flag, [own])
            block_1, own, got_0 = join((block_1, own, spread(sel_0)))
            block_2f = send(block_1, along([(1, 0), (2, 3)]))
            block_2m = send(own, along([(1, 2), (2, 1)]))
            sel_1, placed_1 = take(flag, [block_1])
            got_1 = spread(sel_1)
            done_0 = run(got_0)
            got_1, done_0, own = join((got_1, done_0, own))
            sel_2, placed_2 = take(flag, [block_2m, block_2f])
            sel_2, got_1, own = join((sel_2, got_1, own))
            block_3 = send(own, along([(0, 1), (3, 2), (1, 3), (2, 0)]))
            got_2 = spread(sel_2)
            done_1 = run(got_1, done_0[plane:-1])
            done_1, got_2[1], got_2[2] = join((done_1, got_2[1], got_2[2]))
            back_1 = spread(done_1[:plane])
            sel_3, placed_3 = take(flag, [block_3])
            sel_3, back_1, got_2 = join((sel_3, back_1, got_2))
            got_3 = spread(sel_3)
            done_2 = run(got_2, done_1[plane:-1])
            done_2, got_3[1], got_3[2], done_0 = join((done_2, got_3[1], got_3[2], done_0))
            back_2 = spread(done_2[:plane])
            (part_1,) = sum_rows(placed_1, back_1, wide)
            term_1 = send(part_1, along([(0, 1), (3, 2), (1, 3), (2, 0)]))
            got_3, part_1, back_2, done_0 = join((got_3, part_1, back_2, done_0))
            part_2a, part_2b, tag_2 = sum_rows(placed_2, back_2, width, (tok // 2, tok // 2))
            tag_2 = send(tag_2, across(3 * plane))
            term_2a = send(part_2a, across(3 * plane))
            back_0 = spread(done_0[:plane])
            done_3 = run(got_3, done_2[plane:-1])
            done_3, term_1, term_2a, part_2b, back_0 = join(
                (done_3, term_1, term_2a, part_2b, back_0)
            )
            pieces = spread([done_3[-1][p * cap : (p + 1) * cap] for p in range(plane)])
            done_3, pieces, tag_2 = join((done_3, pieces, tag_2))
            swap_3 = along([(1, 0), (2, 3), (3, 1), (0, 2)])
            tag_3 = dot_tn(placed_3, jnp.concatenate(pieces, axis=0)).astype(bf16)
            tag_3 = send(tag_3, swap_3)
            back_3 = spread(done_3[:plane])
            term_2b = send(part_2b, across(3 * plane))
            part_0, tag_0 = sum_rows(placed_0, back_0, width)
            tag_3, back_3[1], back_3[2] = join((tag_3, back_3[1], back_3[2]))
            tags = [tag_0, term_1[:, width:], tag_2, tag_3]
            done = [done_3]
        else:
            flag = jnp.zeros((1,), jnp.int32)
            done, tags, terms = [], [], []
            for g in range(layers):
                block = own if g == 0 else send(own, across(g * plane))
                sel, placed = take(flag, [block])
                result = run(spread(sel), done[-1][plane:-1] if done else ())
                (part,) = sum_rows(placed, spread(result[:plane]), wide)
                terms.append([part if g == 0 else send(part, across(g * plane))])
                done.append(result)
                tags.append(terms[-1][0][:, width:])

        route_grad = sum(t[:, experts : 2 * experts].astype(f32) for t in tags)
        shared = jnp.sum(route_grad * picked, axis=1, keepdims=True) / (total * total)
        d_pick = route_scale * (route_grad / total - shared)
        d_logit = (mask * d_pick * scores * (1.0 - scores)).astype(bf16)

        router_part = dot_tn(d_logit, layer_input)
        share = width // devices
        router_part = router_part.reshape(experts, devices, share).transpose(1, 0, 2)
        router_got = lax.all_to_all(router_part, "expert", split_axis=0, concat_axis=0, tiled=True)
        if layers == 4:
            back_3, router_got, term_2b = join((back_3, router_got, term_2b))
            part_3, _ = sum_rows(placed_3, back_3, width)
            terms = [[part_0], [term_1], [term_2a, term_2b], [send(part_3, swap_3)]]
        router_grad = jnp.sum(router_got, axis=0).T

        in_grad = final_sum(d_logit, router_matrix.T, terms)

        grad_gate_a, grad_up_a, grad_gate_b, grad_up_b = done[-1][plane:-1]
        return (
            in_grad,
            router_grad,
            grad_gate_a.T[None],
            grad_gate_b[None],
            grad_up_a.T[None],
            grad_up_b[None],
        )

    rows = P(("groups", "expert"), None)
    stack = P(("groups", "expert"), None, None)
    frozen = P("expert", None, None)
    in_specs = (rows, rows, P(), rows, frozen, frozen, frozen, stack, stack, stack, stack)
    out_specs = (rows, rows, stack, stack, stack, stack)
    return jax.shard_map(shards, mesh=mesh, in_specs=in_specs, out_specs=out_specs, check_vma=False)
```

```python
import functools

import jax
import jax.numpy as jnp
from jax import lax
from jax.experimental import pallas as pl
from jax.experimental.pallas import tpu as pltpu
from jax.sharding import PartitionSpec as P

route_scale = 2.5
plane = 4
bf16 = jnp.bfloat16
f32 = jnp.float32
vmem_bytes = 56 * 1024 * 1024
light = pl.CostEstimate(flops=1024, bytes_accessed=1024, transcendentals=0)


def dot_nn(left, right):
    return jnp.dot(left, right, preferred_element_type=f32)


def dot_nt(left, right):
    return lax.dot_general(left, right, (((1,), (1,)), ((), ())), preferred_element_type=f32)


def dot_tn(left, right):
    return lax.dot_general(left, right, (((0,), (0,)), ((), ())), preferred_element_type=f32)


def after(array, *others):
    return lax.optimization_barrier((array, *others))[0]


def chunks(start, stop, step):
    return [(at, min(at + step, stop)) for at in range(start, stop, step)]


def whole_block(shape):
    return pl.BlockSpec(shape, lambda *_: (0,) * len(shape), pipeline_mode=pl.Buffered(1))


vmem = pl.BlockSpec(memory_space=pltpu.VMEM)
smem = pl.BlockSpec(memory_space=pltpu.SMEM)


def select_kernel(parts, meta_at, slots_held, cap, flag_ref, guide_ref, *refs):
    count = sum(len(p) for p in parts)
    ins, outs = refs[:count], refs[count:]
    tok = ins[0].shape[0]
    flag = flag_ref[0] == 1
    groups = []
    for part in parts:
        groups.append((part, ins[: len(part)]))
        ins = ins[len(part) :]

    def load(group, first, last):
        part, arrays = group
        values = [a[:, at + first : at + last] for (at, _), a in zip(part, arrays)]
        return values[0] if len(values) == 1 else jnp.where(flag, values[0], values[1])

    if slots_held:
        placed = guide_ref[...]
    else:
        meta = load(groups[0], *meta_at)
        named = dot_nt(guide_ref[...], meta)
        rank = lax.broadcasted_iota(jnp.int32, (cap, tok), 0).astype(f32) + 1.0
        placed = jnp.concatenate(
            [(named[p : p + 1, :] == rank).astype(bf16) for p in range(plane)], axis=0
        )
        outs[plane][...] = placed
    at = 0
    for group in groups:
        length = group[0][0][1]
        for first, last in chunks(0, length, 512):
            rows = dot_nn(placed, load(group, first, last)).astype(bf16)
            for p in range(plane):
                outs[p][:, at + first : at + last] = rows[p * cap : (p + 1) * cap]
        at += length


def select_rows(flag, guide, parts, arrays, meta_at, slots_held, cap):
    tok = arrays[0].shape[0]
    length = sum(p[0][1] for p in parts)
    shapes = [jax.ShapeDtypeStruct((cap, length), bf16)] * plane
    if not slots_held:
        shapes.append(jax.ShapeDtypeStruct((plane * cap, tok), bf16))
    return pl.pallas_call(
        functools.partial(select_kernel, parts, meta_at, slots_held, cap),
        out_shape=shapes,
        in_specs=[smem] + [vmem] * (1 + len(arrays)),
        out_specs=[vmem] * len(shapes),
        compiler_params=pltpu.CompilerParams(vmem_limit_bytes=vmem_bytes),
        cost_estimate=light,
    )(flag, guide, *arrays)


def sum_kernel(apart, placed_ref, *refs):
    pieces, outs = refs[:plane], refs[plane:]
    wide = pieces[0].shape[1]
    rows, tags = (outs[:-1], outs[-1]) if apart else (outs, None)
    stop = rows[0].shape[1]
    for first, last in chunks(0, stop, 512) + chunks(stop, wide, 512):
        joined = jnp.concatenate([p[:, first:last] for p in pieces], axis=0)
        total = dot_tn(placed_ref[...], joined).astype(bf16)
        if first >= stop:
            tags[...] = total
            continue
        at = 0
        for out in rows:
            out[:, first:last] = total[at : at + out.shape[0]]
            at += out.shape[0]


def sum_rows(placed, pieces, width, lengths=None):
    cap, wide = pieces[0].shape
    tok = placed.shape[1]
    shapes = [jax.ShapeDtypeStruct((length, width), bf16) for length in lengths or (tok,)]
    apart = width < wide
    if apart:
        shapes.append(jax.ShapeDtypeStruct((tok, wide - width), bf16))
    return pl.pallas_call(
        functools.partial(sum_kernel, apart),
        out_shape=shapes,
        in_specs=[vmem] * (1 + plane),
        out_specs=[vmem] * len(shapes),
        compiler_params=pltpu.CompilerParams(vmem_limit_bytes=vmem_bytes),
        cost_estimate=light,
    )(placed, *pieces)


def final_kernel(groups, logit_ref, router_ref, *refs):
    out = refs[-1]
    for first, last in chunks(0, out.shape[1], 512):
        total = dot_nn(logit_ref[...], router_ref[:, first:last])
        left = refs
        for count in groups:
            total = total + jnp.concatenate(
                [r[:, first:last] for r in left[:count]], axis=0
            ).astype(f32)
            left = left[count:]
        out[:, first:last] = total.astype(bf16)


def final_sum(logit, router, terms):
    tok, width = logit.shape[0], router.shape[1]
    return pl.pallas_call(
        functools.partial(final_kernel, [len(t) for t in terms]),
        out_shape=jax.ShapeDtypeStruct((tok, width), bf16),
        in_specs=[vmem] * (2 + sum(len(t) for t in terms)),
        out_specs=vmem,
        compiler_params=pltpu.CompilerParams(vmem_limit_bytes=vmem_bytes),
        cost_estimate=light,
    )(logit, router, *[a for t in terms for a in t])


def expert_kernel(
    held, cap, width, rank, mine_ref, wg_ref, wu_ref, wd_ref, ag_ref, au_ref, bg_ref, bu_ref, *refs
):
    ins, refs = refs[:plane], refs[plane:]
    carry, refs = refs[:held], refs[held:]
    back_refs, refs = refs[:plane], refs[plane:]
    gag_ref, gau_ref, gbg_ref, gbu_ref = refs[:4]
    xs, dys, weight, route, low, proj, both, acc = refs[4:]

    def total(at, value, part=slice(None)):
        return value + carry[at][:, part] if held else value

    step = pl.program_id(0)
    tail = width + mine_ref.shape[1]

    @pl.when(step == 0)
    def _():
        for i, ref in enumerate(ins):
            rows = slice(i * cap, (i + 1) * cap)
            xs[rows, :] = ref[:, :width]
            dys[rows, :] = ref[:, tail:]
            weight[rows, :] = jnp.sum(
                ref[:, width:tail].astype(f32) * mine_ref[...], axis=1, keepdims=True
            )
        both[:rank, :] = ag_ref[...]
        both[rank:, :] = au_ref[...]
        low[...] = dot_nt(xs[...], both[...]).astype(bf16)
        proj[...] = jnp.zeros_like(proj)
        acc[...] = jnp.zeros_like(acc)
        route[...] = jnp.zeros_like(route)

    bg, bu = bg_ref[...], bu_ref[...]
    low_gate, low_up = low[:, :rank], low[:, rank:]
    gate = dot_nn(xs[...], wg_ref[...]) + dot_nn(low_gate, bg)
    upval = dot_nn(xs[...], wu_ref[...]) + dot_nn(low_up, bu)
    back = dot_nt(dys[...], wd_ref[...])
    sigma = jax.nn.sigmoid(gate)
    act = gate * sigma
    route[...] += jnp.sum(back * (act * upval), axis=1, keepdims=True)
    scaled = weight[...] * back
    d_gate = (scaled * upval * sigma * (1.0 + gate * (1.0 - sigma))).astype(bf16)
    d_up = (scaled * act).astype(bf16)
    gbg_ref[...] = total(2, dot_tn(low_gate, d_gate))
    gbu_ref[...] = total(3, dot_tn(low_up, d_up))
    proj[:, :rank] += dot_nt(d_gate, bg)
    proj[:, rank:] += dot_nt(d_up, bu)
    for first, last in chunks(0, width, 512):
        acc[:, first:last] += dot_nt(d_gate, wg_ref[first:last, :]) + dot_nt(
            d_up, wu_ref[first:last, :]
        )

    @pl.when(step == pl.num_programs(0) - 1)
    def _():
        proj_b = proj[...].astype(bf16)
        routes = (route[...] * mine_ref[...]).astype(bf16)
        for i, out in enumerate(back_refs):
            out[:, width:] = routes[i * cap : (i + 1) * cap]
        for first, last in chunks(0, width, 512):
            rows = (acc[:, first:last] + dot_nn(proj_b, both[:, first:last])).astype(bf16)
            for i, out in enumerate(back_refs):
                out[:, first:last] = rows[i * cap : (i + 1) * cap]
            part = slice(first, last)
            grad = dot_tn(proj_b, xs[:, part])
            gag_ref[:, part] = total(0, grad[:rank], part)
            gau_ref[:, part] = total(1, grad[rank:], part)


def expert_rows(mine, mats, pieces, carry=()):
    w_gate, w_up, w_down, a_gate, a_up, b_gate, b_up = mats
    width, hidden = w_gate.shape
    rank = a_gate.shape[0]
    cap = pieces[0].shape[0]
    rows = cap * plane
    wide = width + mine.shape[1]
    tile = 512
    second = pl.BlockSpec((rank, tile), lambda j: (0, j))
    grads = [whole_block((rank, width))] * 2 + [second] * 2
    return pl.pallas_call(
        functools.partial(expert_kernel, len(carry), cap, width, rank),
        grid=(hidden // tile,),
        in_specs=[
            whole_block(mine.shape),
            pl.BlockSpec((width, tile), lambda j: (0, j)),
            pl.BlockSpec((width, tile), lambda j: (0, j)),
            pl.BlockSpec((tile, width), lambda j: (j, 0)),
            whole_block(a_gate.shape),
            whole_block(a_up.shape),
            second,
            second,
        ]
        + [whole_block(a.shape) for a in pieces]
        + (grads if carry else []),
        out_shape=[jax.ShapeDtypeStruct((cap, wide), bf16)] * plane
        + [
            jax.ShapeDtypeStruct((rank, width), f32),
            jax.ShapeDtypeStruct((rank, width), f32),
            jax.ShapeDtypeStruct((rank, hidden), f32),
            jax.ShapeDtypeStruct((rank, hidden), f32),
        ],
        out_specs=[whole_block((cap, wide))] * plane + grads,
        scratch_shapes=[
            pltpu.VMEM((rows, width), bf16),
            pltpu.VMEM((rows, width), bf16),
            pltpu.VMEM((rows, 1), f32),
            pltpu.VMEM((rows, 1), f32),
            pltpu.VMEM((rows, 2 * rank), bf16),
            pltpu.VMEM((rows, 2 * rank), f32),
            pltpu.VMEM((2 * rank, width), bf16),
            pltpu.VMEM((rows, width), f32),
        ],
        compiler_params=pltpu.CompilerParams(vmem_limit_bytes=vmem_bytes),
        cost_estimate=light,
    )(mine, w_gate, w_up, w_down, a_gate, a_up, b_gate, b_up, *pieces, *carry)


def solution(mesh):
    devices = mesh.shape["expert"]
    layers = devices // plane

    def along(pairs):
        return [(a * plane + q, b * plane + q) for a, b in pairs for q in range(plane)]

    def across(step):
        return [(i, i ^ step) for i in range(devices)]

    def send(array, pairs):
        return lax.ppermute(array, "expert", pairs)

    def spread(pieces):
        return [pieces[0]] + [send(pieces[p], across(p)) for p in range(1, plane)]

    def shards(
        layer_input,
        output_gradient,
        router_matrix,
        routed_expert_index,
        gate_weight_frozen,
        up_weight_frozen,
        down_weight_frozen,
        gate_adapter_first,
        gate_adapter_second,
        up_adapter_first,
        up_adapter_second,
    ):
        tok, width = layer_input.shape
        topk = routed_expert_index.shape[1]
        experts = router_matrix.shape[1]
        capacity = 3 * tok * topk // (2 * experts)
        cap = -(-capacity // 16) * 16
        me = lax.axis_index("expert")
        layer = me // plane
        place = me % plane
        mats = (
            gate_weight_frozen[0],
            up_weight_frozen[0],
            down_weight_frozen[0],
            gate_adapter_first[0].T,
            up_adapter_first[0].T,
            gate_adapter_second[0],
            up_adapter_second[0],
        )
        dy = output_gradient
        join = lax.optimization_barrier

        scores = jax.nn.sigmoid(dot_nn(layer_input, router_matrix))
        expert_ids = jnp.arange(experts, dtype=jnp.int32)
        mask = jnp.sum(
            (routed_expert_index[:, :, None] == expert_ids[None, None, :]).astype(f32), axis=1
        )
        picked = mask * scores
        total = jnp.sum(picked, axis=1, keepdims=True)
        combine = (route_scale * picked / total).astype(bf16)
        earlier = (jnp.arange(tok)[:, None] > jnp.arange(tok)[None, :]).astype(bf16)
        slot_dense = mask * (dot_nn(earlier, mask.astype(bf16)) + 1.0)
        meta_width = -(-2 * experts // 128) * 128
        meta = jnp.concatenate(
            [slot_dense.astype(bf16), combine, jnp.zeros((tok, meta_width - 2 * experts), bf16)],
            axis=1,
        )
        own = jnp.concatenate([layer_input, meta, dy], axis=1)
        full = own.shape[1]
        wide = width + meta_width
        meta_at = (width, width + meta_width)

        here = layer * plane + (place ^ jnp.arange(plane, dtype=jnp.int32))
        guide = jnp.zeros((16, meta_width), bf16)
        guide = guide.at[:plane].set(
            (here[:, None] == jnp.arange(meta_width, dtype=jnp.int32)[None, :]).astype(bf16)
        )
        mine = (jnp.arange(meta_width) == experts + me).astype(f32)[None, :]

        def take(flag, arrays):
            *pieces, placed = select_rows(
                flag, guide, [[(0, full)] * len(arrays)], arrays, meta_at, False, cap
            )
            return pieces, placed

        def run(pieces, carry=()):
            return expert_rows(mine, mats, pieces, carry)

        if layers == 4:
            mid = (layer == 1) | (layer == 2)
            flag = mid.astype(jnp.int32)[None]
            block_1 = send(own, along([(0, 2), (3, 1), (1, 0), (2, 3)]))
            sel_0, placed_0 = take(flag, [own])
            block_1, own, got_0 = join((block_1, own, spread(sel_0)))
            block_2f = send(block_1, along([(1, 0), (2, 3)]))
            block_2m = send(own, along([(1, 2), (2, 1)]))
            sel_1, placed_1 = take(flag, [block_1])
            got_1 = spread(sel_1)
            done_0 = run(got_0)
            got_1, done_0, own = join((got_1, done_0, own))
            sel_2, placed_2 = take(flag, [block_2m, block_2f])
            sel_2, got_1, own = join((sel_2, got_1, own))
            block_3 = send(own, along([(0, 1), (3, 2), (1, 3), (2, 0)]))
            got_2 = spread(sel_2)
            done_1 = run(got_1, done_0[plane:])
            done_1, got_2[1], got_2[2] = join((done_1, got_2[1], got_2[2]))
            back_1 = spread(done_1[:plane])
            sel_3, placed_3 = take(flag, [block_3])
            sel_3, back_1, got_2 = join((sel_3, back_1, got_2))
            got_3 = spread(sel_3)
            done_2 = run(got_2, done_1[plane:])
            done_2, got_3[1], got_3[2], done_0 = join((done_2, got_3[1], got_3[2], done_0))
            back_2 = spread(done_2[:plane])
            (part_1,) = sum_rows(placed_1, back_1, wide)
            term_1 = send(part_1, along([(0, 1), (3, 2), (1, 3), (2, 0)]))
            got_3, part_1, back_2, done_0 = join((got_3, part_1, back_2, done_0))
            part_2a, part_2b, tag_2 = sum_rows(placed_2, back_2, width, (tok // 2, tok // 2))
            tag_2 = send(tag_2, across(3 * plane))
            term_2a = send(part_2a, across(3 * plane))
            back_0 = spread(done_0[:plane])
            done_3 = run(got_3, done_2[plane:])
            done_3, term_1, term_2a, part_2b, back_0 = join(
                (done_3, term_1, term_2a, part_2b, back_0)
            )
            back_3 = spread(done_3[:plane])
            term_2b = send(part_2b, across(3 * plane))
            back_3, back_0, term_2b = join((back_3, back_0, term_2b))
            part_0, tag_0 = sum_rows(placed_0, back_0, width)
            part_3, tag_3 = sum_rows(placed_3, back_3, width)
            swap_3 = along([(1, 0), (2, 3), (3, 1), (0, 2)])
            tag_3 = send(tag_3, swap_3)
            term_3 = send(part_3, swap_3)
            tags = [tag_0, term_1[:, width:], tag_2, tag_3]
            terms = [[part_0], [term_1], [term_2a, term_2b], [term_3]]
            done = [done_3]
        else:
            flag = jnp.zeros((1,), jnp.int32)
            done, tags, terms = [], [], []
            for g in range(layers):
                block = own if g == 0 else send(own, across(g * plane))
                sel, placed = take(flag, [block])
                result = run(spread(sel), done[-1][plane:] if done else ())
                (part,) = sum_rows(placed, spread(result[:plane]), wide)
                terms.append([part if g == 0 else send(part, across(g * plane))])
                done.append(result)
                tags.append(terms[-1][0][:, width:])

        route_grad = sum(t[:, experts : 2 * experts].astype(f32) for t in tags)
        shared = jnp.sum(route_grad * picked, axis=1, keepdims=True) / (total * total)
        d_pick = route_scale * (route_grad / total - shared)
        d_logit = (mask * d_pick * scores * (1.0 - scores)).astype(bf16)

        router_part = dot_tn(d_logit, layer_input)
        share = width // devices
        router_part = router_part.reshape(experts, devices, share).transpose(1, 0, 2)
        router_got = lax.all_to_all(router_part, "expert", split_axis=0, concat_axis=0, tiled=True)
        router_grad = jnp.sum(router_got, axis=0).T

        in_grad = final_sum(d_logit, router_matrix.T, terms)

        grad_gate_a, grad_up_a, grad_gate_b, grad_up_b = done[-1][plane:]
        return (
            in_grad,
            router_grad,
            grad_gate_a.T[None],
            grad_gate_b[None],
            grad_up_a.T[None],
            grad_up_b[None],
        )

    rows = P(("groups", "expert"), None)
    stack = P(("groups", "expert"), None, None)
    frozen = P("expert", None, None)
    in_specs = (rows, rows, P(), rows, frozen, frozen, frozen, stack, stack, stack, stack)
    out_specs = (rows, rows, stack, stack, stack, stack)
    return jax.shard_map(shards, mesh=mesh, in_specs=in_specs, out_specs=out_specs, check_vma=False)
```
